32 devices in a mesh: dp: 8 (over z, x), ctx: 4 (over y, core).
Axes of the slice: x: 2, y: 2, z: 4, core: 2. Of those that a mesh axis runs over, the one named last changes fastest.
Arguments:
- block_input: bfloat16 [8, 2048, 2048], P('dp', 'ctx'), may hold values from -6 to 6
- segment_ids: int32 [8, 2048], P('dp', 'ctx'), may hold values from 0 to 5, never falling along the last dimension, each value on 1 to 800 neighbouring positions
- cotangent: bfloat16 [8, 2048, 2048], P('dp', 'ctx'), may hold values from -6 to 6
- in_weight: float32 [2048, 8240], P(('dp', 'ctx')), may hold values from -0.125 to 0.125
- out_weight: float32 [4096, 2048], P(('dp', 'ctx')), may hold values from -0.375 to 0.375
- gate_up_weight: float32 [2048, 8192], P(('dp', 'ctx')), may hold values from -0.125 to 0.125
- down_weight: float32 [4096, 2048], P(('dp', 'ctx')), may hold values from -0.09375 to 0.09375
- in_first: float32 [2048, 8240], P(('dp', 'ctx')), may hold values from -40 to 40
- out_first: float32 [4096, 2048], P(('dp', 'ctx')), may hold values from -40 to 40
- gate_up_first: float32 [2048, 8192], P(('dp', 'ctx')), may hold values from -40 to 40
- down_first: float32 [4096, 2048], P(('dp', 'ctx')), may hold values from -40 to 40
- in_second: float32 [2048, 8240], P(('dp', 'ctx')), may hold values from 212.992 to 868.352
- out_second: float32 [4096, 2048], P(('dp', 'ctx')), may hold values from 212.992 to 868.352
- gate_up_second: float32 [2048, 8192], P(('dp', 'ctx')), may hold values from 212.992 to 868.352
- down_second: float32 [4096, 2048], P(('dp', 'ctx')), may hold values from 212.992 to 868.352
- small_params: float32 [7312], replicated, may hold values from -5 to 1.5
- small_first: float32 [7312], replicated, may hold values from -80 to 80
- small_second: float32 [7312], replicated, may hold values from 819.2 to 3276.8
Outputs:
- block_output: bfloat16 [8, 2048, 2048], P('dp', 'ctx')
- input_grad: float32 [8, 2048, 2048], P('dp', 'ctx')
- new_in_weight: float32 [2048, 8240], P(('dp', 'ctx'))
- new_in_first: float32 [2048, 8240], P(('dp', 'ctx'))
- new_in_second: float32 [2048, 8240], P(('dp', 'ctx'))
- new_out_weight: float32 [4096, 2048], P(('dp', 'ctx'))
- new_out_first: float32 [4096, 2048], P(('dp', 'ctx'))
- new_out_second: float32 [4096, 2048], P(('dp', 'ctx'))
- new_gate_up_weight: float32 [2048, 8192], P(('dp', 'ctx'))
- new_gate_up_first: float32 [2048, 8192], P(('dp', 'ctx'))
- new_gate_up_second: float32 [2048, 8192], P(('dp', 'ctx'))
- new_down_weight: float32 [4096, 2048], P(('dp', 'ctx'))
- new_down_first: float32 [4096, 2048], P(('dp', 'ctx'))
- new_down_second: float32 [4096, 2048], P(('dp', 'ctx'))
- new_small_params: float32 [7312], replicated
- new_small_first: float32 [7312], replicated
- new_small_second: float32 [7312], replicated
The draws below stay inside these ranges and needn't reach their ends.
All inputs are finite; a program needn't handle non-finite values.
Results may differ from the reference program's by a relative error of at most 0.013.
The reference program's roundings to bfloat16 on the way count: a program that leaves them out, or rounds other values in their place, can miss the bound.
Values may be sent and summed in bfloat16 or wider, within the bound.
No kernel may reach another device: no remote copies, remote signals or barrier semaphores. Data moves between devices by JAX's collectives and lax.ppermute only.
A program may use at most 576 MiB of HBM per device.

```python
import math
import jax
import jax.numpy as jnp
import numpy as np
from jax import lax

D = 2048
FF = 4096
QH = 8
KVH = 2
HD = 128
HEADS_M = 48
HEAD_M = 64
STATE = 256
SEQ = 2048
DOC_MOST = 800
SEGS = 6
STEP = 10
DSSM = 3072
F_IN = 8240
SMALL = 7312
SEQS = 8
TOKENS = 16384


def draw_out_weight(key, part):
    key = jax.random.fold_in(key, 11)
    rows = HEADS_M * HEAD_M + QH * HD
    base = jnp.clip(jax.random.normal(key, (rows, D), jnp.float32), -6.0, 6.0) * rows ** (-0.5)
    factor = jnp.where(jnp.arange(rows) < HEADS_M * HEAD_M, 1.0, 4.0)
    return base * factor[:, None]


def draw_small_params(key, part):
    key = jax.random.fold_in(key, 7)
    keys = jax.random.split(key, 6)
    gain_in = jax.random.uniform(keys[0], (D,), jnp.float32, 0.5, 1.5)
    gain_mid = jax.random.uniform(keys[1], (D,), jnp.float32, 0.5, 1.5)
    gain_mix = jax.random.uniform(keys[2], (HEADS_M * HEAD_M,), jnp.float32, 0.5, 1.5)
    step_bias = jax.random.uniform(keys[3], (HEADS_M,), jnp.float32, -5.0, -3.0)
    decay_log = jax.random.uniform(keys[4], (HEADS_M,), jnp.float32, -4.0, 0.7)
    skip = jax.random.uniform(keys[5], (HEADS_M,), jnp.float32, 0.5, 1.5)
    return jnp.concatenate([gain_in, gain_mid, gain_mix, step_bias, decay_log, skip])


def steps_of(rng, shape, cuts, smallest, largest):
    level = 1.0
    for position, blocks in cuts:
        steps = jax.random.uniform(jax.random.fold_in(jax.random.fold_in(rng, 6), position), (blocks,), jnp.float32, smallest / len(cuts), largest / len(cuts))
        level = level * jnp.repeat(jnp.exp(steps), shape[position] // blocks).reshape((-1,) + (1,) * (len(shape) - 1 - position))
    return level


def length_profile(number_of, total, most, lean):
    loads = [(1 << 20) // math.isqrt(grade ** lean) + 1 for grade in range(2, number_of + 1)]
    spare, counts = total - most - (number_of - 1), [1] * (number_of - 1)
    while spare > 0:
        free = [i for i in range(number_of - 1) if counts[i] < most]
        whole, left = sum([loads[i] for i in free]), spare
        for i in free:
            more = min(most - counts[i], max(1, left * loads[i] // whole), spare)
            counts[i] = counts[i] + more
            spare = spare - more
    return np.array([most] + counts)


def ragged_sizes(key, amount, total, most, lean):
    if amount == 2:
        one = jax.random.randint(key, (), max(1, total - most), min(most, total - 1) + 1)
        return jnp.stack([one, total - one])
    sizes = jnp.asarray(length_profile(amount, total, most, lean), jnp.int32)
    pairs = (amount - 1) // 2
    source_of, receiver = sizes[1:1 + 2 * pairs:2], sizes[2:2 + 2 * pairs:2]
    slack = jnp.minimum(source_of - 1, most - receiver)
    shifted = jax.random.randint(jax.random.fold_in(key, 1), (pairs,), 0, 1 << 20) % (slack + 1)
    sizes = sizes.at[1:1 + 2 * pairs:2].set(source_of - shifted).at[2:2 + 2 * pairs:2].set(receiver + shifted)
    return sizes[jax.random.permutation(jax.random.fold_in(key, 2), amount)]


def noise(key, shape, scale, reach, shards=(), dtype=jnp.bfloat16):
    drawn = scale * jax.random.normal(key, shape, jnp.float32)
    if shards:
        drawn = drawn * steps_of(key, shape, shards, -0.22, 0.18)
    return jnp.clip(drawn, -reach, reach).astype(dtype)


def setup_inputs(seed: int = 0) -> dict:
    streams_of = jax.random.split(jax.random.key(seed), 19)
    block_input = noise(streams_of[0], (SEQS, SEQ, D), 1.0, 6.0, ((0, 8), (1, 4)))
    segment_ids = jax.vmap(lambda own: jnp.searchsorted(jnp.cumsum(ragged_sizes(own, SEGS, SEQ, DOC_MOST, 0)), jnp.arange(SEQ), side="right"))(jax.random.split(streams_of[1], SEQS)).reshape((SEQS, SEQ)).astype(jnp.int32)
    cotangent = noise(streams_of[2], (SEQS, SEQ, D), 1.0, 6.0, ((0, 8), (1, 4)))
    in_weight = noise(streams_of[3], (D, F_IN), D ** -0.5, 0.125, ((0, 32),), jnp.float32)
    out_weight = draw_out_weight(jax.random.fold_in(streams_of[18], 71), 0)
    gate_up_weight = noise(streams_of[5], (D, 2 * FF), D ** -0.5, 0.125, ((0, 32),), jnp.float32)
    down_weight = noise(streams_of[6], (FF, D), FF ** -0.5, 0.09375, ((0, 32),), jnp.float32)
    in_first = noise(streams_of[7], (D, F_IN), (0.056 * TOKENS ** 0.5), 40.0, ((0, 32),), jnp.float32)
    out_first = noise(streams_of[8], (DSSM + QH * HD, D), (0.056 * TOKENS ** 0.5), 40.0, ((0, 32),), jnp.float32)
    gate_up_first = noise(streams_of[9], (D, 2 * FF), (0.056 * TOKENS ** 0.5), 40.0, ((0, 32),), jnp.float32)
    down_first = noise(streams_of[10], (FF, D), (0.056 * TOKENS ** 0.5), 40.0, ((0, 32),), jnp.float32)
    in_second = jnp.clip(jnp.exp(math.log(868.352) - 1.40534252 * jax.random.uniform(streams_of[11], (D, F_IN), jnp.float32) ** steps_of(streams_of[11], (D, F_IN), ((0, 32),), -0.2, 0.2)), 212.992, 868.352)
    out_second = jnp.clip(jnp.exp(math.log(868.352) - 1.40534252 * jax.random.uniform(streams_of[12], (DSSM + QH * HD, D), jnp.float32) ** steps_of(streams_of[12], (DSSM + QH * HD, D), ((0, 32),), -0.2, 0.2)), 212.992, 868.352)
    gate_up_second = jnp.clip(jnp.exp(math.log(868.352) - 1.40534252 * jax.random.uniform(streams_of[13], (D, 2 * FF), jnp.float32) ** steps_of(streams_of[13], (D, 2 * FF), ((0, 32),), -0.2, 0.2)), 212.992, 868.352)
    down_second = jnp.clip(jnp.exp(math.log(868.352) - 1.40534252 * jax.random.uniform(streams_of[14], (FF, D), jnp.float32) ** steps_of(streams_of[14], (FF, D), ((0, 32),), -0.2, 0.2)), 212.992, 868.352)
    small_params = draw_small_params(jax.random.fold_in(streams_of[18], 71), 0)
    small_first = noise(streams_of[16], (SMALL,), (0.11 * TOKENS ** 0.5), 80.0, (), jnp.float32)
    small_second = jnp.clip(jnp.exp(jax.random.uniform(streams_of[17], (SMALL,), jnp.float32, math.log(819.2), math.log(3276.8))), 819.2, 3276.8)
    return dict(block_input=block_input, segment_ids=segment_ids, cotangent=cotangent, in_weight=in_weight, out_weight=out_weight, gate_up_weight=gate_up_weight, down_weight=down_weight, in_first=in_first, out_first=out_first, gate_up_first=gate_up_first, down_first=down_first, in_second=in_second, out_second=out_second, gate_up_second=gate_up_second, down_second=down_second, small_params=small_params, small_first=small_first, small_second=small_second)


highest = lax.Precision.HIGHEST
norm_eps = 1e-05
beta_one = 0.9
beta_two = 0.95
adam_eps = 1e-08
weight_decay = 0.1
rate_scale = 3.0
small_rate = 0.3

@jax.custom_vjp
def low(v):
    return lax.optimization_barrier(v.astype(jnp.bfloat16)).astype(jnp.float32)

@jax.custom_vjp
def low_back(v):
    return v

def low_keep(v):
    return (low(v), None)

def low_pass(kept, grad):
    return (grad,)

def back_keep(v):
    return (v, None)

def back_low(kept, grad):
    return (low(grad),)
low.defvjp(low_keep, low_pass)
low_back.defvjp(back_keep, back_low)

def rms_scale(values):
    return lax.rsqrt(lax.optimization_barrier(jnp.mean(values * values, axis=-1, keepdims=True)) + norm_eps)

def split_small(small):
    widths = [D, D, HEADS_M * HEAD_M, HEADS_M, HEADS_M, HEADS_M]
    pieces = []
    start = 0
    for count in widths:
        pieces.append(small[start:start + count])
        start += count
    return pieces

def span_terms(streams, writes, reads, raw_step, segment, before, step_bias, decay_log, skip):
    step_size = jax.nn.softplus(raw_step + step_bias)
    rates = -jnp.exp(decay_log) * step_size
    total = jnp.cumsum(rates, axis=0)
    length = segment.shape[0]
    order = jnp.arange(length)
    causal = (order[:, None] >= order[None, :]) & (segment[:, None] == segment[None, :])
    spread = total[:, None, :] - total[None, :, :]
    decays = jnp.exp(jnp.where(causal[:, :, None], spread, -1e+30))
    intersections = jnp.dot(reads, writes.T, precision=highest, preferred_element_type=jnp.float32)
    scaled = streams * step_size[:, :, None]
    mixing = decays * intersections[:, :, None]
    local_out = jnp.einsum('tsh,shp->thp', mixing, scaled, precision=highest) + skip[None, :, None] * streams
    last = length - 1
    keep_last = segment == segment[last]
    to_end = jnp.exp(jnp.where(keep_last[:, None], total[last][None, :] - total, -1e+30))
    state_part = jnp.einsum('sh,shp,sn->hpn', to_end, scaled, writes, precision=highest)
    entering = (segment == before).astype(jnp.float32)
    from_start = jnp.exp(total) * entering[:, None]
    through = from_start[last]
    return (local_out, state_part, through, from_start)

def sequence_scan(streams, writes, reads, raw_step, segment, step_bias, decay_log, skip):
    block = math.gcd(SEQ, 256)
    count = SEQ // block

    def advance(carry, pieces):
        state, before = carry
        part_streams, part_writes, part_reads, part_raw, part_seg = pieces
        local_out, state_part, through, from_start = span_terms(part_streams, part_writes, part_reads, part_raw, part_seg, before, step_bias, decay_log, skip)
        output = local_out + from_start[:, :, None] * jnp.einsum('tn,hpn->thp', part_reads, state, precision=highest)
        state = through[:, None, None] * state + state_part
        return ((state, part_seg[block - 1]), output)
    start = (jnp.zeros((HEADS_M, HEAD_M, STATE), jnp.float32), jnp.full((), -1, jnp.int32))
    pieces = tuple((item.reshape((count, block) + item.shape[1:]) for item in (streams, writes, reads, raw_step, segment)))
    carry, outputs = lax.scan(jax.checkpoint(advance), start, pieces)
    return outputs.reshape(streams.shape)

def attend(queries, keys, values, segment):
    size = math.gcd(SEQ, 512)
    count = SEQ // size
    group = QH // KVH
    places = jnp.arange(SEQ)
    scale = HD ** (-0.5)

    def one_block(pieces):
        query_block, seg_block, place_block = pieces
        query_groups = query_block.reshape(size, KVH, group, HD)
        scores = jnp.einsum('qkgd,skd->kgqs', query_groups, keys, precision=highest) * scale
        scores = low_back(scores)
        allowed = (places[None, :] <= place_block[:, None]) & (segment[None, :] == seg_block[:, None])
        scores = jnp.where(allowed[None, None], scores, -1e+30)
        peak = lax.optimization_barrier(jnp.max(scores, axis=-1, keepdims=True))
        expo = jnp.exp(scores - peak)
        shares = low(expo / lax.optimization_barrier(jnp.sum(expo, axis=-1, keepdims=True)))
        mixed = jnp.einsum('kgqs,skd->qkgd', shares, values, precision=highest)
        return mixed.reshape(size, QH * HD)
    pieces = (queries.reshape(count, size, QH, HD), segment.reshape(count, size), places.reshape(count, size))
    return lax.map(jax.checkpoint(one_block), pieces).reshape(SEQ, QH * HD)

def layer_forward(tokens, segment, wide_in, wide_out, wide_gate_up, wide_down, small):
    gain_in, gain_mid, gain_mix, step_bias, decay_log, skip = split_small(small)
    mixer_width = HEADS_M * HEAD_M
    normed = low(tokens * rms_scale(tokens) * gain_in)
    project = low_back(jnp.dot(normed, wide_in, precision=highest, preferred_element_type=jnp.float32))
    gate_z = project[:, :mixer_width]
    streams = project[:, mixer_width:2 * mixer_width].reshape(SEQ, HEADS_M, HEAD_M)
    writes = project[:, 2 * mixer_width:2 * mixer_width + STATE]
    reads = project[:, 2 * mixer_width + STATE:2 * mixer_width + 2 * STATE]
    base = 2 * mixer_width + 2 * STATE + HEADS_M
    raw_step = project[:, 2 * mixer_width + 2 * STATE:base]
    queries = low(project[:, base:base + QH * HD]).reshape(SEQ, QH, HD)
    keys = low(project[:, base + QH * HD:base + (QH + KVH) * HD]).reshape(SEQ, KVH, HD)
    values = low(project[:, base + (QH + KVH) * HD:]).reshape(SEQ, KVH, HD)
    scanned = sequence_scan(streams, writes, reads, raw_step, segment, step_bias, decay_log, skip).reshape(SEQ, mixer_width)
    gated = scanned * jax.nn.silu(gate_z)
    unit_mix = gated * rms_scale(gated)
    attended = low_back(attend(queries, keys, values, segment))
    joined = low(jnp.concatenate([unit_mix * gain_mix, attended], axis=1))
    mixed = low_back(jnp.dot(joined, wide_out, precision=highest, preferred_element_type=jnp.float32))
    middle = tokens + mixed
    normed_mid = low(middle * rms_scale(middle) * gain_mid)
    gate_up = low_back(jnp.dot(normed_mid, wide_gate_up, precision=highest, preferred_element_type=jnp.float32))
    hidden = low(jax.nn.silu(gate_up[:, :FF]) * gate_up[:, FF:])
    return middle + low_back(jnp.dot(hidden, wide_down, precision=highest, preferred_element_type=jnp.float32))

def adam_step(weight, grad, first, second, rate):
    first = beta_one * first + (1.0 - beta_one) * grad
    second = beta_two * second + (1.0 - beta_two) * grad * grad
    fixed_first = first / (1.0 - beta_one ** STEP)
    fixed_second = second / (1.0 - beta_two ** STEP)
    weight = weight - rate * (fixed_first / (jnp.sqrt(fixed_second) + adam_eps) + weight_decay * weight)
    return (weight, first, second)

def reference(block_input, segment_ids, cotangent, in_weight, out_weight, gate_up_weight, down_weight, in_first, out_first, gate_up_first, down_first, in_second, out_second, gate_up_second, down_second, small_params, small_first, small_second):
    tokens = block_input.astype(jnp.float32)
    back = cotangent.astype(jnp.float32)

    def whole(tokens, w_in, w_out, w_gate_up, w_down, small):
        wide_in = low(w_in)
        wide_out = low(w_out)
        wide_gate_up = low(w_gate_up)
        wide_down = low(w_down)

        def one_sequence(pieces):
            seq_tokens, seq_segment = pieces
            return layer_forward(seq_tokens, seq_segment, wide_in, wide_out, wide_gate_up, wide_down, small)
        return lax.map(jax.checkpoint(one_sequence), (tokens, segment_ids))
    outputs, pullback = jax.vjp(whole, tokens, in_weight, out_weight, gate_up_weight, down_weight, small_params)
    grad_tokens, grad_in, grad_out, grad_gate_up, grad_down, grad_small = pullback(back)
    new_in = adam_step(in_weight, grad_in, in_first, in_second, rate_scale / math.sqrt(D))
    new_out = adam_step(out_weight, grad_out, out_first, out_second, rate_scale / math.sqrt(HEADS_M * HEAD_M + QH * HD))
    new_gate_up = adam_step(gate_up_weight, grad_gate_up, gate_up_first, gate_up_second, rate_scale / math.sqrt(D))
    new_down = adam_step(down_weight, grad_down, down_first, down_second, rate_scale / math.sqrt(FF))
    new_small = adam_step(small_params, grad_small, small_first, small_second, small_rate)
    return (outputs.astype(jnp.bfloat16), grad_tokens, new_in[0], new_in[1], new_in[2], new_out[0], new_out[1], new_out[2], new_gate_up[0], new_gate_up[1], new_gate_up[2], new_down[0], new_down[1], new_down[2], new_small[0], new_small[1], new_small[2])
```

```python
import functools
import math

import jax
import jax.numpy as jnp
from jax import lax
from jax.experimental import pallas as pl
from jax.experimental.pallas import tpu as pltpu
from jax.sharding import PartitionSpec as P

D = 2048
FF = 4096
QH = 8
KVH = 2
HD = 128
HEADS_M = 48
HEAD_M = 64
STATE = 256
STEP = 10
DOC_MOST = 800
DSSM = HEADS_M * HEAD_M
SHARED = 2 * STATE + 2 * KVH * HD + 128
CHUNK = 256
QBLOCK = 256

norm_eps = 1e-05
beta_one = 0.9
beta_two = 0.95
adam_eps = 1e-08
weight_decay = 0.1
rate_scale = 3.0
small_rate = 0.3
bf16 = jnp.bfloat16
f32 = jnp.float32
NN = (((1,), (0,)), ((), ()))
NT = (((1,), (1,)), ((), ()))
TN = (((0,), (0,)), ((), ()))


def dot(a, b, dims=NN):
    return lax.dot_general(a, b, dims, preferred_element_type=f32)


def from_ctx(x, m):
    count = lax.axis_size("ctx")
    return lax.ppermute(x, "ctx", [(i ^ m, i) for i in range(count)])


def from_dp(x, j, k):
    count = lax.axis_size("dp")
    inner = count // 4
    pairs = []
    for i in range(count):
        z, w = divmod(i, inner)
        pairs.append((((z + j) % 4) * inner + (w + k) % inner, i))
    return lax.ppermute(x, "dp", pairs)


def to_dp(x, j, k):
    return from_dp(x, -j, -k)


ORDER = (2, 1, 3, 0)


def gather_dp(own):
    inner = lax.axis_size("dp") // 4
    blocks = {(0, 0): own}
    for j in (2, 1, 3):
        blocks[j, 0] = from_dp(own, j, 0)
    for j in (0, 1, 3, 2):
        for k in range(1, inner):
            blocks[j, k] = from_dp(blocks[j, 0], 0, k)
    return blocks


def dp_index(j, k):
    count = lax.axis_size("dp")
    inner = count // 4
    place = lax.axis_index("dp")
    return lax.rem(place // inner + j, 4) * inner + lax.rem(lax.rem(place, inner) + k, inner)


def place_dp(blocks):
    own = blocks[0, 0]
    full = jnp.zeros((lax.axis_size("dp"),) + own.shape, own.dtype)
    for (j, k), block in blocks.items():
        full = lax.dynamic_update_index_in_dim(full, block, dp_index(j, k), 0)
    return full


def scatter_dp(full):
    inner = lax.axis_size("dp") // 4

    def part(j, k):
        return lax.dynamic_index_in_dim(full, dp_index(j, k), 0, False)

    rows = {}
    for j in ORDER:
        total = part(j, 0).astype(f32)
        for k in range(1, inner):
            total = total + to_dp(part(j, k), 0, k).astype(f32)
        rows[j] = total
    total = rows[0]
    for j in (2, 1, 3):
        total = total + to_dp(rows[j].astype(bf16), j, 0).astype(f32)
    return total


def gather_ctx(own):
    count = lax.axis_size("ctx")
    blocks = {0: own}
    for m in range(2, count, 2):
        blocks[m] = from_ctx(own, m)
    for m in range(0, count, 2):
        blocks[m + 1] = from_ctx(blocks[m], 1)
    return blocks


def place_ctx(blocks):
    own = blocks[0]
    place = lax.axis_index("ctx")
    full = jnp.zeros((lax.axis_size("ctx"),) + own.shape, own.dtype)
    for m, block in blocks.items():
        full = lax.dynamic_update_index_in_dim(full, block, place ^ m, 0)
    return full


def scatter_ctx(part):
    count = lax.axis_size("ctx")
    sums = {}
    for m in [m for m in range(2, count, 2)] + [0]:
        sums[m] = part(m).astype(f32) + from_ctx(part(m + 1), 1).astype(f32)
    total = sums[0]
    for m in range(2, count, 2):
        total = total + from_ctx(sums[m].astype(bf16), m).astype(f32)
    return total


def exchange_ctx(blocks):
    place = lax.axis_index("ctx")
    got = {}
    for m in range(lax.axis_size("ctx")):
        own = lax.dynamic_index_in_dim(blocks, place ^ m, 0, False)
        got[m] = from_ctx(own, m) if m else own
    return place_ctx(got)


def sum_ctx(x):
    m = 1
    while m < lax.axis_size("ctx"):
        x = x + from_ctx(x, m)
        m *= 2
    return x


def split_cols(a, block):
    count = lax.axis_size("ctx")
    rows, n = a.shape
    a = a.reshape(rows, n // (count * block), count, block)
    return a.transpose(2, 0, 1, 3).reshape(count, rows, n // count)


def join_cols(a, block):
    count, rows, n = a.shape
    a = a.reshape(count, rows, n // block, block)
    return a.transpose(1, 2, 0, 3).reshape(rows, count * n)


def own_cols(a, block):
    count = lax.axis_size("ctx")
    rows, n = a.shape
    a = a.reshape(rows, n // (count * block), count, block)
    a = lax.dynamic_index_in_dim(a, lax.axis_index("ctx"), 2, False)
    return a.reshape(rows, n // count)


def spread_cols(a, block):
    count = lax.axis_size("ctx")
    rows, n = a.shape
    a = a.reshape(rows, n // block, block)
    full = jnp.zeros((rows, n // block, count, block), a.dtype)
    full = lax.dynamic_update_index_in_dim(full, a, lax.axis_index("ctx"), 2)
    return full.reshape(rows, count * n)


def attention_window(total_len):
    reach = -(-(DOC_MOST - 1) // QBLOCK) * QBLOCK
    return min(reach, total_len - QBLOCK), min(reach + QBLOCK, total_len)


def attention_scores(total_len, q_ref, k_ref, col_ref, row_ref):
    back, window = attention_window(total_len)
    first = pl.program_id(1) * QBLOCK
    start = pl.multiple_of(jnp.maximum(first - back, 0), QBLOCK)
    keys = k_ref[pl.ds(start, window), :]
    scores = dot(q_ref[...], keys, NT) * HD ** (-0.5)
    query_place = first + lax.broadcasted_iota(jnp.int32, (QBLOCK, window), 0)
    key_place = start + lax.broadcasted_iota(jnp.int32, (QBLOCK, window), 1)
    key_seg = row_ref[0:1, pl.ds(start, window)]
    allowed = (key_place <= query_place) & (col_ref[:, 0:1] == key_seg)
    return start, window, keys, jnp.where(allowed, scores, -1e30)


def attend_kernel(total_len, q_ref, k_ref, v_ref, col_ref, row_ref, out_ref, log_ref):
    start, window, _, scores = attention_scores(total_len, q_ref, k_ref, col_ref, row_ref)
    peak = jnp.max(scores, axis=1, keepdims=True)
    expo = jnp.exp(scores - peak)
    log_total = peak + jnp.log(jnp.sum(expo, axis=1, keepdims=True))
    shares = jnp.exp(scores - log_total).astype(bf16)
    out_ref[...] = dot(shares, v_ref[pl.ds(start, window), :]).astype(out_ref.dtype)
    log_ref[...] = jnp.broadcast_to(log_total, log_ref.shape)


def attend_back_kernel(
    total_len, q_ref, k_ref, v_ref, col_ref, row_ref, log_ref, grad_ref, dq_ref, dk_ref, dv_ref
):
    @pl.when(pl.program_id(1) == 0)
    def _():
        dk_ref[...] = jnp.zeros_like(dk_ref)
        dv_ref[...] = jnp.zeros_like(dv_ref)

    start, window, keys, scores = attention_scores(total_len, q_ref, k_ref, col_ref, row_ref)
    shares = jnp.exp(scores - log_ref[:, 0:1])
    grad = grad_ref[...]
    grad_shares = dot(grad, v_ref[pl.ds(start, window), :], NT)
    inner = jnp.sum(shares * grad_shares, axis=1, keepdims=True)
    grad_scores = (shares * (grad_shares - inner)).astype(bf16)
    scale = HD ** (-0.5)
    dq_ref[...] = dot(grad_scores, keys) * scale
    span = pl.ds(start, window)
    dk_ref[span, :] += dot(grad_scores, q_ref[...], TN) * scale
    dv_ref[span, :] += dot(shares.astype(bf16), grad, TN)


def attention_specs(total_len):
    tile = pl.BlockSpec((QBLOCK, HD), lambda h, i: (i, h))
    whole = pl.BlockSpec((total_len, HD), lambda h, i: (0, h))
    col = pl.BlockSpec((QBLOCK, 128), lambda h, i: (i, 0))
    row = pl.BlockSpec((8, total_len), lambda h, i: (0, 0))
    return tile, whole, col, row


def attention_call(queries, keys, values, seg_col, seg_row):
    total_len, width = queries.shape
    tile, whole, col, row = attention_specs(total_len)
    return pl.pallas_call(
        functools.partial(attend_kernel, total_len),
        grid=(width // HD, total_len // QBLOCK),
        in_specs=[tile, whole, whole, col, row],
        out_specs=[tile, tile],
        out_shape=[
            jax.ShapeDtypeStruct((total_len, width), bf16),
            jax.ShapeDtypeStruct((total_len, width), f32),
        ],
        compiler_params=pltpu.CompilerParams(vmem_limit_bytes=48 * 2**20),
        cost_estimate=pl.CostEstimate(
            flops=4 * total_len * 1280 * width, bytes_accessed=12 * total_len * width, transcendentals=0
        ),
        name="attend",
    )(queries, keys, values, seg_col, seg_row)


def attention_back_call(queries, keys, values, seg_col, seg_row, log_total, grad):
    total_len, width = queries.shape
    tile, whole, col, row = attention_specs(total_len)
    return pl.pallas_call(
        functools.partial(attend_back_kernel, total_len),
        grid=(width // HD, total_len // QBLOCK),
        in_specs=[tile, whole, whole, col, row, tile, tile],
        out_specs=[tile, whole, whole],
        out_shape=[jax.ShapeDtypeStruct((total_len, width), f32)] * 3,
        compiler_params=pltpu.CompilerParams(vmem_limit_bytes=48 * 2**20),
        cost_estimate=pl.CostEstimate(
            flops=10 * total_len * 1280 * width, bytes_accessed=24 * total_len * width, transcendentals=0
        ),
        name="attend_back",
    )(queries, keys, values, seg_col, seg_row, log_total, grad)


def pair_of(col, offset, j, left):
    a = offset + 2 * j
    return jnp.where(left, col[:, a : a + 1], col[:, a + 1 : a + 2])


def state_decay(col, j, left_rows):
    last = col[CHUNK - 1 : CHUNK, :]
    a = 64 + 2 * j
    return jnp.where(left_rows, last[:, a : a + 1], last[:, a + 1 : a + 2])


def scan_kernel(pairs, x_ref, k_ref, r_ref, col_ref, row_ref, skip_ref, y_ref, s_ref, state):
    @pl.when(pl.program_id(0) == 0)
    def _():
        state[...] = jnp.zeros_like(state)

    writes = k_ref[...].astype(bf16)
    reads = r_ref[...].astype(bf16)
    col = col_ref[...]
    row = row_ref[...]
    entering = state[...].astype(bf16)
    s_ref[0] = entering
    products = dot(reads, writes, NT)
    later = lax.broadcasted_iota(jnp.int32, (CHUNK, CHUNK), 0)
    earlier = lax.broadcasted_iota(jnp.int32, (CHUNK, CHUNK), 1)
    mask = (later >= earlier) & (col[:, 127:128] == row[16:17, :])
    left = lax.broadcasted_iota(jnp.int32, (CHUNK, 128), 1) < HEAD_M
    left_rows = lax.broadcasted_iota(jnp.int32, (128, STATE), 0) < HEAD_M
    through = dot(reads, entering, NT)
    for j in range(pairs):
        lanes = slice(128 * j, 128 * j + 128)
        x = x_ref[:, lanes]
        scaled = x * pair_of(col, 32, j, left)
        scaled_low = scaled.astype(bf16)
        outs = []
        for h in (2 * j, 2 * j + 1):
            spread = col[:, h : h + 1] - row[h : h + 1, :]
            mixing = jnp.exp(jnp.where(mask, spread, -1e30)) * products
            outs.append(dot(mixing.astype(bf16), scaled_low))
        y_ref[:, lanes] = (
            jnp.where(left, outs[0], outs[1])
            + pair_of(col, 64, j, left) * through[:, lanes]
            + skip_ref[0:1, lanes] * x
        )
        to_end = (scaled * pair_of(col, 96, j, left)).astype(bf16)
        state[lanes, :] = state_decay(col, j, left_rows) * state[lanes, :] + dot(to_end, writes, TN)


def scan_back_kernel(
    pairs,
    x_ref,
    k_ref,
    r_ref,
    col_ref,
    row_ref,
    skip_ref,
    y_ref,
    s_ref,
    dy_ref,
    sum_ref,
    dx_ref,
    dk_ref,
    dr_ref,
    red_ref,
    tot_ref,
    adjoint,
    keep,
):
    @pl.when(pl.program_id(0) == 0)
    def _():
        adjoint[...] = jnp.zeros_like(adjoint)

    writes = k_ref[...].astype(bf16)
    reads = r_ref[...].astype(bf16)
    col = col_ref[...]
    row = row_ref[...]
    entering = s_ref[0]
    products = dot(writes, reads, NT)
    earlier = lax.broadcasted_iota(jnp.int32, (CHUNK, CHUNK), 0)
    later = lax.broadcasted_iota(jnp.int32, (CHUNK, CHUNK), 1)
    mask = (later >= earlier) & (col[:, 127:128] == row[16:17, :])
    left = lax.broadcasted_iota(jnp.int32, (CHUNK, 128), 1) < HEAD_M
    left_rows = lax.broadcasted_iota(jnp.int32, (128, STATE), 0) < HEAD_M
    incoming = adjoint[...]
    incoming_low = incoming.astype(bf16)
    values = dot(writes, incoming_low, NT)
    grad_products = jnp.zeros((CHUNK, CHUNK), f32)
    grad_writes = jnp.zeros((CHUNK, STATE), f32)
    grad_reads = jnp.zeros((CHUNK, STATE), f32)
    tot_ref[0] = jnp.zeros(tot_ref.shape[1:], f32)
    for j in range(pairs):
        lanes = slice(128 * j, 128 * j + 128)
        x = x_ref[:, lanes]
        step = pair_of(col, 32, j, left)
        scaled = x * step
        scaled_low = scaled.astype(bf16)
        dy = dy_ref[:, lanes]
        dy_low = dy.astype(bf16)
        grads = []
        for side, h in enumerate((2 * j, 2 * j + 1)):
            spread = row[h : h + 1, :] - col[:, h : h + 1]
            decay = jnp.exp(jnp.where(mask, spread, -1e30))
            half = left if side == 0 else jnp.logical_not(left)
            grad_mixing = dot(jnp.where(half, scaled_low, jnp.zeros_like(scaled_low)), dy_low, NT)
            grad_products += grad_mixing * decay
            grads.append(dot((decay * products).astype(bf16), dy_low))
        grad_scaled = jnp.where(left, grads[0], grads[1])
        decay_end = pair_of(col, 96, j, left)
        to_end = (scaled * decay_end).astype(bf16)
        passed = to_end.astype(f32) * values[:, lanes]
        skip = skip_ref[0:1, lanes]
        flow = (
            dy_low.astype(f32) * (y_ref[:, lanes] - skip * x)
            - scaled_low.astype(f32) * grad_scaled
            - passed
        )
        grad_scaled += decay_end * values[:, lanes]
        dx_ref[:, lanes] = step * grad_scaled + skip * dy
        from_start = (pair_of(col, 64, j, left) * dy).astype(bf16)
        grad_reads += dot(from_start, entering[lanes, :])
        grad_writes += dot(to_end, incoming_low[lanes, :])
        pieces = (flow, x * grad_scaled)
        for n, piece in enumerate(pieces):
            high = piece.astype(bf16)
            keep[2 * n, :, lanes] = high
            keep[2 * n + 1, :, lanes] = (piece - high.astype(f32)).astype(bf16)
        tot_ref[0, 1:2, lanes] = jnp.sum(passed, axis=0, keepdims=True)
        tot_ref[0, 2:3, lanes] = jnp.sum(dy * x, axis=0, keepdims=True)
        product = incoming[lanes, :] * entering[lanes, :].astype(f32)
        high = product.astype(bf16)
        low = (product - high.astype(f32)).astype(bf16)
        ones = jnp.ones((8, STATE), bf16)
        tot_ref[0, 0:1, lanes] = (dot(ones, high, NT) + dot(ones, low, NT))[0:1, :]
        adjoint[lanes, :] = state_decay(col, j, left_rows) * incoming[lanes, :] + dot(
            from_start, reads, TN
        )
    grad_products = grad_products.astype(bf16)
    dk_ref[...] = grad_writes + dot(grad_products, reads)
    dr_ref[...] = grad_reads + dot(grad_products, writes, TN)
    sums = sum_ref[...]
    red_ref[...] = (
        dot(keep[0], sums[0]) + dot(keep[1], sums[0]) + dot(keep[2], sums[1]) + dot(keep[3], sums[1])
    )


def scan_call(own, shared, col, row, skip, width):
    total_len = own.shape[0]
    count = total_len // CHUNK
    return pl.pallas_call(
        functools.partial(scan_kernel, width // 128),
        grid=(count,),
        in_specs=[
            pl.BlockSpec((CHUNK, width), lambda i: (i, 1)),
            pl.BlockSpec((CHUNK, STATE), lambda i: (i, 0)),
            pl.BlockSpec((CHUNK, STATE), lambda i: (i, 1)),
            pl.BlockSpec((CHUNK, 128), lambda i: (i, 0)),
            pl.BlockSpec((24, CHUNK), lambda i: (0, i)),
            pl.BlockSpec((8, width), lambda i: (0, 0)),
        ],
        out_specs=[
            pl.BlockSpec((CHUNK, width), lambda i: (i, 0)),
            pl.BlockSpec((1, width, STATE), lambda i: (i, 0, 0)),
        ],
        out_shape=[
            jax.ShapeDtypeStruct((total_len, width), f32),
            jax.ShapeDtypeStruct((count, width, STATE), bf16),
        ],
        scratch_shapes=[pltpu.VMEM((width, STATE), f32)],
        compiler_params=pltpu.CompilerParams(vmem_limit_bytes=48 * 2**20),
        cost_estimate=pl.CostEstimate(
            flops=8 * total_len * width * STATE, bytes_accessed=12 * total_len * width, transcendentals=0
        ),
        name="state_scan",
    )(own, shared, shared, col, row, skip)


def scan_back_call(own, shared, col, row, skip, scanned, states, grad, width):
    total_len = own.shape[0]
    count = total_len // CHUNK
    owner = jnp.arange(width)[:, None] // HEAD_M
    lane = jnp.arange(128)[None, :]
    sums = jnp.stack([owner == lane, owner + 32 == lane]).astype(bf16)

    def back(i):
        return count - 1 - i

    return pl.pallas_call(
        functools.partial(scan_back_kernel, width // 128),
        grid=(count,),
        in_specs=[
            pl.BlockSpec((CHUNK, width), lambda i: (back(i), 1)),
            pl.BlockSpec((CHUNK, STATE), lambda i: (back(i), 0)),
            pl.BlockSpec((CHUNK, STATE), lambda i: (back(i), 1)),
            pl.BlockSpec((CHUNK, 128), lambda i: (back(i), 0)),
            pl.BlockSpec((24, CHUNK), lambda i: (0, back(i))),
            pl.BlockSpec((8, width), lambda i: (0, 0)),
            pl.BlockSpec((CHUNK, width), lambda i: (back(i), 0)),
            pl.BlockSpec((1, width, STATE), lambda i: (back(i), 0, 0)),
            pl.BlockSpec((CHUNK, width), lambda i: (back(i), 0)),
            pl.BlockSpec((2, width, 128), lambda i: (0, 0, 0)),
        ],
        out_specs=[
            pl.BlockSpec((CHUNK, width), lambda i: (back(i), 0)),
            pl.BlockSpec((CHUNK, STATE), lambda i: (back(i), 0)),
            pl.BlockSpec((CHUNK, STATE), lambda i: (back(i), 0)),
            pl.BlockSpec((CHUNK, 128), lambda i: (back(i), 0)),
            pl.BlockSpec((1, 8, width), lambda i: (back(i), 0, 0)),
        ],
        out_shape=[
            jax.ShapeDtypeStruct((total_len, width), f32),
            jax.ShapeDtypeStruct((total_len, STATE), f32),
            jax.ShapeDtypeStruct((total_len, STATE), f32),
            jax.ShapeDtypeStruct((total_len, 128), f32),
            jax.ShapeDtypeStruct((count, 8, width), f32),
        ],
        scratch_shapes=[pltpu.VMEM((width, STATE), f32), pltpu.VMEM((4, CHUNK, width), bf16)],
        compiler_params=pltpu.CompilerParams(vmem_limit_bytes=48 * 2**20),
        cost_estimate=pl.CostEstimate(
            flops=20 * total_len * width * STATE, bytes_accessed=24 * total_len * width, transcendentals=0
        ),
        name="state_scan_back",
    )(own, shared, shared, col, row, skip, scanned, states, grad, sums)


def rms_scale(values):
    return lax.rsqrt(jnp.mean(values * values, axis=-1, keepdims=True) + norm_eps)


def norm_back(grad_unit, unit, scale):
    return scale * (grad_unit - unit * jnp.mean(grad_unit * unit, axis=-1, keepdims=True))


def silu_slope(values):
    sigma = jax.nn.sigmoid(values)
    return sigma * (1.0 + values * (1.0 - sigma))


def split_small(small):
    widths = [D, D, DSSM, HEADS_M, HEADS_M, HEADS_M]
    pieces = []
    start = 0
    for count in widths:
        pieces.append(small[start : start + count])
        start += count
    return pieces


def adam_step(weight, grad, first, second, rate):
    first = beta_one * first + (1.0 - beta_one) * grad
    second = beta_two * second + (1.0 - beta_two) * grad * grad
    fixed_first = first / (1.0 - beta_one**STEP)
    fixed_second = second / (1.0 - beta_two**STEP)
    weight = weight - rate * (
        fixed_first / (jnp.sqrt(fixed_second) + adam_eps) + weight_decay * weight
    )
    return (weight, first, second)


def pad_lanes(a, width):
    return jnp.pad(a, ((0, 0), (0, width - a.shape[1])))


def shards(
    block_input,
    segment_ids,
    cotangent,
    in_weight,
    out_weight,
    gate_up_weight,
    down_weight,
    in_first,
    out_first,
    gate_up_first,
    down_first,
    in_second,
    out_second,
    gate_up_second,
    down_second,
    small_params,
    small_first,
    small_second,
):
    peers = lax.axis_size("ctx")
    groups = lax.axis_size("dp")
    place = lax.axis_index("ctx")
    length = block_input.shape[0] * block_input.shape[1]
    total_len = length * peers
    row_block = out_weight.shape[0]
    in_rows = in_weight.shape[0]
    strided = row_block == HD
    width = DSSM // peers
    heads = HEADS_M // peers
    query_heads = QH // peers
    query_width = query_heads * HD
    own_width = 2 * width + query_width
    ff_width = FF // peers
    pair_block = 2 * HEAD_M if strided else width
    query_block = HD if strided else query_width
    head_block = 2 if strided else heads
    gain_in, gain_mid, gain_mix, step_bias, decay_log, skip = split_small(small_params)

    x_own = block_input.reshape(length, D)
    x_blocks = gather_ctx(x_own)
    segments = place_ctx(gather_ctx(segment_ids.reshape(length))).reshape(total_len)

    in_low = in_weight.astype(bf16)
    base = 2 * DSSM + 2 * STATE + HEADS_M
    query_end = base + QH * HD
    shared_low = jnp.concatenate(
        [
            in_low[:, 2 * DSSM : 2 * DSSM + 2 * STATE],
            in_low[:, query_end:],
            in_low[:, 2 * DSSM + 2 * STATE : base],
            jnp.zeros((in_rows, 128 - HEADS_M), bf16),
        ],
        axis=1,
    )
    own_low = jnp.concatenate(
        [
            split_cols(in_low[:, :DSSM], pair_block),
            split_cols(in_low[:, DSSM : 2 * DSSM], pair_block),
            split_cols(in_low[:, base:query_end], query_block),
        ],
        axis=2,
    )
    own_rows = exchange_ctx(own_low).reshape(peers * in_rows, own_width)
    w_own = place_dp(gather_dp(own_rows)).reshape(D, own_width)
    shared_rows = place_dp(gather_dp(shared_low))
    w_shared = place_ctx(gather_ctx(shared_rows))
    w_shared = w_shared.transpose(1, 0, 2, 3).reshape(D, SHARED)
    out_low = out_weight.astype(bf16)
    if strided:
        w_out = place_dp(gather_dp(out_low)).reshape(width + query_width, D)
    else:
        whole_out = lax.all_gather(out_low, ("dp", "ctx"), axis=0, tiled=True)
        w_out = jnp.concatenate(
            [
                lax.dynamic_slice_in_dim(whole_out, place * width, width, 0),
                lax.dynamic_slice_in_dim(whole_out, DSSM + place * query_width, query_width, 0),
            ],
            axis=0,
        )
    gu_low = gate_up_weight.astype(bf16)
    gu_low = jnp.concatenate(
        [split_cols(gu_low[:, :FF], row_block), split_cols(gu_low[:, FF:], row_block)], axis=2
    )
    w_gate_up = exchange_ctx(gu_low).reshape(peers * in_rows, 2 * ff_width)
    w_gate_up = place_dp(gather_dp(w_gate_up)).reshape(D, 2 * ff_width)
    w_down = place_dp(gather_dp(down_weight.astype(bf16))).reshape(ff_width, D)
    cot_blocks = gather_ctx(cotangent.reshape(length, D))

    tokens = place_ctx(x_blocks).reshape(total_len, D).astype(f32)
    scale_in = rms_scale(tokens)
    unit_in = tokens * scale_in
    normed = (unit_in * gain_in).astype(bf16)
    shared = dot(normed, w_shared)
    own = dot(normed, w_own)
    gate_z = own[:, :width]
    queries = own[:, 2 * width :].astype(bf16)
    keys = shared[:, 2 * STATE : 2 * STATE + KVH * HD].astype(bf16)
    values = shared[:, 2 * STATE + KVH * HD : 2 * STATE + 2 * KVH * HD].astype(bf16)
    raw_step = own_cols(shared[:, SHARED - 128 : SHARED - 128 + HEADS_M], head_block)
    if query_heads < KVH:
        own_kv = (place * query_heads * KVH // QH) * HD
        keys = lax.dynamic_slice_in_dim(keys, own_kv, query_width, 1)
        values = lax.dynamic_slice_in_dim(values, own_kv, query_width, 1)
    own_bias = own_cols(step_bias[None, :], head_block)
    own_decay = jnp.exp(own_cols(decay_log[None, :], head_block))
    own_skip = jnp.repeat(own_cols(skip[None, :], head_block), HEAD_M, axis=1)
    own_skip = jnp.broadcast_to(own_skip, (8, width))
    own_gain_mix = own_cols(gain_mix[None, :], pair_block)

    chunks = total_len // CHUNK
    step = jax.nn.softplus(raw_step + own_bias)
    rates = (-own_decay * step).reshape(chunks, CHUNK, heads)
    order = jnp.arange(CHUNK)
    lower = (order[:, None] >= order[None, :]).astype(f32)
    running = jnp.einsum("ts,csh->cth", lower, rates, precision=lax.Precision.HIGHEST)
    seg_chunks = segments.reshape(chunks, CHUNK)
    seg_last = seg_chunks[:, -1:]
    seg_before = jnp.concatenate([jnp.full((1, 1), -1, seg_last.dtype), seg_last[:-1]], axis=0)
    from_start = jnp.exp(running) * (seg_chunks == seg_before).astype(f32)[:, :, None]
    to_end = jnp.exp(
        jnp.where((seg_chunks == seg_last)[:, :, None], running[:, -1:, :] - running, -1e30)
    )
    seg_float = segments.astype(f32)
    running = running.reshape(total_len, heads)
    col = jnp.concatenate(
        [
            pad_lanes(running, 32),
            pad_lanes(step, 32),
            pad_lanes(from_start.reshape(total_len, heads), 32),
            pad_lanes(to_end.reshape(total_len, heads), 31),
            seg_float[:, None],
        ],
        axis=1,
    )
    row = jnp.concatenate(
        [
            jnp.pad(running.T, ((0, 16 - heads), (0, 0))),
            jnp.broadcast_to(seg_float[None, :], (8, total_len)),
        ],
        axis=0,
    )
    seg_col = jnp.broadcast_to(seg_float[:, None], (total_len, 128))
    seg_row = jnp.broadcast_to(seg_float[None, :], (8, total_len))

    scanned, states = scan_call(own, shared, col, row, own_skip, width)
    attended, log_total = attention_call(queries, keys, values, seg_col, seg_row)
    gate_act = jax.nn.silu(gate_z)
    gated = scanned * gate_act
    square = sum_ctx(jnp.sum(gated * gated, axis=-1))
    scale_mix = lax.rsqrt(square / DSSM + norm_eps)[:, None]
    unit_mix = gated * scale_mix
    joined = jnp.concatenate([(unit_mix * own_gain_mix).astype(bf16), attended], axis=1)
    mixed_part = dot(joined, w_out).astype(bf16).reshape(peers, length, D)
    mixed = scatter_ctx(lambda m: lax.dynamic_index_in_dim(mixed_part, place ^ m, 0, False))

    middle = x_own.astype(f32) + mixed
    scale_mid = rms_scale(middle)
    unit_mid = middle * scale_mid
    mid_blocks = gather_ctx((unit_mid * gain_mid).astype(bf16))
    normed_mid = jnp.concatenate([mid_blocks[m] for m in range(peers)], axis=0)
    cot = jnp.concatenate([cot_blocks[m] for m in range(peers)], axis=0)
    gate_up = dot(normed_mid, w_gate_up)
    gate = gate_up[:, :ff_width]
    upper = gate_up[:, ff_width:]
    hidden = (jax.nn.silu(gate) * upper).astype(bf16)
    result_part = dot(hidden, w_down).astype(bf16).reshape(peers, length, D)
    result = middle + scatter_ctx(lambda m: result_part[m])
    block_output = result.astype(bf16).reshape(block_input.shape)
    grad_down = dot(hidden, cot, TN).astype(bf16)
    grad_hidden = dot(cot, w_down, NT)
    grad_gu = jnp.concatenate(
        [grad_hidden * upper * silu_slope(gate), grad_hidden * jax.nn.silu(gate)], axis=1
    ).astype(bf16)
    grad_gate_up = dot(normed_mid, grad_gu, TN).astype(bf16)
    back_part = dot(grad_gu, w_gate_up, NT).astype(bf16).reshape(peers, length, D)
    grad_normed_mid = scatter_ctx(lambda m: back_part[m])
    grad_gain_mid = jnp.sum(grad_normed_mid * unit_mid, axis=0)
    grad_middle = cotangent.reshape(length, D).astype(f32) + norm_back(
        grad_normed_mid * gain_mid, unit_mid, scale_mid
    )
    grad_mixed = place_ctx(gather_ctx(grad_middle.astype(bf16))).reshape(total_len, D)
    sum_down = scatter_dp(grad_down.reshape(groups, row_block, D))
    sum_gate_up = scatter_dp(grad_gate_up.reshape(groups, peers * in_rows, 2 * ff_width))

    grad_out = dot(joined, grad_mixed, TN)
    if strided:
        sum_out = scatter_dp(grad_out.astype(bf16).reshape(groups, row_block, D))
    else:
        spread = jnp.zeros((DSSM + QH * HD, D), f32)
        spread = lax.dynamic_update_slice_in_dim(spread, grad_out[:width], place * width, 0)
        spread = lax.dynamic_update_slice_in_dim(
            spread, grad_out[width:], DSSM + place * query_width, 0
        )
        sum_out = lax.psum_scatter(spread, ("dp", "ctx"), scatter_dimension=0, tiled=True)
    grad_joined = dot(grad_mixed, w_out, NT)
    grad_attended = grad_joined[:, width:].astype(bf16)
    grad_mix_part = grad_joined[:, :width]
    grad_unit = grad_mix_part * own_gain_mix
    inner = sum_ctx(jnp.sum(grad_unit * unit_mix, axis=-1))[:, None] / DSSM
    grad_queries, grad_keys, grad_values = attention_back_call(
        queries, keys, values, seg_col, seg_row, log_total, grad_attended
    )
    grad_gain_mix = jnp.sum(grad_mix_part * unit_mix, axis=0)
    grad_gated = scale_mix * (grad_unit - unit_mix * inner)
    grad_scan = grad_gated * gate_act
    grad_z = grad_gated * scanned * silu_slope(gate_z)
    grad_streams, grad_writes, grad_reads, reduced, totals = scan_back_call(
        own, shared, col, row, own_skip, scanned, states, grad_scan, width
    )
    totals = totals.reshape(chunks, 8, heads, HEAD_M).sum(axis=3)
    last = from_start[:, -1, :] * totals[:, 0, :] + totals[:, 1, :]
    flow = reduced[:, :heads].reshape(chunks, CHUNK, heads)
    grad_rate = jnp.einsum("ts,cth->csh", lower, flow, precision=lax.Precision.HIGHEST)
    grad_rate = (grad_rate + last[:, None, :]).reshape(total_len, heads)
    grad_step = reduced[:, 32 : 32 + heads] - own_decay * grad_rate
    grad_raw = grad_step * jax.nn.sigmoid(raw_step + own_bias)
    grad_bias = jnp.sum(grad_raw, axis=0)
    grad_decay = jnp.sum(grad_rate * rates.reshape(total_len, heads), axis=0)
    grad_skip = jnp.sum(totals[:, 2, :], axis=0)
    if query_heads < KVH:
        blank = jnp.zeros((total_len, KVH * HD), f32)
        grad_keys = lax.dynamic_update_slice_in_dim(blank, grad_keys, own_kv, 1)
        grad_values = lax.dynamic_update_slice_in_dim(blank, grad_values, own_kv, 1)
    grad_own = jnp.concatenate(
        [grad_z.astype(bf16), grad_streams.astype(bf16), grad_queries.astype(bf16)], axis=1
    )
    grad_shared = jnp.concatenate(
        [
            grad_writes.astype(bf16),
            grad_reads.astype(bf16),
            grad_keys.astype(bf16),
            grad_values.astype(bf16),
            pad_lanes(spread_cols(grad_raw.astype(bf16), head_block), 128),
        ],
        axis=1,
    )
    grad_in_own = dot(normed, grad_own, TN).astype(bf16)
    grad_in_shared = dot(normed, grad_shared, TN).astype(bf16)
    sum_own = scatter_dp(grad_in_own.reshape(groups, peers * in_rows, own_width))
    shared_part = grad_in_shared.reshape(groups, peers, in_rows, SHARED)
    sum_shared = scatter_ctx(
        lambda m: lax.dynamic_index_in_dim(shared_part, place ^ m, 1, False)
    ).astype(bf16)
    sum_shared = scatter_dp(sum_shared)
    normed_part = (dot(grad_own, w_own, NT) + dot(grad_shared, w_shared, NT)).astype(bf16)
    normed_part = normed_part.reshape(peers, length, D)
    grad_normed = scatter_ctx(lambda m: lax.dynamic_index_in_dim(normed_part, place ^ m, 0, False))
    x_float = x_own.astype(f32)
    own_scale = rms_scale(x_float)
    own_unit = x_float * own_scale
    grad_gain_in = jnp.sum(grad_normed * own_unit, axis=0)
    input_grad = grad_middle + norm_back(grad_normed * gain_in, own_unit, own_scale)
    input_grad = input_grad.reshape(block_input.shape)

    got = exchange_ctx(sum_own.astype(bf16).reshape(peers, in_rows, own_width)).astype(f32)
    sum_in = jnp.concatenate(
        [
            join_cols(got[:, :, :width], pair_block),
            join_cols(got[:, :, width : 2 * width], pair_block),
            sum_shared[:, : 2 * STATE],
            sum_shared[:, SHARED - 128 : SHARED - 128 + HEADS_M],
            join_cols(got[:, :, 2 * width :], query_block),
            sum_shared[:, 2 * STATE : SHARED - 128],
        ],
        axis=1,
    )
    got = exchange_ctx(sum_gate_up.astype(bf16).reshape(peers, in_rows, 2 * ff_width)).astype(f32)
    sum_gate_up = jnp.concatenate(
        [join_cols(got[:, :, :ff_width], row_block), join_cols(got[:, :, ff_width:], row_block)],
        axis=1,
    )
    small_grad = lax.psum(
        jnp.concatenate(
            [
                grad_gain_in,
                grad_gain_mid,
                spread_cols(grad_gain_mix[None, :], pair_block)[0],
                spread_cols(grad_bias[None, :], head_block)[0],
                spread_cols(grad_decay[None, :], head_block)[0],
                spread_cols(grad_skip[None, :], head_block)[0],
            ]
        ),
        ("dp", "ctx"),
    )
    new_in = adam_step(in_weight, sum_in, in_first, in_second, rate_scale / math.sqrt(D))
    new_out = adam_step(
        out_weight, sum_out, out_first, out_second, rate_scale / math.sqrt(DSSM + QH * HD)
    )
    new_gate_up = adam_step(
        gate_up_weight, sum_gate_up, gate_up_first, gate_up_second, rate_scale / math.sqrt(D)
    )
    new_down = adam_step(
        down_weight, sum_down, down_first, down_second, rate_scale / math.sqrt(FF)
    )
    new_small = adam_step(small_params, small_grad, small_first, small_second, small_rate)
    return (block_output, input_grad) + new_in + new_out + new_gate_up + new_down + new_small


def solution(mesh):
    rows = P(("dp", "ctx"), None)
    tokens = P("dp", "ctx", None)
    return jax.shard_map(
        shards,
        mesh=mesh,
        in_specs=(tokens, P("dp", "ctx"), tokens) + (rows,) * 12 + (P(),) * 3,
        out_specs=(tokens, tokens) + (rows,) * 12 + (P(),) * 3,
        check_vma=False,
    )
```

```python
import functools
import math

import jax
import jax.numpy as jnp
from jax import lax
from jax.experimental import pallas as pl
from jax.experimental.pallas import tpu as pltpu
from jax.sharding import PartitionSpec as P

D = 2048
FF = 4096
QH = 8
KVH = 2
HD = 128
HEADS_M = 48
HEAD_M = 64
STATE = 256
STEP = 10
DOC_MOST = 800
DSSM = HEADS_M * HEAD_M
SHARED = 2 * STATE + 2 * KVH * HD + 128
CHUNK = 256
QBLOCK = 256

norm_eps = 1e-05
beta_one = 0.9
beta_two = 0.95
adam_eps = 1e-08
weight_decay = 0.1
rate_scale = 3.0
small_rate = 0.3
bf16 = jnp.bfloat16
f32 = jnp.float32
NN = (((1,), (0,)), ((), ()))
NT = (((1,), (1,)), ((), ()))
TN = (((0,), (0,)), ((), ()))


def dot(a, b, dims=NN):
    return lax.dot_general(a, b, dims, preferred_element_type=f32)


def from_ctx(x, m):
    count = lax.axis_size("ctx")
    return lax.ppermute(x, "ctx", [(i ^ m, i) for i in range(count)])


def from_dp(x, j, k):
    count = lax.axis_size("dp")
    inner = count // 4
    pairs = []
    for i in range(count):
        z, w = divmod(i, inner)
        pairs.append((((z + j) % 4) * inner + (w + k) % inner, i))
    return lax.ppermute(x, "dp", pairs)


def fence(*trees):
    return lax.optimization_barrier(trees)


def outer_groups():
    count = lax.axis_size("dp")
    inner = count // 4
    return [[j * inner + k for j in range(4)] for k in range(inner)]


def gather_outer(own):
    return lax.all_gather(own, "dp", axis_index_groups=outer_groups())


def gather_outer_permuted(own):
    outer = lax.axis_index("dp") // (lax.axis_size("dp") // 4)
    full = jnp.stack([own] * 4)
    for j in (1, 3, 2):
        full = lax.dynamic_update_index_in_dim(
            full, from_dp(own, j, 0), lax.rem(outer + j, 4), 0
        )
    return full


def gather_inner(along):
    return {k: from_dp(along, 0, k) for k in range(1, lax.axis_size("dp") // 4)}


def place_dp(along, others):
    inner = lax.axis_size("dp") // 4
    place = lax.rem(lax.axis_index("dp"), inner)
    full = jnp.stack([along] * inner, axis=1)
    for k, block in others.items():
        full = lax.dynamic_update_index_in_dim(full, block, lax.rem(place + k, inner), 1)
    return full


def scatter_inner(full):
    inner = lax.axis_size("dp") // 4
    place = lax.rem(lax.axis_index("dp"), inner)
    full = full.reshape((4, inner) + full.shape[1:])

    def part(k):
        return lax.dynamic_index_in_dim(full, lax.rem(place + k, inner), 1, False)

    return part(0), {k: from_dp(part(k), 0, -k) for k in range(1, inner)}


def scatter_outer(own, got):
    total = own.astype(f32)
    for block in got.values():
        total = total + block.astype(f32)
    total = total.astype(bf16)
    total = lax.psum_scatter(
        total, "dp", scatter_dimension=0, axis_index_groups=outer_groups(), tiled=True
    )
    return total[0]


def across(own):
    return {m: from_ctx(own, m) for m in range(2, lax.axis_size("ctx"), 2)}


def beside(blocks):
    out = {}
    for m, block in blocks.items():
        out[m] = block
        out[m + 1] = from_ctx(block, 1)
    return out


def place_ctx(blocks, dim=0):
    shape = blocks[0].shape
    place = lax.axis_index("ctx")
    full = jnp.zeros(shape[:dim] + (lax.axis_size("ctx"),) + shape[dim:], blocks[0].dtype)
    for m, block in blocks.items():
        full = lax.dynamic_update_index_in_dim(full, block, place ^ m, dim)
    return full


def chip_sum(part, m):
    return part(m).astype(f32) + from_ctx(part(m + 1), 1).astype(f32)


def far_sums(part):
    return {m: chip_sum(part, m).astype(bf16) for m in range(2, lax.axis_size("ctx"), 2)}


def send_far(sums):
    return {m: from_ctx(block, m) for m, block in sums.items()}


def total_of(near, got):
    for block in got.values():
        near = near + block.astype(f32)
    return near


def scatter_ctx(part):
    got = send_far(far_sums(part))
    return total_of(chip_sum(part, 0), got)


def exchange_ctx(blocks):
    moved = [m for m in range(2, lax.axis_size("ctx"))] + [1]
    return {0: blocks[0], **{m: from_ctx(blocks[m], m) for m in moved}}


def by_distance(blocks):
    place = lax.axis_index("ctx")
    return [
        lax.dynamic_index_in_dim(blocks, place ^ m, 0, False) for m in range(lax.axis_size("ctx"))
    ]


def sum_ctx(x):
    m = 1
    while m < lax.axis_size("ctx"):
        x = x + from_ctx(x, m)
        m *= 2
    return x


def sum_dp(x):
    count = lax.axis_size("dp")
    m = 1
    while m < count:
        x = x + lax.ppermute(x, "dp", [(i ^ m, i) for i in range(count)])
        m *= 2
    return x


def split_cols(a, block):
    count = lax.axis_size("ctx")
    rows, n = a.shape
    a = a.reshape(rows, n // (count * block), count, block)
    return a.transpose(2, 0, 1, 3).reshape(count, rows, n // count)


def join_cols(a, block):
    count, rows, n = a.shape
    a = a.reshape(count, rows, n // block, block)
    return a.transpose(1, 2, 0, 3).reshape(rows, count * n)


def own_cols(a, block):
    count = lax.axis_size("ctx")
    rows, n = a.shape
    a = a.reshape(rows, n // (count * block), count, block)
    a = lax.dynamic_index_in_dim(a, lax.axis_index("ctx"), 2, False)
    return a.reshape(rows, n // count)


def spread_cols(a, block):
    count = lax.axis_size("ctx")
    rows, n = a.shape
    a = a.reshape(rows, n // block, block)
    full = jnp.zeros((rows, n // block, count, block), a.dtype)
    full = lax.dynamic_update_index_in_dim(full, a, lax.axis_index("ctx"), 2)
    return full.reshape(rows, count * n)


def attention_window(total_len):
    reach = -(-(DOC_MOST - 1) // QBLOCK) * QBLOCK
    return min(reach, total_len - QBLOCK), min(reach + QBLOCK, total_len)


def attention_scores(total_len, q_ref, k_ref, col_ref, row_ref):
    back, window = attention_window(total_len)
    first = pl.program_id(1) * QBLOCK
    start = pl.multiple_of(jnp.maximum(first - back, 0), QBLOCK)
    keys = k_ref[pl.ds(start, window), :]
    scores = dot(q_ref[...], keys, NT) * HD ** (-0.5)
    query_place = first + lax.broadcasted_iota(jnp.int32, (QBLOCK, window), 0)
    key_place = start + lax.broadcasted_iota(jnp.int32, (QBLOCK, window), 1)
    key_seg = row_ref[0:1, pl.ds(start, window)]
    allowed = (key_place <= query_place) & (col_ref[:, 0:1] == key_seg)
    return start, window, keys, jnp.where(allowed, scores, -1e30)


def attend_kernel(total_len, q_ref, k_ref, v_ref, col_ref, row_ref, out_ref, log_ref):
    start, window, _, scores = attention_scores(total_len, q_ref, k_ref, col_ref, row_ref)
    peak = jnp.max(scores, axis=1, keepdims=True)
    expo = jnp.exp(scores - peak)
    log_total = peak + jnp.log(jnp.sum(expo, axis=1, keepdims=True))
    shares = jnp.exp(scores - log_total).astype(bf16)
    out_ref[...] = dot(shares, v_ref[pl.ds(start, window), :]).astype(out_ref.dtype)
    log_ref[...] = jnp.broadcast_to(log_total, log_ref.shape)


def attend_back_kernel(
    total_len, q_ref, k_ref, v_ref, col_ref, row_ref, log_ref, grad_ref, dq_ref, dk_ref, dv_ref
):
    @pl.when(pl.program_id(1) == 0)
    def _():
        dk_ref[...] = jnp.zeros_like(dk_ref)
        dv_ref[...] = jnp.zeros_like(dv_ref)

    start, window, keys, scores = attention_scores(total_len, q_ref, k_ref, col_ref, row_ref)
    shares = jnp.exp(scores - log_ref[:, 0:1])
    grad = grad_ref[...]
    grad_shares = dot(grad, v_ref[pl.ds(start, window), :], NT)
    inner = jnp.sum(shares * grad_shares, axis=1, keepdims=True)
    grad_scores = (shares * (grad_shares - inner)).astype(bf16)
    scale = HD ** (-0.5)
    dq_ref[...] = dot(grad_scores, keys) * scale
    span = pl.ds(start, window)
    dk_ref[span, :] += dot(grad_scores, q_ref[...], TN) * scale
    dv_ref[span, :] += dot(shares.astype(bf16), grad, TN)


def attention_specs(total_len, offset):
    tile = pl.BlockSpec((QBLOCK, HD), lambda h, i: (i, h))
    whole = pl.BlockSpec((total_len, HD), lambda h, i: (0, h))
    later = pl.BlockSpec((total_len, HD), lambda h, i: (0, h + offset))
    col = pl.BlockSpec((QBLOCK, 128), lambda h, i: (i, 0))
    row = pl.BlockSpec((8, total_len), lambda h, i: (0, 0))
    return tile, whole, later, col, row


def attention_call(queries, pairs, offset, seg_col, seg_row):
    total_len, width = queries.shape
    tile, whole, later, col, row = attention_specs(total_len, offset)
    return pl.pallas_call(
        functools.partial(attend_kernel, total_len),
        grid=(width // HD, total_len // QBLOCK),
        in_specs=[tile, whole, later, col, row],
        out_specs=[tile, tile],
        out_shape=[
            jax.ShapeDtypeStruct((total_len, width), bf16),
            jax.ShapeDtypeStruct((total_len, width), f32),
        ],
        compiler_params=pltpu.CompilerParams(vmem_limit_bytes=48 * 2**20),
        cost_estimate=pl.CostEstimate(
            flops=4 * total_len * 1280 * width, bytes_accessed=12 * total_len * width, transcendentals=0
        ),
        name="attend",
    )(queries, pairs, pairs, seg_col, seg_row)


def attention_back_call(queries, pairs, offset, seg_col, seg_row, log_total, grad):
    total_len, width = queries.shape
    tile, whole, later, col, row = attention_specs(total_len, offset)
    return pl.pallas_call(
        functools.partial(attend_back_kernel, total_len),
        grid=(width // HD, total_len // QBLOCK),
        in_specs=[tile, whole, later, col, row, tile, tile],
        out_specs=[tile, whole, whole],
        out_shape=[jax.ShapeDtypeStruct((total_len, width), f32)] * 3,
        compiler_params=pltpu.CompilerParams(vmem_limit_bytes=48 * 2**20),
        cost_estimate=pl.CostEstimate(
            flops=10 * total_len * 1280 * width, bytes_accessed=24 * total_len * width, transcendentals=0
        ),
        name="attend_back",
    )(queries, pairs, pairs, seg_col, seg_row, log_total, grad)


def pair_of(col, offset, j, left):
    a = offset + 2 * j
    return jnp.where(left, col[:, a : a + 1], col[:, a + 1 : a + 2])


def state_decay(col, j, left_rows):
    last = col[CHUNK - 1 : CHUNK, :]
    a = 64 + 2 * j
    return jnp.where(left_rows, last[:, a : a + 1], last[:, a + 1 : a + 2])


def scan_kernel(pairs, x_ref, k_ref, r_ref, col_ref, row_ref, skip_ref, y_ref, s_ref, state):
    @pl.when(pl.program_id(0) == 0)
    def _():
        state[...] = jnp.zeros_like(state)

    writes = k_ref[...].astype(bf16)
    reads = r_ref[...].astype(bf16)
    col = col_ref[...]
    row = row_ref[...]
    entering = state[...].astype(bf16)
    s_ref[0] = entering
    products = dot(reads, writes, NT)
    later = lax.broadcasted_iota(jnp.int32, (CHUNK, CHUNK), 0)
    earlier = lax.broadcasted_iota(jnp.int32, (CHUNK, CHUNK), 1)
    mask = (later >= earlier) & (col[:, 127:128] == row[16:17, :])
    left = lax.broadcasted_iota(jnp.int32, (CHUNK, 128), 1) < HEAD_M
    left_rows = lax.broadcasted_iota(jnp.int32, (128, STATE), 0) < HEAD_M
    through = dot(reads, entering, NT)
    for j in range(pairs):
        lanes = slice(128 * j, 128 * j + 128)
        x = x_ref[:, lanes]
        scaled = x * pair_of(col, 32, j, left)
        scaled_low = scaled.astype(bf16)
        outs = []
        for h in (2 * j, 2 * j + 1):
            spread = col[:, h : h + 1] - row[h : h + 1, :]
            mixing = jnp.exp(jnp.where(mask, spread, -1e30)) * products
            outs.append(dot(mixing.astype(bf16), scaled_low))
        y_ref[:, lanes] = (
            jnp.where(left, outs[0], outs[1])
            + pair_of(col, 64, j, left) * through[:, lanes]
            + skip_ref[0:1, lanes] * x
        )
        to_end = (scaled * pair_of(col, 96, j, left)).astype(bf16)
        state[lanes, :] = state_decay(col, j, left_rows) * state[lanes, :] + dot(to_end, writes, TN)


def scan_back_kernel(
    pairs,
    x_ref,
    k_ref,
    r_ref,
    col_ref,
    row_ref,
    skip_ref,
    y_ref,
    s_ref,
    dy_ref,
    sum_ref,
    dx_ref,
    dk_ref,
    dr_ref,
    red_ref,
    tot_ref,
    adjoint,
    keep,
):
    @pl.when(pl.program_id(0) == 0)
    def _():
        adjoint[...] = jnp.zeros_like(adjoint)

    writes = k_ref[...].astype(bf16)
    reads = r_ref[...].astype(bf16)
    col = col_ref[...]
    row = row_ref[...]
    entering = s_ref[0]
    products = dot(writes, reads, NT)
    earlier = lax.broadcasted_iota(jnp.int32, (CHUNK, CHUNK), 0)
    later = lax.broadcasted_iota(jnp.int32, (CHUNK, CHUNK), 1)
    mask = (later >= earlier) & (col[:, 127:128] == row[16:17, :])
    left = lax.broadcasted_iota(jnp.int32, (CHUNK, 128), 1) < HEAD_M
    left_rows = lax.broadcasted_iota(jnp.int32, (128, STATE), 0) < HEAD_M
    incoming = adjoint[...]
    incoming_low = incoming.astype(bf16)
    values = dot(writes, incoming_low, NT)
    grad_products = jnp.zeros((CHUNK, CHUNK), f32)
    grad_writes = jnp.zeros((CHUNK, STATE), f32)
    grad_reads = jnp.zeros((CHUNK, STATE), f32)
    tot_ref[0] = jnp.zeros(tot_ref.shape[1:], f32)
    for j in range(pairs):
        lanes = slice(128 * j, 128 * j + 128)
        x = x_ref[:, lanes]
        step = pair_of(col, 32, j, left)
        scaled = x * step
        scaled_low = scaled.astype(bf16)
        dy = dy_ref[:, lanes]
        dy_low = dy.astype(bf16)
        grads = []
        for side, h in enumerate((2 * j, 2 * j + 1)):
            spread = row[h : h + 1, :] - col[:, h : h + 1]
            decay = jnp.exp(jnp.where(mask, spread, -1e30))
            half = left if side == 0 else jnp.logical_not(left)
            grad_mixing = dot(jnp.where(half, scaled_low, jnp.zeros_like(scaled_low)), dy_low, NT)
            grad_products += grad_mixing * decay
            grads.append(dot((decay * products).astype(bf16), dy_low))
        grad_scaled = jnp.where(left, grads[0], grads[1])
        decay_end = pair_of(col, 96, j, left)
        to_end = (scaled * decay_end).astype(bf16)
        passed = to_end.astype(f32) * values[:, lanes]
        skip = skip_ref[0:1, lanes]
        flow = (
            dy_low.astype(f32) * (y_ref[:, lanes] - skip * x)
            - scaled_low.astype(f32) * grad_scaled
            - passed
        )
        grad_scaled += decay_end * values[:, lanes]
        dx_ref[:, lanes] = step * grad_scaled + skip * dy
        from_start = (pair_of(col, 64, j, left) * dy).astype(bf16)
        grad_reads += dot(from_start, entering[lanes, :])
        grad_writes += dot(to_end, incoming_low[lanes, :])
        pieces = (flow, x * grad_scaled)
        for n, piece in enumerate(pieces):
            high = piece.astype(bf16)
            keep[2 * n, :, lanes] = high
            keep[2 * n + 1, :, lanes] = (piece - high.astype(f32)).astype(bf16)
        tot_ref[0, 1:2, lanes] = jnp.sum(passed, axis=0, keepdims=True)
        tot_ref[0, 2:3, lanes] = jnp.sum(dy * x, axis=0, keepdims=True)
        product = incoming[lanes, :] * entering[lanes, :].astype(f32)
        high = product.astype(bf16)
        low = (product - high.astype(f32)).astype(bf16)
        ones = jnp.ones((8, STATE), bf16)
        tot_ref[0, 0:1, lanes] = (dot(ones, high, NT) + dot(ones, low, NT))[0:1, :]
        adjoint[lanes, :] = state_decay(col, j, left_rows) * incoming[lanes, :] + dot(
            from_start, reads, TN
        )
    grad_products = grad_products.astype(bf16)
    dk_ref[...] = grad_writes + dot(grad_products, reads)
    dr_ref[...] = grad_reads + dot(grad_products, writes, TN)
    sums = sum_ref[...]
    red_ref[...] = (
        dot(keep[0], sums[0]) + dot(keep[1], sums[0]) + dot(keep[2], sums[1]) + dot(keep[3], sums[1])
    )


def scan_call(own, shared, col, row, skip, width):
    total_len = own.shape[0]
    count = total_len // CHUNK
    return pl.pallas_call(
        functools.partial(scan_kernel, width // 128),
        grid=(count,),
        in_specs=[
            pl.BlockSpec((CHUNK, width), lambda i: (i, 0)),
            pl.BlockSpec((CHUNK, STATE), lambda i: (i, 0)),
            pl.BlockSpec((CHUNK, STATE), lambda i: (i, 1)),
            pl.BlockSpec((CHUNK, 128), lambda i: (i, 0)),
            pl.BlockSpec((24, CHUNK), lambda i: (0, i)),
            pl.BlockSpec((8, width), lambda i: (0, 0)),
        ],
        out_specs=[
            pl.BlockSpec((CHUNK, width), lambda i: (i, 0)),
            pl.BlockSpec((1, width, STATE), lambda i: (i, 0, 0)),
        ],
        out_shape=[
            jax.ShapeDtypeStruct((total_len, width), f32),
            jax.ShapeDtypeStruct((count, width, STATE), bf16),
        ],
        scratch_shapes=[pltpu.VMEM((width, STATE), f32)],
        compiler_params=pltpu.CompilerParams(vmem_limit_bytes=48 * 2**20),
        cost_estimate=pl.CostEstimate(
            flops=8 * total_len * width * STATE, bytes_accessed=12 * total_len * width, transcendentals=0
        ),
        name="state_scan",
    )(own, shared, shared, col, row, skip)


def scan_back_call(own, shared, col, row, skip, scanned, states, grad, width):
    total_len = own.shape[0]
    count = total_len // CHUNK
    owner = jnp.arange(width)[:, None] // HEAD_M
    lane = jnp.arange(128)[None, :]
    sums = jnp.stack([owner == lane, owner + 32 == lane]).astype(bf16)

    def back(i):
        return count - 1 - i

    return pl.pallas_call(
        functools.partial(scan_back_kernel, width // 128),
        grid=(count,),
        in_specs=[
            pl.BlockSpec((CHUNK, width), lambda i: (back(i), 0)),
            pl.BlockSpec((CHUNK, STATE), lambda i: (back(i), 0)),
            pl.BlockSpec((CHUNK, STATE), lambda i: (back(i), 1)),
            pl.BlockSpec((CHUNK, 128), lambda i: (back(i), 0)),
            pl.BlockSpec((24, CHUNK), lambda i: (0, back(i))),
            pl.BlockSpec((8, width), lambda i: (0, 0)),
            pl.BlockSpec((CHUNK, width), lambda i: (back(i), 0)),
            pl.BlockSpec((1, width, STATE), lambda i: (back(i), 0, 0)),
            pl.BlockSpec((CHUNK, width), lambda i: (back(i), 0)),
            pl.BlockSpec((2, width, 128), lambda i: (0, 0, 0)),
        ],
        out_specs=[
            pl.BlockSpec((CHUNK, width), lambda i: (back(i), 0)),
            pl.BlockSpec((CHUNK, STATE), lambda i: (back(i), 0)),
            pl.BlockSpec((CHUNK, STATE), lambda i: (back(i), 0)),
            pl.BlockSpec((CHUNK, 128), lambda i: (back(i), 0)),
            pl.BlockSpec((1, 8, width), lambda i: (back(i), 0, 0)),
        ],
        out_shape=[
            jax.ShapeDtypeStruct((total_len, width), f32),
            jax.ShapeDtypeStruct((total_len, STATE), f32),
            jax.ShapeDtypeStruct((total_len, STATE), f32),
            jax.ShapeDtypeStruct((total_len, 128), f32),
            jax.ShapeDtypeStruct((count, 8, width), f32),
        ],
        scratch_shapes=[pltpu.VMEM((width, STATE), f32), pltpu.VMEM((4, CHUNK, width), bf16)],
        compiler_params=pltpu.CompilerParams(vmem_limit_bytes=48 * 2**20),
        cost_estimate=pl.CostEstimate(
            flops=20 * total_len * width * STATE, bytes_accessed=24 * total_len * width, transcendentals=0
        ),
        name="state_scan_back",
    )(own, shared, shared, col, row, skip, scanned, states, grad, sums)


def pack_in_kernel(count, place_ref, w_ref, own_ref, shared_ref):
    place = place_ref[0]
    width = DSSM // count
    first_z = width + QH * HD // count
    query = 2 * DSSM + 2 * STATE + HEADS_M
    for c in range(count):
        m = c ^ place
        for n in range(DSSM // (count * HD)):
            at = (n * count + c) * HD
            to = slice(n * HD, (n + 1) * HD)
            own_ref[m, :, to] = w_ref[:, DSSM + at : DSSM + at + HD].astype(bf16)
            to = slice(first_z + n * HD, first_z + (n + 1) * HD)
            own_ref[m, :, to] = w_ref[:, at : at + HD].astype(bf16)
        for n in range(QH // count):
            at = query + (n * count + c) * HD
            to = slice(width + n * HD, width + (n + 1) * HD)
            own_ref[m, :, to] = w_ref[:, at : at + HD].astype(bf16)
    shared_ref[:, : 2 * STATE] = w_ref[:, 2 * DSSM : 2 * DSSM + 2 * STATE].astype(bf16)
    shared_ref[:, 2 * STATE : SHARED - 128] = w_ref[:, query + QH * HD :].astype(bf16)
    steps = w_ref[:, query - HEADS_M : query - HEADS_M + 128]
    lane = lax.broadcasted_iota(jnp.int32, steps.shape, 1)
    shared_ref[:, SHARED - 128 :] = jnp.where(lane < HEADS_M, steps, 0.0).astype(bf16)


def pack_in(place, weight):
    rows = weight.shape[0]
    count = lax.axis_size("ctx")
    own_width = (2 * DSSM + QH * HD) // count
    return pl.pallas_call(
        functools.partial(pack_in_kernel, count),
        in_specs=[pl.BlockSpec(memory_space=pltpu.SMEM), pl.BlockSpec(memory_space=pltpu.VMEM)],
        out_specs=[pl.BlockSpec(memory_space=pltpu.VMEM)] * 2,
        out_shape=[
            jax.ShapeDtypeStruct((count, rows, own_width), bf16),
            jax.ShapeDtypeStruct((rows, SHARED), bf16),
        ],
        compiler_params=pltpu.CompilerParams(vmem_limit_bytes=48 * 2**20),
        name="pack_in",
    )(place, weight)


def pack_gate_up_kernel(count, place_ref, w_ref, out_ref):
    place = place_ref[0]
    blocks = FF // (count * HD)
    for c in range(count):
        m = c ^ place
        for n in range(2 * blocks):
            at = (n * count + c) * HD
            out_ref[m, :, n * HD : (n + 1) * HD] = w_ref[:, at : at + HD].astype(bf16)


def pack_gate_up(place, weight):
    rows = weight.shape[0]
    count = lax.axis_size("ctx")
    return pl.pallas_call(
        functools.partial(pack_gate_up_kernel, count),
        in_specs=[pl.BlockSpec(memory_space=pltpu.SMEM), pl.BlockSpec(memory_space=pltpu.VMEM)],
        out_specs=pl.BlockSpec(memory_space=pltpu.VMEM),
        out_shape=jax.ShapeDtypeStruct((count, rows, 2 * FF // count), bf16),
        compiler_params=pltpu.CompilerParams(vmem_limit_bytes=48 * 2**20),
        name="pack_gate_up",
    )(place, weight)


def update_kernel(count, spans, rate, place_ref, g_ref, *refs):
    tail_ref = refs[0] if len(refs) == 7 else None
    w_ref, first_ref, second_ref, new_w_ref, new_first_ref, new_second_ref = refs[-6:]
    place = place_ref[0]

    def update(cols, grad):
        new = adam_step(w_ref[:, cols], grad, first_ref[:, cols], second_ref[:, cols], rate)
        new_w_ref[:, cols], new_first_ref[:, cols], new_second_ref[:, cols] = new

    for first, columns, at in spans:
        for n in range(columns // (count * HD)):
            for c in range(count):
                start = first + (n * count + c) * HD
                grad = g_ref[c ^ place, :, at : at + HD].astype(f32)
                update(slice(start, start + HD), grad)
            at += HD
    if tail_ref is not None:
        update(slice(2 * DSSM, w_ref.shape[1]), tail_ref[...])


def update_dealt(place, got, tail, weight, first, second, spans, rate):
    rows, columns = weight.shape
    count = lax.axis_size("ctx")
    got = jnp.stack([got[m] for m in range(count)])
    block = 16

    def flat(n):
        return pl.BlockSpec((block, n), lambda i: (i, 0))

    tails = [] if tail is None else [tail]
    return pl.pallas_call(
        functools.partial(update_kernel, count, spans, rate),
        grid=(rows // block,),
        in_specs=[
            pl.BlockSpec(memory_space=pltpu.SMEM),
            pl.BlockSpec((count, block, got.shape[2]), lambda i: (0, i, 0)),
        ]
        + [flat(t.shape[1]) for t in tails]
        + [flat(columns)] * 3,
        out_specs=[flat(columns)] * 3,
        out_shape=[jax.ShapeDtypeStruct((rows, columns), f32)] * 3,
        compiler_params=pltpu.CompilerParams(vmem_limit_bytes=48 * 2**20),
        name="update",
    )(place, got, *tails, weight, first, second)


def rms_scale(values):
    return lax.rsqrt(jnp.mean(values * values, axis=-1, keepdims=True) + norm_eps)


def norm_back(grad_unit, unit, scale):
    return scale * (grad_unit - unit * jnp.mean(grad_unit * unit, axis=-1, keepdims=True))


def silu_slope(values):
    sigma = jax.nn.sigmoid(values)
    return sigma * (1.0 + values * (1.0 - sigma))


def split_small(small):
    widths = [D, D, DSSM, HEADS_M, HEADS_M, HEADS_M]
    pieces = []
    start = 0
    for count in widths:
        pieces.append(small[start : start + count])
        start += count
    return pieces


def adam_step(weight, grad, first, second, rate):
    first = beta_one * first + (1.0 - beta_one) * grad
    second = beta_two * second + (1.0 - beta_two) * grad * grad
    fixed_first = first / (1.0 - beta_one**STEP)
    fixed_second = second / (1.0 - beta_two**STEP)
    weight = weight - rate * (
        fixed_first / (jnp.sqrt(fixed_second) + adam_eps) + weight_decay * weight
    )
    return (weight, first, second)


def pad_lanes(a, width):
    return jnp.pad(a, ((0, 0), (0, width - a.shape[1])))


def shards(
    block_input,
    segment_ids,
    cotangent,
    in_weight,
    out_weight,
    gate_up_weight,
    down_weight,
    in_first,
    out_first,
    gate_up_first,
    down_first,
    in_second,
    out_second,
    gate_up_second,
    down_second,
    small_params,
    small_first,
    small_second,
):
    peers = lax.axis_size("ctx")
    groups = lax.axis_size("dp")
    place = lax.axis_index("ctx")
    length = block_input.shape[0] * block_input.shape[1]
    total_len = length * peers
    row_block = out_weight.shape[0]
    in_rows = in_weight.shape[0]
    strided = row_block == HD
    width = DSSM // peers
    heads = HEADS_M // peers
    query_heads = QH // peers
    query_width = query_heads * HD
    own_width = 2 * width + query_width
    ff_width = FF // peers
    pair_block = 2 * HEAD_M if strided else width
    query_block = HD if strided else query_width
    head_block = 2 if strided else heads
    gain_in, gain_mid, gain_mix, step_bias, decay_log, skip = split_small(small_params)

    place_arg = place.astype(jnp.int32).reshape(1)
    base = 2 * DSSM + 2 * STATE + HEADS_M
    query_end = base + QH * HD
    if strided:
        own_low, shared_low = pack_in(place_arg, in_weight)
        gu_low = pack_gate_up(place_arg, gate_up_weight)
        own_low = [own_low[m] for m in range(peers)]
        gu_low = [gu_low[m] for m in range(peers)]
    else:
        in_low = in_weight.astype(bf16)
        shared_low = jnp.concatenate(
            [
                in_low[:, 2 * DSSM : 2 * DSSM + 2 * STATE],
                in_low[:, query_end:],
                in_low[:, 2 * DSSM + 2 * STATE : base],
                jnp.zeros((in_rows, 128 - HEADS_M), bf16),
            ],
            axis=1,
        )
        own_low = jnp.concatenate(
            [
                split_cols(in_low[:, DSSM : 2 * DSSM], pair_block),
                split_cols(in_low[:, base:query_end], query_block),
                split_cols(in_low[:, :DSSM], pair_block),
            ],
            axis=2,
        )
        own_low = by_distance(own_low)
        gu_low = gate_up_weight.astype(bf16)
        gu_low = jnp.concatenate(
            [split_cols(gu_low[:, :FF], row_block), split_cols(gu_low[:, FF:], row_block)], axis=2
        )
        gu_low = by_distance(gu_low)
    own_rows = place_ctx(exchange_ctx(own_low)).reshape(peers * in_rows, own_width)
    x_own = block_input.reshape(length, D)
    shared_along = gather_outer_permuted(shared_low)
    out_low = out_weight.astype(bf16)
    own_rows, x_own, shared_along, gu_low = fence(own_rows, x_own, shared_along, gu_low)

    sq_width = width + query_width
    sq_along = gather_outer(own_rows[:, :sq_width])
    z_along = gather_outer(own_rows[:, sq_width:])
    x_far = across(x_own)
    seg_own = segment_ids.reshape(length)
    segments = place_ctx(beside({0: seg_own, **across(seg_own)})).reshape(total_len)
    shared_rows = place_dp(shared_along, gather_inner(shared_along))
    shared_rows = shared_rows.reshape((groups,) + shared_low.shape)
    cot_own = cotangent.reshape(length, D)
    x_own, x_far, shared_rows, gu_low, cot_own, segments, sq_along, out_low = fence(
        x_own, x_far, shared_rows, gu_low, cot_own, segments, sq_along, out_low
    )

    shared_far = across(shared_rows)
    if strided:
        out_along = gather_outer(out_low)
    sq_others = gather_inner(sq_along)
    tokens = place_ctx(beside({0: x_own, **x_far})).reshape(total_len, D)
    scale_in = rms_scale(tokens.astype(f32))
    normed = (tokens.astype(f32) * scale_in * gain_in).astype(bf16)
    normed, shared_rows, shared_far, cot_own, gu_low = fence(
        normed, shared_rows, shared_far, cot_own, gu_low
    )

    gu_rows = place_ctx(exchange_ctx(gu_low)).reshape(peers * in_rows, 2 * ff_width)
    gate_along = gather_outer(gu_rows[:, :ff_width])
    up_along = gather_outer(gu_rows[:, ff_width:])
    w_shared = place_ctx(beside({0: shared_rows, **shared_far}), 1).reshape(D, SHARED)
    pairs = dot(normed, w_shared[:, 2 * STATE : SHARED - 128]).astype(bf16)
    writes_reads = dot(normed, w_shared[:, : 2 * STATE])
    raw_all = dot(normed, w_shared[:, SHARED - 128 :])
    if not strided:
        out_along = {}
    normed, pairs, writes_reads, raw_all, sq_others, z_along, out_along, cot_own = fence(
        normed, pairs, writes_reads, raw_all, sq_others, z_along, out_along, cot_own
    )

    z_others = gather_inner(z_along)
    out_others = gather_inner(out_along) if strided else {}
    down_low = down_weight.astype(bf16)
    cot_far = across(cot_own)
    w_sq = place_dp(sq_along, sq_others).reshape(D, sq_width)
    streams = dot(normed, w_sq[:, :width])
    queries = dot(normed, w_sq[:, width:]).astype(bf16)
    raw_step = own_cols(raw_all[:, :HEADS_M], head_block)
    offset = KVH
    if query_heads < KVH:
        offset = query_heads
        own_kv = (place * query_heads * KVH // QH) * HD
        pairs = jnp.concatenate(
            [
                lax.dynamic_slice_in_dim(pairs, own_kv, query_width, 1),
                lax.dynamic_slice_in_dim(pairs, KVH * HD + own_kv, query_width, 1),
            ],
            axis=1,
        )
    own_bias = own_cols(step_bias[None, :], head_block)
    own_decay = jnp.exp(own_cols(decay_log[None, :], head_block))
    own_skip = jnp.repeat(own_cols(skip[None, :], head_block), HEAD_M, axis=1)
    own_skip = jnp.broadcast_to(own_skip, (8, width))
    own_gain_mix = own_cols(gain_mix[None, :], pair_block)

    chunks = total_len // CHUNK
    step = jax.nn.softplus(raw_step + own_bias)
    rates = (-own_decay * step).reshape(chunks, CHUNK, heads)
    order = jnp.arange(CHUNK)
    lower = (order[:, None] >= order[None, :]).astype(f32)
    running = jnp.einsum("ts,csh->cth", lower, rates, precision=lax.Precision.HIGHEST)
    seg_chunks = segments.reshape(chunks, CHUNK)
    seg_last = seg_chunks[:, -1:]
    seg_before = jnp.concatenate([jnp.full((1, 1), -1, seg_last.dtype), seg_last[:-1]], axis=0)
    from_start = jnp.exp(running) * (seg_chunks == seg_before).astype(f32)[:, :, None]
    to_end = jnp.exp(
        jnp.where((seg_chunks == seg_last)[:, :, None], running[:, -1:, :] - running, -1e30)
    )
    seg_float = segments.astype(f32)
    running = running.reshape(total_len, heads)
    col = jnp.concatenate(
        [
            pad_lanes(running, 32),
            pad_lanes(step, 32),
            pad_lanes(from_start.reshape(total_len, heads), 32),
            pad_lanes(to_end.reshape(total_len, heads), 31),
            seg_float[:, None],
        ],
        axis=1,
    )
    row = jnp.concatenate(
        [
            jnp.pad(running.T, ((0, 16 - heads), (0, 0))),
            jnp.broadcast_to(seg_float[None, :], (8, total_len)),
        ],
        axis=0,
    )
    seg_col = jnp.broadcast_to(seg_float[:, None], (total_len, 128))
    seg_row = jnp.broadcast_to(seg_float[None, :], (8, total_len))

    scanned, states = scan_call(streams, writes_reads, col, row, own_skip, width)
    normed, scanned, queries, z_along, z_others, cot_own, cot_far, down_low = fence(
        normed, scanned, queries, z_along, z_others, cot_own, cot_far, down_low
    )

    gate_others = gather_inner(gate_along)
    w_down = lax.all_gather(down_low, "dp", axis=0, tiled=True)
    cot = jnp.concatenate(
        [block for _, block in sorted(beside({0: cot_own, **cot_far}).items())], axis=0
    )
    w_z = place_dp(z_along, z_others).reshape(D, width)
    gate_z = dot(normed, w_z)
    attended, log_total = attention_call(queries, pairs, offset, seg_col, seg_row)
    gate_act = jax.nn.silu(gate_z)
    gated = scanned * gate_act
    square = sum_ctx(jnp.sum(gated * gated, axis=-1))
    scale_mix = lax.rsqrt(square / DSSM + norm_eps)[:, None]
    unit_mix = gated * scale_mix
    joined = jnp.concatenate([(unit_mix * own_gain_mix).astype(bf16), attended], axis=1)
    joined, out_along, out_others, gate_along, gate_others, up_along = fence(
        joined, out_along, out_others, gate_along, gate_others, up_along
    )
    if strided:
        w_out = place_dp(out_along, out_others).reshape(sq_width, D)
    else:
        whole_out = lax.all_gather(out_low, ("dp", "ctx"), axis=0, tiled=True)
        w_out = jnp.concatenate(
            [
                lax.dynamic_slice_in_dim(whole_out, place * width, width, 0),
                lax.dynamic_slice_in_dim(whole_out, DSSM + place * query_width, query_width, 0),
            ],
            axis=0,
        )

    up_others = gather_inner(up_along)
    chips = list(range(peers // 2))
    parity = place % 2

    def chip_rows(full, e):
        start = ((place // 2) ^ e) * 2 * length
        return lax.dynamic_slice_in_dim(full, start, 2 * length, 0)

    def core_part(parts):
        return lambda m: lax.dynamic_index_in_dim(parts[m // 2], (m % 2) ^ parity, 0, False)

    def mixed_rows(e):
        return dot(chip_rows(joined, e), w_out).astype(bf16).reshape(2, length, D)

    sums = far_sums(core_part({e: mixed_rows(e) for e in chips[1:]}))
    sums, joined = fence(sums, joined)
    got = send_far(sums)
    near = chip_sum(core_part({0: mixed_rows(0)}), 0)
    got, near, up_others = fence(got, near, up_others)

    middle = x_own.astype(f32) + total_of(near, got)
    scale_mid = rms_scale(middle)
    unit_mid = middle * scale_mid
    mid_own = (unit_mid * gain_mid).astype(bf16)
    w_gate = place_dp(gate_along, gate_others).reshape(D, ff_width)
    w_up = place_dp(up_along, up_others).reshape(D, ff_width)
    rows = 2 * length

    def feed_forward(e, blocks, kept):
        normed_mid, hidden, grad_gate, grad_up = kept
        for m in (2 * e, 2 * e + 1):
            normed_mid = lax.dynamic_update_slice_in_dim(normed_mid, blocks[m], m * length, 0)
        at = slice(e * rows, (e + 1) * rows)
        gate = dot(normed_mid[at], w_gate)
        upper = dot(normed_mid[at], w_up)
        grad_hidden = dot(cot[at], w_down, NT)
        gate_half = jax.nn.silu(gate)
        part = (gate_half * upper).astype(bf16)
        hidden = lax.dynamic_update_slice_in_dim(hidden, part, e * rows, 0)
        part_gate = (grad_hidden * upper * silu_slope(gate)).astype(bf16)
        grad_gate = lax.dynamic_update_slice_in_dim(grad_gate, part_gate, e * rows, 0)
        part_up = (grad_hidden * gate_half).astype(bf16)
        grad_up = lax.dynamic_update_slice_in_dim(grad_up, part_up, e * rows, 0)
        back = (dot(part_gate, w_gate, NT) + dot(part_up, w_up, NT)).astype(bf16)
        return back.reshape(2, length, D), (normed_mid, hidden, grad_gate, grad_up)

    kept = tuple(jnp.zeros((total_len, n), bf16) for n in (D, ff_width, ff_width, ff_width))
    far = across(mid_own)
    near_back, kept = feed_forward(0, beside({0: mid_own}), kept)
    far, near_back, kept = fence(far, near_back, kept)
    far = beside(far)
    far_back = {}
    for e in chips[1:]:
        far_back[e], kept = feed_forward(e, far, kept)
    sums = far_sums(lambda m: far_back[m // 2][m % 2])
    sums, near_back, kept = fence(sums, near_back, kept)
    normed_mid, hidden, grad_gate, grad_up = kept
    got = send_far(sums)
    near = chip_sum(lambda m: near_back[m], 0)
    grad_gate = dot(normed_mid, grad_gate, TN).astype(bf16)
    grad_down = dot(hidden, cot, TN).astype(bf16)
    got, near, grad_gate, grad_down, normed_mid, grad_up = fence(
        got, near, grad_gate, grad_down, normed_mid, grad_up
    )

    gate_parts = scatter_inner(grad_gate.reshape(groups, -1, ff_width))
    sum_down = lax.psum_scatter(grad_down, "dp", scatter_dimension=0, tiled=True)
    grad_normed_mid = total_of(near, got)
    grad_middle = cot_own.astype(f32) + norm_back(grad_normed_mid * gain_mid, unit_mid, scale_mid)
    grad_middle_low = grad_middle.astype(bf16)
    grad_middle_low, hidden, normed_mid, grad_up = fence(
        grad_middle_low, hidden, normed_mid, grad_up
    )

    far = across(grad_middle_low)
    beside_own = beside({0: grad_middle_low})
    result_part = dot(hidden, w_down).astype(bf16).reshape(peers, length, D)
    grad_up = dot(normed_mid, grad_up, TN).astype(bf16)
    far, beside_own, result_part, gate_parts, grad_up = fence(
        far, beside_own, result_part, gate_parts, grad_up
    )

    grad_mixed = place_ctx({**beside_own, **beside(far)}).reshape(total_len, D)
    sum_gate = scatter_outer(*gate_parts)
    up_parts = scatter_inner(grad_up.reshape(groups, -1, ff_width))
    grad_gain_mid = jnp.sum(grad_normed_mid * unit_mid, axis=0)
    sums = far_sums(lambda m: result_part[m])
    result_near = chip_sum(lambda m: result_part[m], 0)
    grad_joined = dot(grad_mixed, w_out, NT)
    grad_out = dot(joined, grad_mixed, TN)
    if strided:
        out_parts = scatter_inner(grad_out.astype(bf16).reshape(groups, row_block, D))
    else:
        out_parts = ()
        spread = jnp.zeros((DSSM + QH * HD, D), f32)
        spread = lax.dynamic_update_slice_in_dim(spread, grad_out[:width], place * width, 0)
        spread = lax.dynamic_update_slice_in_dim(
            spread, grad_out[width:], DSSM + place * query_width, 0
        )
        sum_out = lax.psum_scatter(spread, ("dp", "ctx"), scatter_dimension=0, tiled=True)
    grad_attended = grad_joined[:, width:].astype(bf16)
    grad_mix_part = grad_joined[:, :width]
    grad_unit = grad_mix_part * own_gain_mix
    inner = sum_ctx(jnp.sum(grad_unit * unit_mix, axis=-1))[:, None] / DSSM
    grad_queries, grad_keys, grad_values = attention_back_call(
        queries, pairs, offset, seg_col, seg_row, log_total, grad_attended
    )
    grad_queries, inner, up_parts, out_parts, sums = fence(
        grad_queries, inner, up_parts, out_parts, sums
    )

    result_got = send_far(sums)
    sum_up = scatter_outer(*up_parts)
    if strided:
        sum_out = scatter_outer(*out_parts).astype(f32)
    grad_gain_mix = jnp.sum(grad_mix_part * unit_mix, axis=0)
    grad_gated = scale_mix * (grad_unit - unit_mix * inner)
    grad_scan = grad_gated * gate_act
    grad_z = grad_gated * scanned * silu_slope(gate_z)
    grad_qz = jnp.concatenate([grad_queries.astype(bf16), grad_z.astype(bf16)], axis=1)
    grad_in_qz = dot(normed, grad_qz, TN).astype(bf16)
    grad_in_qz, grad_scan = fence(grad_in_qz, grad_scan)

    qz_parts = scatter_inner(grad_in_qz.reshape(groups, -1, sq_width))
    grad_streams, grad_writes, grad_reads, reduced, totals = scan_back_call(
        streams, writes_reads, col, row, own_skip, scanned, states, grad_scan, width
    )
    grad_streams, grad_writes, grad_reads, reduced, totals, qz_parts, result_got = fence(
        grad_streams, grad_writes, grad_reads, reduced, totals, qz_parts, result_got
    )

    grad_streams = grad_streams.astype(bf16)
    grad_in_streams = dot(normed, grad_streams, TN).astype(bf16)
    sum_qz = scatter_outer(*qz_parts)
    sum_gate_up = jnp.concatenate([sum_gate, sum_up], axis=1)
    sum_gate_up = sum_gate_up.reshape(peers, in_rows, 2 * ff_width)
    gu_sums = by_distance(sum_gate_up)
    totals = totals.reshape(chunks, 8, heads, HEAD_M).sum(axis=3)
    last = from_start[:, -1, :] * totals[:, 0, :] + totals[:, 1, :]
    flow = reduced[:, :heads].reshape(chunks, CHUNK, heads)
    grad_rate = jnp.einsum("ts,cth->csh", lower, flow, precision=lax.Precision.HIGHEST)
    grad_rate = (grad_rate + last[:, None, :]).reshape(total_len, heads)
    grad_step = reduced[:, 32 : 32 + heads] - own_decay * grad_rate
    grad_raw = grad_step * jax.nn.sigmoid(raw_step + own_bias)
    grad_bias = jnp.sum(grad_raw, axis=0)
    grad_decay = jnp.sum(grad_rate * rates.reshape(total_len, heads), axis=0)
    grad_skip = jnp.sum(totals[:, 2, :], axis=0)
    if query_heads < KVH:
        blank = jnp.zeros((total_len, KVH * HD), f32)
        grad_keys = lax.dynamic_update_slice_in_dim(blank, grad_keys, own_kv, 1)
        grad_values = lax.dynamic_update_slice_in_dim(blank, grad_values, own_kv, 1)
    grad_shared = jnp.concatenate(
        [
            grad_writes.astype(bf16),
            grad_reads.astype(bf16),
            grad_keys.astype(bf16),
            grad_values.astype(bf16),
            pad_lanes(spread_cols(grad_raw.astype(bf16), head_block), 128),
        ],
        axis=1,
    )
    w_qz = jnp.concatenate([w_sq[:, width:], w_z], axis=1)

    def normed_rows(e):
        part = dot(chip_rows(grad_shared, e), w_shared, NT)
        part = part + dot(chip_rows(grad_streams, e), w_sq[:, :width], NT)
        part = part + dot(chip_rows(grad_qz, e), w_qz, NT)
        return part.astype(bf16).reshape(2, length, D)

    grad_in_shared = dot(normed, grad_shared, TN).astype(bf16)
    shared_part = grad_in_shared.reshape(groups, peers, in_rows, SHARED)
    shared_part = by_distance(shared_part.transpose(1, 0, 2, 3))
    shared_sums = far_sums(lambda m: shared_part[m])
    grad_in_streams, shared_sums, shared_part, grad_shared, gu_sums = fence(
        grad_in_streams, shared_sums, shared_part, grad_shared, gu_sums
    )

    streams_parts = scatter_inner(grad_in_streams.reshape(groups, -1, width))
    got_shared = send_far(shared_sums)
    far_rows = {e: normed_rows(e) for e in chips[1:]}
    sums = far_sums(core_part(far_rows))
    shared_near = chip_sum(lambda m: shared_part[m], 0)
    sums, grad_shared, streams_parts, got_shared, shared_near = fence(
        sums, grad_shared, streams_parts, got_shared, shared_near
    )

    sum_streams = scatter_outer(*streams_parts)
    sum_shared = total_of(shared_near, got_shared).astype(bf16)
    sum_shared = lax.psum_scatter(sum_shared, "dp", scatter_dimension=0, tiled=True)
    sum_shared = sum_shared[0].astype(f32)
    got = send_far(sums)
    got_gate_up = exchange_ctx(gu_sums)
    near_rows = normed_rows(0)
    near = chip_sum(core_part({0: near_rows}), 0)
    grad_gain_in = 0.0
    for e, rows in {0: near_rows, **far_rows}.items():
        unit = chip_rows(tokens, e).astype(f32) * chip_rows(scale_in, e)
        grad_gain_in += jnp.sum(rows.reshape(2 * length, D).astype(f32) * unit, axis=0)
    got, near, got_gate_up, grad_gain_in = fence(got, near, got_gate_up, grad_gain_in)

    result = middle + total_of(result_near, result_got)
    block_output = result.astype(bf16).reshape(block_input.shape)
    grad_normed = total_of(near, got)
    x_float = x_own.astype(f32)
    own_scale = rms_scale(x_float)
    own_unit = x_float * own_scale
    input_grad = grad_middle + norm_back(grad_normed * gain_in, own_unit, own_scale)
    input_grad = input_grad.reshape(block_input.shape)
    small_grad = jnp.concatenate(
        [
            grad_gain_in,
            grad_gain_mid,
            spread_cols(grad_gain_mix[None, :], pair_block)[0],
            spread_cols(grad_bias[None, :], head_block)[0],
            spread_cols(grad_decay[None, :], head_block)[0],
            spread_cols(grad_skip[None, :], head_block)[0],
        ]
    )
    small_grad = sum_dp(sum_ctx(small_grad))
    in_rate = rate_scale / math.sqrt(D)
    gate_up_state = (gate_up_weight, gate_up_first, gate_up_second)
    if strided:
        new_gate_up = update_dealt(
            place_arg, got_gate_up, None, *gate_up_state, ((0, 2 * FF, 0),), in_rate
        )
    else:
        got = place_ctx(got_gate_up).astype(f32)
        sum_gate_up = jnp.concatenate(
            [
                join_cols(got[:, :, :ff_width], row_block),
                join_cols(got[:, :, ff_width:], row_block),
            ],
            axis=1,
        )
        new_gate_up = adam_step(gate_up_weight, sum_gate_up, *gate_up_state[1:], in_rate)
    new_out = adam_step(
        out_weight, sum_out, out_first, out_second, rate_scale / math.sqrt(DSSM + QH * HD)
    )
    new_down = adam_step(
        down_weight, sum_down.astype(f32), down_first, down_second, rate_scale / math.sqrt(FF)
    )
    sum_own = jnp.concatenate([sum_streams, sum_qz], axis=1)
    sum_own, sum_shared, new_gate_up, new_out, new_down, input_grad, block_output = fence(
        sum_own, sum_shared, new_gate_up, new_out, new_down, input_grad, block_output
    )
    got = exchange_ctx(by_distance(sum_own.reshape(peers, in_rows, own_width)))
    placed = place_ctx({m: block[:, width:sq_width] for m, block in got.items()}).astype(f32)
    tail = jnp.concatenate(
        [
            sum_shared[:, : 2 * STATE],
            sum_shared[:, SHARED - 128 : SHARED - 128 + HEADS_M],
            join_cols(placed, query_block),
            sum_shared[:, 2 * STATE : SHARED - 128],
        ],
        axis=1,
    )
    if strided:
        spans = ((0, DSSM, sq_width), (DSSM, DSSM, 0))
        new_in = update_dealt(
            place_arg, got, tail, in_weight, in_first, in_second, spans, in_rate
        )
    else:
        got = place_ctx(got).astype(f32)
        sum_in = jnp.concatenate(
            [
                join_cols(got[:, :, sq_width:], pair_block),
                join_cols(got[:, :, :width], pair_block),
                tail,
            ],
            axis=1,
        )
        new_in = adam_step(in_weight, sum_in, in_first, in_second, in_rate)
    new_small = adam_step(small_params, small_grad, small_first, small_second, small_rate)
    return (block_output, input_grad, *new_in, *new_out, *new_gate_up, *new_down, *new_small)


def solution(mesh):
    rows = P(("dp", "ctx"), None)
    tokens = P("dp", "ctx", None)
    return jax.shard_map(
        shards,
        mesh=mesh,
        in_specs=(tokens, P("dp", "ctx"), tokens) + (rows,) * 12 + (P(),) * 3,
        out_specs=(tokens, tokens) + (rows,) * 12 + (P(),) * 3,
        check_vma=False,
    )
```

```python
import functools
import math

import jax
import jax.numpy as jnp
from jax import lax
from jax.experimental import pallas as pl
from jax.experimental.pallas import tpu as pltpu
from jax.sharding import PartitionSpec as P

D = 2048
FF = 4096
QH = 8
KVH = 2
HD = 128
HEADS_M = 48
HEAD_M = 64
STATE = 256
STEP = 10
DOC_MOST = 800
DSSM = HEADS_M * HEAD_M
SHARED = 2 * STATE + 2 * KVH * HD + 128
CHUNK = 256
QBLOCK = 256

norm_eps = 1e-05
beta_one = 0.9
beta_two = 0.95
adam_eps = 1e-08
weight_decay = 0.1
rate_scale = 3.0
small_rate = 0.3
bf16 = jnp.bfloat16
f32 = jnp.float32
NN = (((1,), (0,)), ((), ()))
NT = (((1,), (1,)), ((), ()))
TN = (((0,), (0,)), ((), ()))


def dot(a, b, dims=NN):
    return lax.dot_general(a, b, dims, preferred_element_type=f32)


def from_ctx(x, m):
    count = lax.axis_size("ctx")
    return lax.ppermute(x, "ctx", [(i ^ m, i) for i in range(count)])


def from_dp(x, j, k):
    count = lax.axis_size("dp")
    inner = count // 4
    pairs = []
    for i in range(count):
        z, w = divmod(i, inner)
        pairs.append((((z + j) % 4) * inner + (w + k) % inner, i))
    return lax.ppermute(x, "dp", pairs)


def fence(*trees):
    return lax.optimization_barrier(trees)


def outer_groups():
    count = lax.axis_size("dp")
    inner = count // 4
    return [[j * inner + k for j in range(4)] for k in range(inner)]


def gather_outer(own):
    return lax.all_gather(own, "dp", axis_index_groups=outer_groups())


def gather_outer_permuted(own):
    outer = lax.axis_index("dp") // (lax.axis_size("dp") // 4)
    full = jnp.stack([own] * 4)
    for j in (1, 3, 2):
        full = lax.dynamic_update_index_in_dim(
            full, from_dp(own, j, 0), lax.rem(outer + j, 4), 0
        )
    return full


def gather_inner(along):
    return {k: from_dp(along, 0, k) for k in range(1, lax.axis_size("dp") // 4)}


def place_dp(along, others):
    inner = lax.axis_size("dp") // 4
    place = lax.rem(lax.axis_index("dp"), inner)
    full = jnp.stack([along] * inner, axis=1)
    for k, block in others.items():
        full = lax.dynamic_update_index_in_dim(full, block, lax.rem(place + k, inner), 1)
    return full


def scatter_inner(full):
    inner = lax.axis_size("dp") // 4
    place = lax.rem(lax.axis_index("dp"), inner)
    full = full.reshape((4, inner) + full.shape[1:])

    def part(k):
        return lax.dynamic_index_in_dim(full, lax.rem(place + k, inner), 1, False)

    return part(0), {k: from_dp(part(k), 0, -k) for k in range(1, inner)}


def scatter_outer(own, got):
    total = own.astype(f32)
    for block in got.values():
        total = total + block.astype(f32)
    total = total.astype(bf16)
    total = lax.psum_scatter(
        total, "dp", scatter_dimension=0, axis_index_groups=outer_groups(), tiled=True
    )
    return total[0]


def across(own):
    return {m: from_ctx(own, m) for m in range(2, lax.axis_size("ctx"), 2)}


def beside(blocks):
    out = {}
    for m, block in blocks.items():
        out[m] = block
        out[m + 1] = from_ctx(block, 1)
    return out


def place_ctx(blocks, dim=0):
    shape = blocks[0].shape
    place = lax.axis_index("ctx")
    full = jnp.zeros(shape[:dim] + (lax.axis_size("ctx"),) + shape[dim:], blocks[0].dtype)
    for m, block in blocks.items():
        full = lax.dynamic_update_index_in_dim(full, block, place ^ m, dim)
    return full


def chip_sum(part, m):
    return part(m).astype(f32) + from_ctx(part(m + 1), 1).astype(f32)


def far_sums(part):
    return {m: chip_sum(part, m).astype(bf16) for m in range(2, lax.axis_size("ctx"), 2)}


def send_far(sums):
    return {m: from_ctx(block, m) for m, block in sums.items()}


def total_of(near, got):
    for block in got.values():
        near = near + block.astype(f32)
    return near


def scatter_ctx(part):
    got = send_far(far_sums(part))
    return total_of(chip_sum(part, 0), got)


def exchange_ctx(blocks):
    moved = [m for m in range(2, lax.axis_size("ctx"))] + [1]
    return {0: blocks[0], **{m: from_ctx(blocks[m], m) for m in moved}}


def by_distance(blocks):
    place = lax.axis_index("ctx")
    return [
        lax.dynamic_index_in_dim(blocks, place ^ m, 0, False) for m in range(lax.axis_size("ctx"))
    ]


def sum_ctx(x):
    m = 1
    while m < lax.axis_size("ctx"):
        x = x + from_ctx(x, m)
        m *= 2
    return x


def sum_dp(x):
    count = lax.axis_size("dp")
    m = 1
    while m < count:
        x = x + lax.ppermute(x, "dp", [(i ^ m, i) for i in range(count)])
        m *= 2
    return x


def split_cols(a, block):
    count = lax.axis_size("ctx")
    rows, n = a.shape
    a = a.reshape(rows, n // (count * block), count, block)
    return a.transpose(2, 0, 1, 3).reshape(count, rows, n // count)


def join_cols(a, block):
    count, rows, n = a.shape
    a = a.reshape(count, rows, n // block, block)
    return a.transpose(1, 2, 0, 3).reshape(rows, count * n)


def own_cols(a, block):
    count = lax.axis_size("ctx")
    rows, n = a.shape
    a = a.reshape(rows, n // (count * block), count, block)
    a = lax.dynamic_index_in_dim(a, lax.axis_index("ctx"), 2, False)
    return a.reshape(rows, n // count)


def spread_cols(a, block):
    count = lax.axis_size("ctx")
    rows, n = a.shape
    a = a.reshape(rows, n // block, block)
    full = jnp.zeros((rows, n // block, count, block), a.dtype)
    full = lax.dynamic_update_index_in_dim(full, a, lax.axis_index("ctx"), 2)
    return full.reshape(rows, count * n)


def attention_window(total_len):
    reach = -(-(DOC_MOST - 1) // QBLOCK) * QBLOCK
    return min(reach, total_len - QBLOCK), min(reach + QBLOCK, total_len)


def attention_scores(total_len, q_ref, k_ref, col_ref, row_ref):
    back, window = attention_window(total_len)
    first = pl.program_id(1) * QBLOCK
    start = pl.multiple_of(jnp.maximum(first - back, 0), QBLOCK)
    keys = k_ref[pl.ds(start, window), :]
    scores = dot(q_ref[...], keys, NT) * HD ** (-0.5)
    query_place = first + lax.broadcasted_iota(jnp.int32, (QBLOCK, window), 0)
    key_place = start + lax.broadcasted_iota(jnp.int32, (QBLOCK, window), 1)
    key_seg = row_ref[0:1, pl.ds(start, window)]
    allowed = (key_place <= query_place) & (col_ref[:, 0:1] == key_seg)
    return start, window, keys, jnp.where(allowed, scores, -1e30)


def attend_kernel(total_len, q_ref, k_ref, v_ref, col_ref, row_ref, out_ref, log_ref):
    start, window, _, scores = attention_scores(total_len, q_ref, k_ref, col_ref, row_ref)
    peak = jnp.max(scores, axis=1, keepdims=True)
    expo = jnp.exp(scores - peak)
    log_total = peak + jnp.log(jnp.sum(expo, axis=1, keepdims=True))
    shares = jnp.exp(scores - log_total).astype(bf16)
    out_ref[...] = dot(shares, v_ref[pl.ds(start, window), :]).astype(out_ref.dtype)
    log_ref[...] = jnp.broadcast_to(log_total, log_ref.shape)


def attend_back_kernel(
    total_len, q_ref, k_ref, v_ref, col_ref, row_ref, log_ref, grad_ref, dq_ref, dk_ref, dv_ref
):
    @pl.when(pl.program_id(1) == 0)
    def _():
        dk_ref[...] = jnp.zeros_like(dk_ref)
        dv_ref[...] = jnp.zeros_like(dv_ref)

    start, window, keys, scores = attention_scores(total_len, q_ref, k_ref, col_ref, row_ref)
    shares = jnp.exp(scores - log_ref[:, 0:1])
    grad = grad_ref[...]
    grad_shares = dot(grad, v_ref[pl.ds(start, window), :], NT)
    inner = jnp.sum(shares * grad_shares, axis=1, keepdims=True)
    grad_scores = (shares * (grad_shares - inner)).astype(bf16)
    scale = HD ** (-0.5)
    dq_ref[...] = dot(grad_scores, keys) * scale
    span = pl.ds(start, window)
    dk_ref[span, :] += dot(grad_scores, q_ref[...], TN) * scale
    dv_ref[span, :] += dot(shares.astype(bf16), grad, TN)


def attention_specs(total_len, offset):
    tile = pl.BlockSpec((QBLOCK, HD), lambda h, i: (i, h))
    whole = pl.BlockSpec((total_len, HD), lambda h, i: (0, h))
    later = pl.BlockSpec((total_len, HD), lambda h, i: (0, h + offset))
    col = pl.BlockSpec((QBLOCK, 128), lambda h, i: (i, 0))
    row = pl.BlockSpec((8, total_len), lambda h, i: (0, 0))
    return tile, whole, later, col, row


def attention_call(queries, pairs, offset, seg_col, seg_row):
    total_len, width = queries.shape
    tile, whole, later, col, row = attention_specs(total_len, offset)
    return pl.pallas_call(
        functools.partial(attend_kernel, total_len),
        grid=(width // HD, total_len // QBLOCK),
        in_specs=[tile, whole, later, col, row],
        out_specs=[tile, tile],
        out_shape=[
            jax.ShapeDtypeStruct((total_len, width), bf16),
            jax.ShapeDtypeStruct((total_len, width), f32),
        ],
        compiler_params=pltpu.CompilerParams(vmem_limit_bytes=48 * 2**20),
        cost_estimate=pl.CostEstimate(flops=1, bytes_accessed=1, transcendentals=0),
        name="attend",
    )(queries, pairs, pairs, seg_col, seg_row)


def attention_back_call(queries, pairs, offset, seg_col, seg_row, log_total, grad):
    total_len, width = queries.shape
    tile, whole, later, col, row = attention_specs(total_len, offset)
    return pl.pallas_call(
        functools.partial(attend_back_kernel, total_len),
        grid=(width // HD, total_len // QBLOCK),
        in_specs=[tile, whole, later, col, row, tile, tile],
        out_specs=[tile, whole, whole],
        out_shape=[jax.ShapeDtypeStruct((total_len, width), f32)] * 3,
        compiler_params=pltpu.CompilerParams(vmem_limit_bytes=48 * 2**20),
        cost_estimate=pl.CostEstimate(flops=1, bytes_accessed=1, transcendentals=0),
        name="attend_back",
    )(queries, pairs, pairs, seg_col, seg_row, log_total, grad)


def pair_of(col, offset, j, left):
    a = offset + 2 * j
    return jnp.where(left, col[:, a : a + 1], col[:, a + 1 : a + 2])


def state_decay(col, j, left_rows):
    last = col[CHUNK - 1 : CHUNK, :]
    a = 64 + 2 * j
    return jnp.where(left_rows, last[:, a : a + 1], last[:, a + 1 : a + 2])


def scan_kernel(pairs, x_ref, k_ref, r_ref, col_ref, row_ref, skip_ref, y_ref, s_ref, state):
    @pl.when(pl.program_id(0) == 0)
    def _():
        state[...] = jnp.zeros_like(state)

    writes = k_ref[...].astype(bf16)
    reads = r_ref[...].astype(bf16)
    col = col_ref[...]
    row = row_ref[...]
    entering = state[...].astype(bf16)
    s_ref[0] = entering
    products = dot(reads, writes, NT)
    later = lax.broadcasted_iota(jnp.int32, (CHUNK, CHUNK), 0)
    earlier = lax.broadcasted_iota(jnp.int32, (CHUNK, CHUNK), 1)
    mask = (later >= earlier) & (col[:, 127:128] == row[16:17, :])
    left = lax.broadcasted_iota(jnp.int32, (CHUNK, 128), 1) < HEAD_M
    left_rows = lax.broadcasted_iota(jnp.int32, (128, STATE), 0) < HEAD_M
    through = dot(reads, entering, NT)
    for j in range(pairs):
        lanes = slice(128 * j, 128 * j + 128)
        x = x_ref[:, lanes]
        scaled = x * pair_of(col, 32, j, left)
        scaled_low = scaled.astype(bf16)
        outs = []
        for h in (2 * j, 2 * j + 1):
            spread = col[:, h : h + 1] - row[h : h + 1, :]
            mixing = jnp.exp(jnp.where(mask, spread, -1e30)) * products
            outs.append(dot(mixing.astype(bf16), scaled_low))
        y_ref[:, lanes] = (
            jnp.where(left, outs[0], outs[1])
            + pair_of(col, 64, j, left) * through[:, lanes]
            + skip_ref[0:1, lanes] * x
        )
        to_end = (scaled * pair_of(col, 96, j, left)).astype(bf16)
        state[lanes, :] = state_decay(col, j, left_rows) * state[lanes, :] + dot(to_end, writes, TN)


def scan_back_kernel(
    pairs,
    x_ref,
    k_ref,
    r_ref,
    col_ref,
    row_ref,
    skip_ref,
    y_ref,
    s_ref,
    dy_ref,
    sum_ref,
    dx_ref,
    dk_ref,
    dr_ref,
    red_ref,
    tot_ref,
    adjoint,
    keep,
):
    @pl.when(pl.program_id(0) == 0)
    def _():
        adjoint[...] = jnp.zeros_like(adjoint)

    writes = k_ref[...].astype(bf16)
    reads = r_ref[...].astype(bf16)
    col = col_ref[...]
    row = row_ref[...]
    entering = s_ref[0]
    products = dot(writes, reads, NT)
    earlier = lax.broadcasted_iota(jnp.int32, (CHUNK, CHUNK), 0)
    later = lax.broadcasted_iota(jnp.int32, (CHUNK, CHUNK), 1)
    mask = (later >= earlier) & (col[:, 127:128] == row[16:17, :])
    left = lax.broadcasted_iota(jnp.int32, (CHUNK, 128), 1) < HEAD_M
    left_rows = lax.broadcasted_iota(jnp.int32, (128, STATE), 0) < HEAD_M
    incoming = adjoint[...]
    incoming_low = incoming.astype(bf16)
    values = dot(writes, incoming_low, NT)
    grad_products = jnp.zeros((CHUNK, CHUNK), f32)
    grad_writes = jnp.zeros((CHUNK, STATE), f32)
    grad_reads = jnp.zeros((CHUNK, STATE), f32)
    tot_ref[0] = jnp.zeros(tot_ref.shape[1:], f32)
    for j in range(pairs):
        lanes = slice(128 * j, 128 * j + 128)
        x = x_ref[:, lanes]
        step = pair_of(col, 32, j, left)
        scaled = x * step
        scaled_low = scaled.astype(bf16)
        dy = dy_ref[:, lanes]
        dy_low = dy.astype(bf16)
        grads = []
        for side, h in enumerate((2 * j, 2 * j + 1)):
            spread = row[h : h + 1, :] - col[:, h : h + 1]
            decay = jnp.exp(jnp.where(mask, spread, -1e30))
            half = left if side == 0 else jnp.logical_not(left)
            grad_mixing = dot(jnp.where(half, scaled_low, jnp.zeros_like(scaled_low)), dy_low, NT)
            grad_products += grad_mixing * decay
            grads.append(dot((decay * products).astype(bf16), dy_low))
        grad_scaled = jnp.where(left, grads[0], grads[1])
        decay_end = pair_of(col, 96, j, left)
        to_end = (scaled * decay_end).astype(bf16)
        passed = to_end.astype(f32) * values[:, lanes]
        skip = skip_ref[0:1, lanes]
        flow = (
            dy_low.astype(f32) * (y_ref[:, lanes] - skip * x)
            - scaled_low.astype(f32) * grad_scaled
            - passed
        )
        grad_scaled += decay_end * values[:, lanes]
        dx_ref[:, lanes] = (step * grad_scaled + skip * dy).astype(bf16)
        from_start = (pair_of(col, 64, j, left) * dy).astype(bf16)
        grad_reads += dot(from_start, entering[lanes, :])
        grad_writes += dot(to_end, incoming_low[lanes, :])
        pieces = (flow, x * grad_scaled)
        for n, piece in enumerate(pieces):
            high = piece.astype(bf16)
            keep[2 * n, :, lanes] = high
            keep[2 * n + 1, :, lanes] = (piece - high.astype(f32)).astype(bf16)
        tot_ref[0, 1:2, lanes] = jnp.sum(passed, axis=0, keepdims=True)
        tot_ref[0, 2:3, lanes] = jnp.sum(dy * x, axis=0, keepdims=True)
        product = incoming[lanes, :] * entering[lanes, :].astype(f32)
        high = product.astype(bf16)
        low = (product - high.astype(f32)).astype(bf16)
        ones = jnp.ones((8, STATE), bf16)
        tot_ref[0, 0:1, lanes] = (dot(ones, high, NT) + dot(ones, low, NT))[0:1, :]
        adjoint[lanes, :] = state_decay(col, j, left_rows) * incoming[lanes, :] + dot(
            from_start, reads, TN
        )
    grad_products = grad_products.astype(bf16)
    dk_ref[...] = (grad_writes + dot(grad_products, reads)).astype(bf16)
    dr_ref[...] = (grad_reads + dot(grad_products, writes, TN)).astype(bf16)
    sums = sum_ref[...]
    red_ref[...] = (
        dot(keep[0], sums[0]) + dot(keep[1], sums[0]) + dot(keep[2], sums[1]) + dot(keep[3], sums[1])
    )


def scan_call(own, shared, col, row, skip, width):
    total_len = own.shape[0]
    count = total_len // CHUNK
    return pl.pallas_call(
        functools.partial(scan_kernel, width // 128),
        grid=(count,),
        in_specs=[
            pl.BlockSpec((CHUNK, width), lambda i: (i, 0)),
            pl.BlockSpec((CHUNK, STATE), lambda i: (i, 0)),
            pl.BlockSpec((CHUNK, STATE), lambda i: (i, 1)),
            pl.BlockSpec((CHUNK, 128), lambda i: (i, 0)),
            pl.BlockSpec((24, CHUNK), lambda i: (0, i)),
            pl.BlockSpec((8, width), lambda i: (0, 0)),
        ],
        out_specs=[
            pl.BlockSpec((CHUNK, width), lambda i: (i, 0)),
            pl.BlockSpec((1, width, STATE), lambda i: (i, 0, 0)),
        ],
        out_shape=[
            jax.ShapeDtypeStruct((total_len, width), f32),
            jax.ShapeDtypeStruct((count, width, STATE), bf16),
        ],
        scratch_shapes=[pltpu.VMEM((width, STATE), f32)],
        compiler_params=pltpu.CompilerParams(vmem_limit_bytes=48 * 2**20),
        cost_estimate=pl.CostEstimate(flops=1, bytes_accessed=1, transcendentals=0),
        name="state_scan",
    )(own, shared, shared, col, row, skip)


def scan_back_call(own, shared, col, row, skip, scanned, states, grad, width):
    total_len = own.shape[0]
    count = total_len // CHUNK
    owner = jnp.arange(width)[:, None] // HEAD_M
    lane = jnp.arange(128)[None, :]
    sums = jnp.stack([owner == lane, owner + 32 == lane]).astype(bf16)

    def back(i):
        return count - 1 - i

    return pl.pallas_call(
        functools.partial(scan_back_kernel, width // 128),
        grid=(count,),
        in_specs=[
            pl.BlockSpec((CHUNK, width), lambda i: (back(i), 0)),
            pl.BlockSpec((CHUNK, STATE), lambda i: (back(i), 0)),
            pl.BlockSpec((CHUNK, STATE), lambda i: (back(i), 1)),
            pl.BlockSpec((CHUNK, 128), lambda i: (back(i), 0)),
            pl.BlockSpec((24, CHUNK), lambda i: (0, back(i))),
            pl.BlockSpec((8, width), lambda i: (0, 0)),
            pl.BlockSpec((CHUNK, width), lambda i: (back(i), 0)),
            pl.BlockSpec((1, width, STATE), lambda i: (back(i), 0, 0)),
            pl.BlockSpec((CHUNK, width), lambda i: (back(i), 0)),
            pl.BlockSpec((2, width, 128), lambda i: (0, 0, 0)),
        ],
        out_specs=[
            pl.BlockSpec((CHUNK, width), lambda i: (back(i), 0)),
            pl.BlockSpec((CHUNK, STATE), lambda i: (back(i), 0)),
            pl.BlockSpec((CHUNK, STATE), lambda i: (back(i), 0)),
            pl.BlockSpec((CHUNK, 128), lambda i: (back(i), 0)),
            pl.BlockSpec((1, 8, width), lambda i: (back(i), 0, 0)),
        ],
        out_shape=[
            jax.ShapeDtypeStruct((total_len, width), bf16),
            jax.ShapeDtypeStruct((total_len, STATE), bf16),
            jax.ShapeDtypeStruct((total_len, STATE), bf16),
            jax.ShapeDtypeStruct((total_len, 128), f32),
            jax.ShapeDtypeStruct((count, 8, width), f32),
        ],
        scratch_shapes=[pltpu.VMEM((width, STATE), f32), pltpu.VMEM((4, CHUNK, width), bf16)],
        compiler_params=pltpu.CompilerParams(vmem_limit_bytes=48 * 2**20),
        cost_estimate=pl.CostEstimate(flops=1, bytes_accessed=1, transcendentals=0),
        name="state_scan_back",
    )(own, shared, shared, col, row, skip, scanned, states, grad, sums)


def feed_kernel(per_block, *refs):
    own_ref, side_ref, cot_ref, gate_ref, up_ref, down_ref = refs[:6]
    back_ref, mid_ref, hidden_ref, grad_gate_ref, grad_up_ref = refs[-5:]
    first = pl.program_id(0) < per_block
    mid = jnp.where(first, own_ref[...], side_ref[...])
    mid_ref[...] = mid
    gate = dot(mid, gate_ref[...])
    upper = dot(mid, up_ref[...])
    grad_hidden = dot(cot_ref[...], down_ref[...], NT)
    sigma = jax.nn.sigmoid(gate)
    gate_half = gate * sigma
    hidden_ref[...] = (gate_half * upper).astype(bf16)
    grad_gate = (grad_hidden * upper * (sigma * (1.0 + gate * (1.0 - sigma)))).astype(bf16)
    grad_up = (grad_hidden * gate_half).astype(bf16)
    grad_gate_ref[...] = grad_gate
    grad_up_ref[...] = grad_up
    back_ref[...] = (dot(grad_gate, gate_ref[...], NT) + dot(grad_up, up_ref[...], NT)).astype(bf16)


def feed_call(e, own, side, cot, w_gate, w_up, w_down, kept):
    length = own.shape[0]
    total_len = cot.shape[0]
    columns = w_gate.shape[1]
    tile = min(256, length)
    per_block = length // tile
    tiles = 2 * per_block

    def held(shape):
        return pl.BlockSpec(shape, lambda i: (0, 0), pipeline_mode=pl.Buffered(1))

    def spread(n):
        return pl.BlockSpec((tile, n), lambda i: (i + e * tiles, 0))

    kept_shapes = [(total_len, D)] + [(total_len, columns)] * 3
    return pl.pallas_call(
        functools.partial(feed_kernel, per_block),
        grid=(tiles,),
        in_specs=[
            pl.BlockSpec((tile, D), lambda i: (jnp.minimum(i, per_block - 1), 0)),
            pl.BlockSpec((tile, D), lambda i: (jnp.maximum(i - per_block, 0), 0)),
            spread(D),
            held(w_gate.shape),
            held(w_up.shape),
            held(w_down.shape),
        ]
        + [pl.BlockSpec(memory_space=pl.ANY)] * len(kept),
        out_specs=[
            pl.BlockSpec((tile, D), lambda i: (i, 0)),
            spread(D),
            spread(columns),
            spread(columns),
            spread(columns),
        ],
        out_shape=[jax.ShapeDtypeStruct((2 * length, D), bf16)]
        + [jax.ShapeDtypeStruct(shape, bf16) for shape in kept_shapes],
        input_output_aliases={6 + n: 1 + n for n in range(len(kept))},
        compiler_params=pltpu.CompilerParams(vmem_limit_bytes=56 * 2**20),
        cost_estimate=pl.CostEstimate(flops=1, bytes_accessed=1, transcendentals=0),
        name="feed_forward",
    )(own, side, cot, w_gate, w_up, w_down, *kept)


def token_sum_kernel(a_ref, b_ref, out_ref):
    out_ref[...] = dot(a_ref[...], b_ref[...], TN).astype(bf16)


def token_sum(a, b):
    total_len, rows = a.shape
    columns = b.shape[1]
    tile = math.gcd(rows, 512)
    return pl.pallas_call(
        token_sum_kernel,
        grid=(rows // tile,),
        in_specs=[
            pl.BlockSpec((total_len, tile), lambda i: (0, i)),
            pl.BlockSpec((total_len, columns), lambda i: (0, 0), pipeline_mode=pl.Buffered(1)),
        ],
        out_specs=pl.BlockSpec((tile, columns), lambda i: (i, 0)),
        out_shape=jax.ShapeDtypeStruct((rows, columns), bf16),
        compiler_params=pltpu.CompilerParams(vmem_limit_bytes=56 * 2**20),
        cost_estimate=pl.CostEstimate(flops=1, bytes_accessed=1, transcendentals=0),
        name="token_sum",
    )(a, b)


def normed_kernel(width, chip_ref, streams_ref, qz_ref, shared_ref, sq_w_ref, z_w_ref, sh_w_ref, out_ref):
    query = qz_ref.shape[1] - width
    total = dot(streams_ref[...], sq_w_ref[:, :width], NT)
    total += dot(qz_ref[:, :query], sq_w_ref[:, width:], NT)
    total += dot(qz_ref[:, query:], z_w_ref[...], NT)
    total += dot(shared_ref[...], sh_w_ref[...], NT)
    out_ref[...] = total.astype(bf16)


def normed_call(chip, rows, streams, qz, shared, w_sq, w_z, w_shared):
    width = streams.shape[1]
    tile = 256
    tiles = rows // tile

    def picked(n):
        return pl.BlockSpec((tile, n), lambda i, chip: (chip[0] * tiles + i, 0))

    def held(shape):
        return pl.BlockSpec(shape, lambda i, chip: (0, 0), pipeline_mode=pl.Buffered(1))

    return pl.pallas_call(
        functools.partial(normed_kernel, width),
        grid_spec=pltpu.PrefetchScalarGridSpec(
            num_scalar_prefetch=1,
            grid=(tiles,),
            in_specs=[
                picked(width),
                picked(qz.shape[1]),
                picked(shared.shape[1]),
                held(w_sq.shape),
                held(w_z.shape),
                held(w_shared.shape),
            ],
            out_specs=pl.BlockSpec((tile, D), lambda i, chip: (i, 0)),
        ),
        out_shape=jax.ShapeDtypeStruct((rows, D), bf16),
        compiler_params=pltpu.CompilerParams(vmem_limit_bytes=48 * 2**20),
        cost_estimate=pl.CostEstimate(flops=1, bytes_accessed=1, transcendentals=0),
        name="grad_normed",
    )(chip, streams, qz, shared, w_sq, w_z, w_shared)


def pack_in_kernel(count, place_ref, w_ref, own_ref, shared_ref):
    place = place_ref[0]
    width = DSSM // count
    first_z = width + QH * HD // count
    query = 2 * DSSM + 2 * STATE + HEADS_M
    for c in range(count):
        m = c ^ place
        for n in range(DSSM // (count * HD)):
            at = (n * count + c) * HD
            to = slice(n * HD, (n + 1) * HD)
            own_ref[m, :, to] = w_ref[:, DSSM + at : DSSM + at + HD].astype(bf16)
            to = slice(first_z + n * HD, first_z + (n + 1) * HD)
            own_ref[m, :, to] = w_ref[:, at : at + HD].astype(bf16)
        for n in range(QH // count):
            at = query + (n * count + c) * HD
            to = slice(width + n * HD, width + (n + 1) * HD)
            own_ref[m, :, to] = w_ref[:, at : at + HD].astype(bf16)
    shared_ref[:, : 2 * STATE] = w_ref[:, 2 * DSSM : 2 * DSSM + 2 * STATE].astype(bf16)
    shared_ref[:, 2 * STATE : SHARED - 128] = w_ref[:, query + QH * HD :].astype(bf16)
    steps = w_ref[:, query - HEADS_M : query - HEADS_M + 128]
    lane = lax.broadcasted_iota(jnp.int32, steps.shape, 1)
    shared_ref[:, SHARED - 128 :] = jnp.where(lane < HEADS_M, steps, 0.0).astype(bf16)


def pack_in(place, weight):
    rows = weight.shape[0]
    count = lax.axis_size("ctx")
    own_width = (2 * DSSM + QH * HD) // count
    return pl.pallas_call(
        functools.partial(pack_in_kernel, count),
        in_specs=[pl.BlockSpec(memory_space=pltpu.SMEM), pl.BlockSpec(memory_space=pltpu.VMEM)],
        out_specs=[pl.BlockSpec(memory_space=pltpu.VMEM)] * 2,
        out_shape=[
            jax.ShapeDtypeStruct((count, rows, own_width), bf16),
            jax.ShapeDtypeStruct((rows, SHARED), bf16),
        ],
        compiler_params=pltpu.CompilerParams(vmem_limit_bytes=48 * 2**20),
        name="pack_in",
    )(place, weight)


def pack_gate_up_kernel(count, place_ref, w_ref, out_ref):
    place = place_ref[0]
    blocks = FF // (count * HD)
    for c in range(count):
        m = c ^ place
        for n in range(2 * blocks):
            at = (n * count + c) * HD
            out_ref[m, :, n * HD : (n + 1) * HD] = w_ref[:, at : at + HD].astype(bf16)


def pack_gate_up(place, weight):
    rows = weight.shape[0]
    count = lax.axis_size("ctx")
    return pl.pallas_call(
        functools.partial(pack_gate_up_kernel, count),
        in_specs=[pl.BlockSpec(memory_space=pltpu.SMEM), pl.BlockSpec(memory_space=pltpu.VMEM)],
        out_specs=pl.BlockSpec(memory_space=pltpu.VMEM),
        out_shape=jax.ShapeDtypeStruct((count, rows, 2 * FF // count), bf16),
        compiler_params=pltpu.CompilerParams(vmem_limit_bytes=48 * 2**20),
        name="pack_gate_up",
    )(place, weight)


def update_kernel(count, spans, rate, place_ref, g_ref, *refs):
    tail_ref = refs[0] if len(refs) == 7 else None
    w_ref, first_ref, second_ref, new_w_ref, new_first_ref, new_second_ref = refs[-6:]
    place = place_ref[0]

    def update(cols, grad):
        new = adam_step(w_ref[:, cols], grad, first_ref[:, cols], second_ref[:, cols], rate)
        new_w_ref[:, cols], new_first_ref[:, cols], new_second_ref[:, cols] = new

    for first, columns, at in spans:
        for n in range(columns // (count * HD)):
            for c in range(count):
                start = first + (n * count + c) * HD
                grad = g_ref[c ^ place, :, at : at + HD].astype(f32)
                update(slice(start, start + HD), grad)
            at += HD
    if tail_ref is not None:
        update(slice(2 * DSSM, w_ref.shape[1]), tail_ref[...])


def update_dealt(place, got, tail, weight, first, second, spans, rate):
    rows, columns = weight.shape
    count = lax.axis_size("ctx")
    got = jnp.stack([got[m] for m in range(count)])
    block = 16

    def flat(n):
        return pl.BlockSpec((block, n), lambda i: (i, 0))

    tails = [] if tail is None else [tail]
    return pl.pallas_call(
        functools.partial(update_kernel, count, spans, rate),
        grid=(rows // block,),
        in_specs=[
            pl.BlockSpec(memory_space=pltpu.SMEM),
            pl.BlockSpec((count, block, got.shape[2]), lambda i: (0, i, 0)),
        ]
        + [flat(t.shape[1]) for t in tails]
        + [flat(columns)] * 3,
        out_specs=[flat(columns)] * 3,
        out_shape=[jax.ShapeDtypeStruct((rows, columns), f32)] * 3,
        compiler_params=pltpu.CompilerParams(vmem_limit_bytes=48 * 2**20),
        cost_estimate=pl.CostEstimate(flops=1, bytes_accessed=1, transcendentals=0),
        name="update",
    )(place, got, *tails, weight, first, second)


def rms_scale(values):
    return lax.rsqrt(jnp.mean(values * values, axis=-1, keepdims=True) + norm_eps)


def norm_back(grad_unit, unit, scale):
    return scale * (grad_unit - unit * jnp.mean(grad_unit * unit, axis=-1, keepdims=True))


def silu_slope(values):
    sigma = jax.nn.sigmoid(values)
    return sigma * (1.0 + values * (1.0 - sigma))


def split_small(small):
    widths = [D, D, DSSM, HEADS_M, HEADS_M, HEADS_M]
    pieces = []
    start = 0
    for count in widths:
        pieces.append(small[start : start + count])
        start += count
    return pieces


def adam_step(weight, grad, first, second, rate):
    first = beta_one * first + (1.0 - beta_one) * grad
    second = beta_two * second + (1.0 - beta_two) * grad * grad
    fixed_first = first / (1.0 - beta_one**STEP)
    fixed_second = second / (1.0 - beta_two**STEP)
    weight = weight - rate * (
        fixed_first / (jnp.sqrt(fixed_second) + adam_eps) + weight_decay * weight
    )
    return (weight, first, second)


def pad_lanes(a, width):
    return jnp.pad(a, ((0, 0), (0, width - a.shape[1])))


def shards(
    block_input,
    segment_ids,
    cotangent,
    in_weight,
    out_weight,
    gate_up_weight,
    down_weight,
    in_first,
    out_first,
    gate_up_first,
    down_first,
    in_second,
    out_second,
    gate_up_second,
    down_second,
    small_params,
    small_first,
    small_second,
):
    peers = lax.axis_size("ctx")
    groups = lax.axis_size("dp")
    place = lax.axis_index("ctx")
    length = block_input.shape[0] * block_input.shape[1]
    total_len = length * peers
    row_block = out_weight.shape[0]
    in_rows = in_weight.shape[0]
    strided = row_block == HD
    width = DSSM // peers
    heads = HEADS_M // peers
    query_heads = QH // peers
    query_width = query_heads * HD
    own_width = 2 * width + query_width
    ff_width = FF // peers
    pair_block = 2 * HEAD_M if strided else width
    query_block = HD if strided else query_width
    head_block = 2 if strided else heads
    gain_in, gain_mid, gain_mix, step_bias, decay_log, skip = split_small(small_params)

    place_arg = place.astype(jnp.int32).reshape(1)
    base = 2 * DSSM + 2 * STATE + HEADS_M
    query_end = base + QH * HD
    if strided:
        own_low, shared_low = pack_in(place_arg, in_weight)
        gu_low = pack_gate_up(place_arg, gate_up_weight)
        own_low = [own_low[m] for m in range(peers)]
        gu_low = [gu_low[m] for m in range(peers)]
    else:
        in_low = in_weight.astype(bf16)
        shared_low = jnp.concatenate(
            [
                in_low[:, 2 * DSSM : 2 * DSSM + 2 * STATE],
                in_low[:, query_end:],
                in_low[:, 2 * DSSM + 2 * STATE : base],
                jnp.zeros((in_rows, 128 - HEADS_M), bf16),
            ],
            axis=1,
        )
        own_low = jnp.concatenate(
            [
                split_cols(in_low[:, DSSM : 2 * DSSM], pair_block),
                split_cols(in_low[:, base:query_end], query_block),
                split_cols(in_low[:, :DSSM], pair_block),
            ],
            axis=2,
        )
        own_low = by_distance(own_low)
        gu_low = gate_up_weight.astype(bf16)
        gu_low = jnp.concatenate(
            [split_cols(gu_low[:, :FF], row_block), split_cols(gu_low[:, FF:], row_block)], axis=2
        )
        gu_low = by_distance(gu_low)
    seg_own = segment_ids.reshape(length)
    segments = place_ctx(beside({0: seg_own, **across(seg_own)})).reshape(total_len)
    own_rows = place_ctx(exchange_ctx(own_low)).reshape(peers * in_rows, own_width)
    x_own = block_input.reshape(length, D)
    shared_along = gather_outer_permuted(shared_low)
    out_low = out_weight.astype(bf16)
    down_low = down_weight.astype(bf16)
    own_rows, x_own, shared_along, gu_low, down_low, segments = fence(
        own_rows, x_own, shared_along, gu_low, down_low, segments
    )

    sq_width = width + query_width
    sq_along = gather_outer(own_rows[:, :sq_width])
    z_along = gather_outer(own_rows[:, sq_width:])
    x_far = across(x_own)
    shared_rows = place_dp(shared_along, gather_inner(shared_along))
    shared_rows = shared_rows.reshape((groups,) + shared_low.shape)
    down_inner = gather_inner(down_low)
    cot_own = cotangent.reshape(length, D)
    own_bias = own_cols(step_bias[None, :], head_block)
    own_decay = jnp.exp(own_cols(decay_log[None, :], head_block))
    own_skip = jnp.repeat(own_cols(skip[None, :], head_block), HEAD_M, axis=1)
    own_skip = jnp.broadcast_to(own_skip, (8, width))
    own_gain_mix = own_cols(gain_mix[None, :], pair_block)
    chunks = total_len // CHUNK
    seg_chunks = segments.reshape(chunks, CHUNK)
    seg_last = seg_chunks[:, -1:]
    seg_before = jnp.concatenate([jnp.full((1, 1), -1, seg_last.dtype), seg_last[:-1]], axis=0)
    entering = (seg_chunks == seg_before).astype(f32)[:, :, None]
    leaving = jnp.where(seg_chunks == seg_last, 0.0, -1e30)[:, :, None]
    seg_float = segments.astype(f32)
    seg_col = jnp.broadcast_to(seg_float[:, None], (total_len, 128))
    seg_row = jnp.broadcast_to(seg_float[None, :], (8, total_len))
    (x_own, x_far, shared_rows, gu_low, cot_own, sq_along, out_low, down_low, down_inner) = fence(
        x_own, x_far, shared_rows, gu_low, cot_own, sq_along, out_low, down_low, down_inner
    )
    own_bias, own_decay, own_skip, own_gain_mix, entering, leaving, seg_col, seg_row, x_far = fence(
        own_bias, own_decay, own_skip, own_gain_mix, entering, leaving, seg_col, seg_row, x_far
    )

    shared_far = across(shared_rows)
    if strided:
        out_along = gather_outer(out_low)
    sq_others = gather_inner(sq_along)
    tokens = place_ctx(beside({0: x_own, **x_far})).reshape(total_len, D)
    scale_in = rms_scale(tokens.astype(f32))
    normed = (tokens.astype(f32) * scale_in * gain_in).astype(bf16)
    normed, shared_rows, shared_far, sq_along, sq_others, z_along, cot_own, gu_low = fence(
        normed, shared_rows, shared_far, sq_along, sq_others, z_along, cot_own, gu_low
    )

    z_others = gather_inner(z_along)
    w_shared = place_ctx(beside({0: shared_rows, **shared_far}), 1).reshape(D, SHARED)
    pairs = dot(normed, w_shared[:, 2 * STATE : SHARED - 128]).astype(bf16)
    writes_reads = dot(normed, w_shared[:, : 2 * STATE])
    raw_all = dot(normed, w_shared[:, SHARED - 128 :])
    if not strided:
        out_along = {}
    normed, pairs, writes_reads, raw_all, z_along, z_others, out_along, cot_own, gu_low = fence(
        normed, pairs, writes_reads, raw_all, z_along, z_others, out_along, cot_own, gu_low
    )

    gu_rows = place_ctx(exchange_ctx(gu_low)).reshape(peers * in_rows, 2 * ff_width)
    gate_along = gather_outer(gu_rows[:, :ff_width])
    up_along = gather_outer(gu_rows[:, ff_width:])
    out_others = gather_inner(out_along) if strided else {}
    cot_far = across(cot_own)
    w_sq = place_dp(sq_along, sq_others).reshape(D, sq_width)
    streams = dot(normed, w_sq[:, :width])
    queries = dot(normed, w_sq[:, width:]).astype(bf16)
    raw_step = own_cols(raw_all[:, :HEADS_M], head_block)
    offset = KVH
    if query_heads < KVH:
        offset = query_heads
        own_kv = (place * query_heads * KVH // QH) * HD
        pairs = jnp.concatenate(
            [
                lax.dynamic_slice_in_dim(pairs, own_kv, query_width, 1),
                lax.dynamic_slice_in_dim(pairs, KVH * HD + own_kv, query_width, 1),
            ],
            axis=1,
        )
    step = jax.nn.softplus(raw_step + own_bias)
    rates = (-own_decay * step).reshape(chunks, CHUNK, heads)
    order = jnp.arange(CHUNK)
    lower = (order[:, None] >= order[None, :]).astype(f32)
    running = jnp.einsum("ts,csh->cth", lower, rates, precision=lax.Precision.HIGHEST)
    from_start = jnp.exp(running) * entering
    to_end = jnp.exp(jnp.where(leaving == 0.0, running[:, -1:, :] - running, -1e30))
    running = running.reshape(total_len, heads)
    col = jnp.concatenate(
        [
            pad_lanes(running, 32),
            pad_lanes(step, 32),
            pad_lanes(from_start.reshape(total_len, heads), 32),
            pad_lanes(to_end.reshape(total_len, heads), 31),
            seg_col[:, :1],
        ],
        axis=1,
    )
    row = jnp.concatenate([jnp.pad(running.T, ((0, 16 - heads), (0, 0))), seg_row], axis=0)

    scanned, states = scan_call(streams, writes_reads, col, row, own_skip, width)
    normed, scanned, queries, out_along, out_others, gate_along, cot_own, cot_far = fence(
        normed, scanned, queries, out_along, out_others, gate_along, cot_own, cot_far
    )

    gate_others = gather_inner(gate_along)
    inner_place = lax.rem(lax.axis_index("dp"), groups // 4)
    down_pair = jnp.stack([down_low] * (groups // 4))
    for k, block in down_inner.items():
        at = lax.rem(inner_place + k, groups // 4)
        down_pair = lax.dynamic_update_index_in_dim(down_pair, block, at, 0)
    w_down = gather_outer(down_pair).reshape(ff_width, D)
    cot = jnp.concatenate(
        [block for _, block in sorted(beside({0: cot_own, **cot_far}).items())], axis=0
    )
    w_z = place_dp(z_along, z_others).reshape(D, width)
    gate_z = dot(normed, w_z)
    attended, log_total = attention_call(queries, pairs, offset, seg_col, seg_row)
    gate_act = jax.nn.silu(gate_z)
    gated = scanned * gate_act
    square = sum_ctx(jnp.sum(gated * gated, axis=-1))
    scale_mix = lax.rsqrt(square / DSSM + norm_eps)[:, None]
    unit_mix = gated * scale_mix
    joined = jnp.concatenate([(unit_mix * own_gain_mix).astype(bf16), attended], axis=1)
    joined, gate_along, gate_others, up_along = fence(joined, gate_along, gate_others, up_along)
    up_others = gather_inner(up_along)
    if strided:
        w_out = place_dp(out_along, out_others).reshape(sq_width, D)
    else:
        whole_out = lax.all_gather(out_low, ("dp", "ctx"), axis=0, tiled=True)
        w_out = jnp.concatenate(
            [
                lax.dynamic_slice_in_dim(whole_out, place * width, width, 0),
                lax.dynamic_slice_in_dim(whole_out, DSSM + place * query_width, query_width, 0),
            ],
            axis=0,
        )

    chips = list(range(peers // 2))
    parity = place % 2

    def chip_rows(full, e):
        start = ((place // 2) ^ e) * 2 * length
        return lax.dynamic_slice_in_dim(full, start, 2 * length, 0)

    def core_part(parts):
        return lambda m: lax.dynamic_index_in_dim(parts[m // 2], (m % 2) ^ parity, 0, False)

    def mixed_rows(e):
        return dot(chip_rows(joined, e), w_out).astype(bf16).reshape(2, length, D)

    sums = far_sums(core_part({e: mixed_rows(e) for e in chips[1:]}))
    sums, joined, gate_along, gate_others = fence(sums, joined, gate_along, gate_others)
    w_gate = place_dp(gate_along, gate_others).reshape(D, ff_width)
    got = send_far(sums)
    near = chip_sum(core_part({0: mixed_rows(0)}), 0)
    got, near, up_others, w_gate = fence(got, near, up_others, w_gate)

    middle = x_own.astype(f32) + total_of(near, got)
    scale_mid = rms_scale(middle)
    unit_mid = middle * scale_mid
    mid_own = (unit_mid * gain_mid).astype(bf16)
    w_up = place_dp(up_along, up_others).reshape(D, ff_width)
    def feed_forward(e, own, side, kept):
        back, *kept = feed_call(e, own, side, cot, w_gate, w_up, w_down, kept)
        return back.reshape(2, length, D), kept

    far = across(mid_own)
    near_back, kept = feed_forward(0, mid_own, from_ctx(mid_own, 1), [])
    far, near_back, kept = fence(far, near_back, kept)
    far = beside(far)
    far_back = {}
    for e in chips[1:]:
        far_back[e], kept = feed_forward(e, far[2 * e], far[2 * e + 1], kept)
    sums = far_sums(lambda m: far_back[m // 2][m % 2])
    sums, near_back, kept = fence(sums, near_back, kept)
    normed_mid, hidden, grad_gate, grad_up = kept
    got = send_far(sums)
    near = chip_sum(lambda m: near_back[m], 0)
    grad_gate = token_sum(normed_mid, grad_gate)
    grad_down = token_sum(hidden, cot)
    got, near, grad_gate, grad_down, normed_mid, grad_up = fence(
        got, near, grad_gate, grad_down, normed_mid, grad_up
    )

    gate_parts = scatter_inner(grad_gate.reshape(groups, -1, ff_width))
    sum_down = lax.psum_scatter(
        grad_down.reshape(4, groups // 4, row_block, D),
        "dp",
        scatter_dimension=0,
        axis_index_groups=outer_groups(),
        tiled=True,
    )
    grad_normed_mid = total_of(near, got)
    grad_middle = cot_own.astype(f32) + norm_back(grad_normed_mid * gain_mid, unit_mid, scale_mid)
    grad_middle_low = grad_middle.astype(bf16)
    grad_middle_low, hidden, normed_mid, grad_up = fence(
        grad_middle_low, hidden, normed_mid, grad_up
    )

    far = across(grad_middle_low)
    beside_own = beside({0: grad_middle_low})
    result_part = dot(hidden, w_down).astype(bf16).reshape(peers, length, D)
    grad_up = token_sum(normed_mid, grad_up)
    far, beside_own, result_part, gate_parts, grad_up = fence(
        far, beside_own, result_part, gate_parts, grad_up
    )

    grad_mixed = place_ctx({**beside_own, **beside(far)}).reshape(total_len, D)
    sum_gate = scatter_outer(*gate_parts)
    up_parts = scatter_inner(grad_up.reshape(groups, -1, ff_width))
    grad_gain_mid = jnp.sum(grad_normed_mid * unit_mid, axis=0)
    sums = far_sums(lambda m: result_part[m])
    result_near = chip_sum(lambda m: result_part[m], 0)
    grad_joined = dot(grad_mixed, w_out, NT)
    if strided:
        grad_out = token_sum(joined, grad_mixed)
        out_parts = scatter_inner(grad_out.reshape(groups, row_block, D))
    else:
        grad_out = dot(joined, grad_mixed, TN)
        out_parts = ()
        spread = jnp.zeros((DSSM + QH * HD, D), f32)
        spread = lax.dynamic_update_slice_in_dim(spread, grad_out[:width], place * width, 0)
        spread = lax.dynamic_update_slice_in_dim(
            spread, grad_out[width:], DSSM + place * query_width, 0
        )
        sum_out = lax.psum_scatter(spread, ("dp", "ctx"), scatter_dimension=0, tiled=True)
    grad_attended = grad_joined[:, width:].astype(bf16)
    grad_mix_part = grad_joined[:, :width]
    grad_unit = grad_mix_part * own_gain_mix
    inner = sum_ctx(jnp.sum(grad_unit * unit_mix, axis=-1))[:, None] / DSSM
    grad_queries, grad_keys, grad_values = attention_back_call(
        queries, pairs, offset, seg_col, seg_row, log_total, grad_attended
    )
    grad_queries, inner, up_parts, out_parts, sums = fence(
        grad_queries, inner, up_parts, out_parts, sums
    )

    result_got = send_far(sums)
    inner_count = groups // 4
    down_own = lax.dynamic_index_in_dim(sum_down[0], inner_place, 0, False)
    down_got = {
        k: from_dp(
            lax.dynamic_index_in_dim(
                sum_down[0], lax.rem(inner_place + k, inner_count), 0, False
            ),
            0,
            -k,
        )
        for k in range(1, inner_count)
    }
    sum_down = total_of(down_own.astype(f32), down_got)
    sum_up = scatter_outer(*up_parts)
    if strided:
        sum_out = scatter_outer(*out_parts).astype(f32)
    grad_gain_mix = jnp.sum(grad_mix_part * unit_mix, axis=0)
    grad_gated = scale_mix * (grad_unit - unit_mix * inner)
    grad_scan = grad_gated * gate_act
    grad_z = grad_gated * scanned * silu_slope(gate_z)
    grad_qz = jnp.concatenate([grad_queries.astype(bf16), grad_z.astype(bf16)], axis=1)
    grad_in_qz = token_sum(normed, grad_qz)
    grad_in_qz, grad_scan = fence(grad_in_qz, grad_scan)

    qz_parts = scatter_inner(grad_in_qz.reshape(groups, -1, sq_width))
    grad_streams, grad_writes, grad_reads, reduced, totals = scan_back_call(
        streams, writes_reads, col, row, own_skip, scanned, states, grad_scan, width
    )
    grad_streams, grad_writes, grad_reads, reduced, totals, qz_parts, result_got = fence(
        grad_streams, grad_writes, grad_reads, reduced, totals, qz_parts, result_got
    )

    grad_in_streams = token_sum(normed, grad_streams)
    sum_qz = scatter_outer(*qz_parts)
    totals = totals.reshape(chunks, 8, heads, HEAD_M).sum(axis=3)
    last = from_start[:, -1, :] * totals[:, 0, :] + totals[:, 1, :]
    flow = reduced[:, :heads].reshape(chunks, CHUNK, heads)
    grad_rate = jnp.einsum("ts,cth->csh", lower, flow, precision=lax.Precision.HIGHEST)
    grad_rate = (grad_rate + last[:, None, :]).reshape(total_len, heads)
    grad_step = reduced[:, 32 : 32 + heads] - own_decay * grad_rate
    grad_raw = grad_step * jax.nn.sigmoid(raw_step + own_bias)
    if query_heads < KVH:
        blank = jnp.zeros((total_len, KVH * HD), f32)
        grad_keys = lax.dynamic_update_slice_in_dim(blank, grad_keys, own_kv, 1)
        grad_values = lax.dynamic_update_slice_in_dim(blank, grad_values, own_kv, 1)
    grad_shared = jnp.concatenate(
        [
            grad_writes,
            grad_reads,
            grad_keys.astype(bf16),
            grad_values.astype(bf16),
            pad_lanes(spread_cols(grad_raw.astype(bf16), head_block), 128),
        ],
        axis=1,
    )
    grad_in_streams, grad_shared, normed, grad_raw, grad_rate, totals, sum_gate, sum_up = fence(
        grad_in_streams, grad_shared, normed, grad_raw, grad_rate, totals, sum_gate, sum_up
    )

    def normed_rows(e):
        chip = ((place // 2) ^ e).astype(jnp.int32).reshape(1)
        part = normed_call(
            chip, 2 * length, grad_streams, grad_qz, grad_shared, w_sq, w_z, w_shared
        )
        return part.reshape(2, length, D)

    streams_parts = scatter_inner(grad_in_streams.reshape(groups, -1, width))
    grad_in_shared = token_sum(normed, grad_shared)
    far_rows = {e: normed_rows(e) for e in chips[1:]}
    streams_parts, grad_in_shared, far_rows, sum_gate, sum_up, sum_out, sum_down, result_got = fence(
        streams_parts, grad_in_shared, far_rows, sum_gate, sum_up, sum_out, sum_down, result_got
    )

    sum_streams = scatter_outer(*streams_parts)
    shared_part = grad_in_shared.reshape(groups, peers, in_rows, SHARED)

    def shared_of(m):
        return lax.dynamic_index_in_dim(shared_part, place ^ m, 1, False)

    shared_sums = far_sums(shared_of)
    sums = far_sums(core_part(far_rows))
    shared_sums, sums, shared_part, grad_shared = fence(shared_sums, sums, shared_part, grad_shared)

    got_shared = send_far(shared_sums)
    shared_near = chip_sum(shared_of, 0)
    near_rows = normed_rows(0)
    got_shared, shared_near, near_rows, sums = fence(got_shared, shared_near, near_rows, sums)

    got = send_far(sums)
    sum_shared = total_of(shared_near, got_shared).astype(bf16)
    sum_shared = scatter_outer(*scatter_inner(sum_shared)).astype(f32)
    near = chip_sum(core_part({0: near_rows}), 0)
    grad_gain_in = 0.0
    for e, rows in {0: near_rows, **far_rows}.items():
        unit = chip_rows(tokens, e).astype(f32) * chip_rows(scale_in, e)
        grad_gain_in += jnp.sum(rows.reshape(2 * length, D).astype(f32) * unit, axis=0)
    got, near, grad_gain_in = fence(got, near, grad_gain_in)

    sum_own = jnp.concatenate([sum_streams, sum_qz], axis=1)
    got_own = exchange_ctx(by_distance(sum_own.reshape(peers, in_rows, own_width)))
    sum_gate_up = jnp.concatenate([sum_gate, sum_up], axis=1)
    gu_sums = by_distance(sum_gate_up.reshape(peers, in_rows, 2 * ff_width))
    got_gate_up = exchange_ctx(gu_sums)
    grad_bias = jnp.sum(grad_raw, axis=0)
    grad_decay = jnp.sum(grad_rate * rates.reshape(total_len, heads), axis=0)
    grad_skip = jnp.sum(totals[:, 2, :], axis=0)

    result = middle + total_of(result_near, result_got)
    block_output = result.astype(bf16).reshape(block_input.shape)
    grad_normed = total_of(near, got)
    x_float = x_own.astype(f32)
    own_scale = rms_scale(x_float)
    own_unit = x_float * own_scale
    input_grad = grad_middle + norm_back(grad_normed * gain_in, own_unit, own_scale)
    input_grad = input_grad.reshape(block_input.shape)
    small_grad = jnp.concatenate(
        [
            grad_gain_in,
            grad_gain_mid,
            spread_cols(grad_gain_mix[None, :], pair_block)[0],
            spread_cols(grad_bias[None, :], head_block)[0],
            spread_cols(grad_decay[None, :], head_block)[0],
            spread_cols(grad_skip[None, :], head_block)[0],
        ]
    )
    small_grad = sum_dp(sum_ctx(small_grad))
    in_rate = rate_scale / math.sqrt(D)
    gate_up_state = (gate_up_weight, gate_up_first, gate_up_second)
    if strided:
        new_gate_up = update_dealt(
            place_arg, got_gate_up, None, *gate_up_state, ((0, 2 * FF, 0),), in_rate
        )
    else:
        got = place_ctx(got_gate_up).astype(f32)
        sum_gate_up = jnp.concatenate(
            [
                join_cols(got[:, :, :ff_width], row_block),
                join_cols(got[:, :, ff_width:], row_block),
            ],
            axis=1,
        )
        new_gate_up = adam_step(gate_up_weight, sum_gate_up, *gate_up_state[1:], in_rate)
    new_out = adam_step(
        out_weight, sum_out, out_first, out_second, rate_scale / math.sqrt(DSSM + QH * HD)
    )
    new_down = adam_step(
        down_weight, sum_down, down_first, down_second, rate_scale / math.sqrt(FF)
    )
    got = got_own
    placed = place_ctx({m: block[:, width:sq_width] for m, block in got.items()}).astype(f32)
    tail = jnp.concatenate(
        [
            sum_shared[:, : 2 * STATE],
            sum_shared[:, SHARED - 128 : SHARED - 128 + HEADS_M],
            join_cols(placed, query_block),
            sum_shared[:, 2 * STATE : SHARED - 128],
        ],
        axis=1,
    )
    if strided:
        spans = ((0, DSSM, sq_width), (DSSM, DSSM, 0))
        new_in = update_dealt(
            place_arg, got, tail, in_weight, in_first, in_second, spans, in_rate
        )
    else:
        got = place_ctx(got).astype(f32)
        sum_in = jnp.concatenate(
            [
                join_cols(got[:, :, sq_width:], pair_block),
                join_cols(got[:, :, :width], pair_block),
                tail,
            ],
            axis=1,
        )
        new_in = adam_step(in_weight, sum_in, in_first, in_second, in_rate)
    new_small = adam_step(small_params, small_grad, small_first, small_second, small_rate)
    return (block_output, input_grad, *new_in, *new_out, *new_gate_up, *new_down, *new_small)


def solution(mesh):
    rows = P(("dp", "ctx"), None)
    tokens = P("dp", "ctx", None)
    return jax.shard_map(
        shards,
        mesh=mesh,
        in_specs=(tokens, P("dp", "ctx"), tokens) + (rows,) * 12 + (P(),) * 3,
        out_specs=(tokens, tokens) + (rows,) * 12 + (P(),) * 3,
        check_vma=False,
    )
```

```python
import functools
import math

import jax
import jax.numpy as jnp
from jax import lax
from jax.experimental import pallas as pl
from jax.experimental.pallas import tpu as pltpu
from jax.sharding import PartitionSpec as P

D = 2048
FF = 4096
QH = 8
KVH = 2
HD = 128
HEADS_M = 48
HEAD_M = 64
STATE = 256
STEP = 10
DOC_MOST = 800
DSSM = HEADS_M * HEAD_M
SHARED = 2 * STATE + 2 * KVH * HD + 128
CHUNK = 256
QBLOCK = 256

norm_eps = 1e-05
beta_one = 0.9
beta_two = 0.95
adam_eps = 1e-08
weight_decay = 0.1
rate_scale = 3.0
small_rate = 0.3
bf16 = jnp.bfloat16
f32 = jnp.float32
NN = (((1,), (0,)), ((), ()))
NT = (((1,), (1,)), ((), ()))
TN = (((0,), (0,)), ((), ()))


def dot(a, b, dims=NN):
    return lax.dot_general(a, b, dims, preferred_element_type=f32)


def from_ctx(x, m):
    count = lax.axis_size("ctx")
    return lax.ppermute(x, "ctx", [(i ^ m, i) for i in range(count)])


def from_dp(x, j, k):
    count = lax.axis_size("dp")
    inner = count // 4
    pairs = []
    for i in range(count):
        z, w = divmod(i, inner)
        pairs.append((((z + j) % 4) * inner + (w + k) % inner, i))
    return lax.ppermute(x, "dp", pairs)


def fence(*trees):
    return lax.optimization_barrier(trees)


def outer_groups():
    count = lax.axis_size("dp")
    inner = count // 4
    return [[j * inner + k for j in range(4)] for k in range(inner)]


def gather_outer(own):
    return lax.all_gather(own, "dp", axis_index_groups=outer_groups())


def gather_outer_permuted(own):
    outer = lax.axis_index("dp") // (lax.axis_size("dp") // 4)
    full = jnp.stack([own] * 4)
    for j in (1, 3, 2):
        full = lax.dynamic_update_index_in_dim(
            full, from_dp(own, j, 0), lax.rem(outer + j, 4), 0
        )
    return full


def gather_inner(along):
    return {k: from_dp(along, 0, k) for k in range(1, lax.axis_size("dp") // 4)}


def place_dp(along, others):
    inner = lax.axis_size("dp") // 4
    place = lax.rem(lax.axis_index("dp"), inner)
    full = jnp.stack([along] * inner, axis=1)
    for k, block in others.items():
        full = lax.dynamic_update_index_in_dim(full, block, lax.rem(place + k, inner), 1)
    return full


def scatter_inner(full):
    inner = lax.axis_size("dp") // 4
    place = lax.rem(lax.axis_index("dp"), inner)
    full = full.reshape((4, inner) + full.shape[1:])

    def part(k):
        return lax.dynamic_index_in_dim(full, lax.rem(place + k, inner), 1, False)

    return part(0), {k: from_dp(part(k), 0, -k) for k in range(1, inner)}


def scatter_outer(own, got):
    total = own.astype(f32)
    for block in got.values():
        total = total + block.astype(f32)
    total = total.astype(bf16)
    total = lax.psum_scatter(
        total, "dp", scatter_dimension=0, axis_index_groups=outer_groups(), tiled=True
    )
    return total[0]


def across(own):
    return {m: from_ctx(own, m) for m in range(2, lax.axis_size("ctx"), 2)}


def beside(blocks):
    out = {}
    for m, block in blocks.items():
        out[m] = block
        out[m + 1] = from_ctx(block, 1)
    return out


def place_ctx(blocks, dim=0):
    shape = blocks[0].shape
    place = lax.axis_index("ctx")
    full = jnp.zeros(shape[:dim] + (lax.axis_size("ctx"),) + shape[dim:], blocks[0].dtype)
    for m, block in blocks.items():
        full = lax.dynamic_update_index_in_dim(full, block, place ^ m, dim)
    return full


def chip_sum(part, m):
    return part(m).astype(f32) + from_ctx(part(m + 1), 1).astype(f32)


def far_sums(part):
    return {m: chip_sum(part, m).astype(bf16) for m in range(2, lax.axis_size("ctx"), 2)}


def send_far(sums):
    return {m: from_ctx(block, m) for m, block in sums.items()}


def total_of(near, got):
    for block in got.values():
        near = near + block.astype(f32)
    return near


def scatter_ctx(part):
    got = send_far(far_sums(part))
    return total_of(chip_sum(part, 0), got)


def exchange_ctx(blocks):
    moved = [m for m in range(2, lax.axis_size("ctx"))] + [1]
    return {0: blocks[0], **{m: from_ctx(blocks[m], m) for m in moved}}


def by_distance(blocks):
    place = lax.axis_index("ctx")
    return [
        lax.dynamic_index_in_dim(blocks, place ^ m, 0, False) for m in range(lax.axis_size("ctx"))
    ]


def sum_ctx(x):
    m = 1
    while m < lax.axis_size("ctx"):
        x = x + from_ctx(x, m)
        m *= 2
    return x


def sum_dp(x):
    count = lax.axis_size("dp")
    m = 1
    while m < count:
        x = x + lax.ppermute(x, "dp", [(i ^ m, i) for i in range(count)])
        m *= 2
    return x


def split_cols(a, block):
    count = lax.axis_size("ctx")
    rows, n = a.shape
    a = a.reshape(rows, n // (count * block), count, block)
    return a.transpose(2, 0, 1, 3).reshape(count, rows, n // count)


def join_cols(a, block):
    count, rows, n = a.shape
    a = a.reshape(count, rows, n // block, block)
    return a.transpose(1, 2, 0, 3).reshape(rows, count * n)


def own_cols(a, block):
    count = lax.axis_size("ctx")
    rows, n = a.shape
    a = a.reshape(rows, n // (count * block), count, block)
    a = lax.dynamic_index_in_dim(a, lax.axis_index("ctx"), 2, False)
    return a.reshape(rows, n // count)


def spread_cols(a, block):
    count = lax.axis_size("ctx")
    rows, n = a.shape
    a = a.reshape(rows, n // block, block)
    full = jnp.zeros((rows, n // block, count, block), a.dtype)
    full = lax.dynamic_update_index_in_dim(full, a, lax.axis_index("ctx"), 2)
    return full.reshape(rows, count * n)


def attention_window(total_len):
    reach = -(-(DOC_MOST - 1) // QBLOCK) * QBLOCK
    return min(reach, total_len - QBLOCK), min(reach + QBLOCK, total_len)


def attention_scores(total_len, q_ref, k_ref, col_ref, row_ref):
    back, window = attention_window(total_len)
    first = pl.program_id(1) * QBLOCK
    start = pl.multiple_of(jnp.maximum(first - back, 0), QBLOCK)
    keys = k_ref[pl.ds(start, window), :]
    scores = dot(q_ref[...], keys, NT) * HD ** (-0.5)
    query_place = first + lax.broadcasted_iota(jnp.int32, (QBLOCK, window), 0)
    key_place = start + lax.broadcasted_iota(jnp.int32, (QBLOCK, window), 1)
    key_seg = row_ref[0:1, pl.ds(start, window)]
    allowed = (key_place <= query_place) & (col_ref[:, 0:1] == key_seg)
    return start, window, keys, jnp.where(allowed, scores, -1e30)


def attend_kernel(total_len, q_ref, k_ref, v_ref, col_ref, row_ref, out_ref, log_ref):
    start, window, _, scores = attention_scores(total_len, q_ref, k_ref, col_ref, row_ref)
    peak = jnp.max(scores, axis=1, keepdims=True)
    expo = jnp.exp(scores - peak)
    log_total = peak + jnp.log(jnp.sum(expo, axis=1, keepdims=True))
    shares = jnp.exp(scores - log_total).astype(bf16)
    out_ref[...] = dot(shares, v_ref[pl.ds(start, window), :]).astype(out_ref.dtype)
    log_ref[...] = jnp.broadcast_to(log_total, log_ref.shape)


def attend_back_kernel(
    total_len, q_ref, k_ref, v_ref, col_ref, row_ref, log_ref, grad_ref, dq_ref, dk_ref, dv_ref
):
    @pl.when(pl.program_id(1) == 0)
    def _():
        dk_ref[...] = jnp.zeros_like(dk_ref)
        dv_ref[...] = jnp.zeros_like(dv_ref)

    start, window, keys, scores = attention_scores(total_len, q_ref, k_ref, col_ref, row_ref)
    shares = jnp.exp(scores - log_ref[:, 0:1])
    grad = grad_ref[...]
    grad_shares = dot(grad, v_ref[pl.ds(start, window), :], NT)
    inner = jnp.sum(shares * grad_shares, axis=1, keepdims=True)
    grad_scores = (shares * (grad_shares - inner)).astype(bf16)
    scale = HD ** (-0.5)
    dq_ref[...] = dot(grad_scores, keys) * scale
    span = pl.ds(start, window)
    dk_ref[span, :] += dot(grad_scores, q_ref[...], TN) * scale
    dv_ref[span, :] += dot(shares.astype(bf16), grad, TN)


def attention_specs(total_len, offset):
    tile = pl.BlockSpec((QBLOCK, HD), lambda h, i: (i, h))
    whole = pl.BlockSpec((total_len, HD), lambda h, i: (0, h))
    later = pl.BlockSpec((total_len, HD), lambda h, i: (0, h + offset))
    col = pl.BlockSpec((QBLOCK, 128), lambda h, i: (i, 0))
    row = pl.BlockSpec((8, total_len), lambda h, i: (0, 0))
    return tile, whole, later, col, row


def attention_call(queries, pairs, offset, seg_col, seg_row):
    total_len, width = queries.shape
    tile, whole, later, col, row = attention_specs(total_len, offset)
    return pl.pallas_call(
        functools.partial(attend_kernel, total_len),
        grid=(width // HD, total_len // QBLOCK),
        in_specs=[tile, whole, later, col, row],
        out_specs=[tile, tile],
        out_shape=[
            jax.ShapeDtypeStruct((total_len, width), bf16),
            jax.ShapeDtypeStruct((total_len, width), f32),
        ],
        compiler_params=pltpu.CompilerParams(vmem_limit_bytes=48 * 2**20),
        cost_estimate=pl.CostEstimate(flops=1, bytes_accessed=1, transcendentals=0),
        name="attend",
    )(queries, pairs, pairs, seg_col, seg_row)


def attention_back_call(queries, pairs, offset, seg_col, seg_row, log_total, grad):
    total_len, width = queries.shape
    tile, whole, later, col, row = attention_specs(total_len, offset)
    return pl.pallas_call(
        functools.partial(attend_back_kernel, total_len),
        grid=(width // HD, total_len // QBLOCK),
        in_specs=[tile, whole, later, col, row, tile, tile],
        out_specs=[tile, whole, whole],
        out_shape=[jax.ShapeDtypeStruct((total_len, width), f32)] * 3,
        compiler_params=pltpu.CompilerParams(vmem_limit_bytes=48 * 2**20),
        cost_estimate=pl.CostEstimate(flops=1, bytes_accessed=1, transcendentals=0),
        name="attend_back",
    )(queries, pairs, pairs, seg_col, seg_row, log_total, grad)


def pair_of(col, offset, j, left):
    a = offset + 2 * j
    return jnp.where(left, col[:, a : a + 1], col[:, a + 1 : a + 2])


def state_decay(col, j, left_rows):
    last = col[CHUNK - 1 : CHUNK, :]
    a = 64 + 2 * j
    return jnp.where(left_rows, last[:, a : a + 1], last[:, a + 1 : a + 2])


def scan_kernel(pairs, x_ref, k_ref, r_ref, col_ref, row_ref, skip_ref, y_ref, s_ref, state):
    @pl.when(pl.program_id(0) == 0)
    def _():
        state[...] = jnp.zeros_like(state)

    writes = k_ref[...].astype(bf16)
    reads = r_ref[...].astype(bf16)
    col = col_ref[...]
    row = row_ref[...]
    entering = state[...].astype(bf16)
    s_ref[0] = entering
    products = dot(reads, writes, NT)
    later = lax.broadcasted_iota(jnp.int32, (CHUNK, CHUNK), 0)
    earlier = lax.broadcasted_iota(jnp.int32, (CHUNK, CHUNK), 1)
    mask = (later >= earlier) & (col[:, 127:128] == row[16:17, :])
    left = lax.broadcasted_iota(jnp.int32, (CHUNK, 128), 1) < HEAD_M
    left_rows = lax.broadcasted_iota(jnp.int32, (128, STATE), 0) < HEAD_M
    through = dot(reads, entering, NT)
    for j in range(pairs):
        lanes = slice(128 * j, 128 * j + 128)
        x = x_ref[:, lanes]
        scaled = x * pair_of(col, 32, j, left)
        scaled_low = scaled.astype(bf16)
        outs = []
        for h in (2 * j, 2 * j + 1):
            spread = col[:, h : h + 1] - row[h : h + 1, :]
            mixing = jnp.exp(jnp.where(mask, spread, -1e30)) * products
            outs.append(dot(mixing.astype(bf16), scaled_low))
        y_ref[:, lanes] = (
            jnp.where(left, outs[0], outs[1])
            + pair_of(col, 64, j, left) * through[:, lanes]
            + skip_ref[0:1, lanes] * x
        )
        to_end = (scaled * pair_of(col, 96, j, left)).astype(bf16)
        state[lanes, :] = state_decay(col, j, left_rows) * state[lanes, :] + dot(to_end, writes, TN)


def scan_back_kernel(
    pairs,
    x_ref,
    k_ref,
    r_ref,
    col_ref,
    row_ref,
    skip_ref,
    y_ref,
    s_ref,
    dy_ref,
    sum_ref,
    dx_ref,
    dk_ref,
    dr_ref,
    red_ref,
    tot_ref,
    adjoint,
    keep,
):
    @pl.when(pl.program_id(0) == 0)
    def _():
        adjoint[...] = jnp.zeros_like(adjoint)

    writes = k_ref[...].astype(bf16)
    reads = r_ref[...].astype(bf16)
    col = col_ref[...]
    row = row_ref[...]
    entering = s_ref[0]
    products = dot(writes, reads, NT)
    earlier = lax.broadcasted_iota(jnp.int32, (CHUNK, CHUNK), 0)
    later = lax.broadcasted_iota(jnp.int32, (CHUNK, CHUNK), 1)
    mask = (later >= earlier) & (col[:, 127:128] == row[16:17, :])
    left = lax.broadcasted_iota(jnp.int32, (CHUNK, 128), 1) < HEAD_M
    left_rows = lax.broadcasted_iota(jnp.int32, (128, STATE), 0) < HEAD_M
    incoming = adjoint[...]
    incoming_low = incoming.astype(bf16)
    values = dot(writes, incoming_low, NT)
    grad_products = jnp.zeros((CHUNK, CHUNK), f32)
    grad_writes = jnp.zeros((CHUNK, STATE), f32)
    grad_reads = jnp.zeros((CHUNK, STATE), f32)
    tot_ref[0] = jnp.zeros(tot_ref.shape[1:], f32)
    for j in range(pairs):
        lanes = slice(128 * j, 128 * j + 128)
        x = x_ref[:, lanes]
        step = pair_of(col, 32, j, left)
        scaled = x * step
        scaled_low = scaled.astype(bf16)
        dy = dy_ref[:, lanes]
        dy_low = dy.astype(bf16)
        grads = []
        for side, h in enumerate((2 * j, 2 * j + 1)):
            spread = row[h : h + 1, :] - col[:, h : h + 1]
            decay = jnp.exp(jnp.where(mask, spread, -1e30))
            half = left if side == 0 else jnp.logical_not(left)
            grad_mixing = dot(jnp.where(half, scaled_low, jnp.zeros_like(scaled_low)), dy_low, NT)
            grad_products += grad_mixing * decay
            grads.append(dot((decay * products).astype(bf16), dy_low))
        grad_scaled = jnp.where(left, grads[0], grads[1])
        decay_end = pair_of(col, 96, j, left)
        to_end = (scaled * decay_end).astype(bf16)
        passed = to_end.astype(f32) * values[:, lanes]
        skip = skip_ref[0:1, lanes]
        flow = (
            dy_low.astype(f32) * (y_ref[:, lanes] - skip * x)
            - scaled_low.astype(f32) * grad_scaled
            - passed
        )
        grad_scaled += decay_end * values[:, lanes]
        dx_ref[:, lanes] = (step * grad_scaled + skip * dy).astype(bf16)
        from_start = (pair_of(col, 64, j, left) * dy).astype(bf16)
        grad_reads += dot(from_start, entering[lanes, :])
        grad_writes += dot(to_end, incoming_low[lanes, :])
        pieces = (flow, x * grad_scaled)
        for n, piece in enumerate(pieces):
            high = piece.astype(bf16)
            keep[2 * n, :, lanes] = high
            keep[2 * n + 1, :, lanes] = (piece - high.astype(f32)).astype(bf16)
        tot_ref[0, 1:2, lanes] = jnp.sum(passed, axis=0, keepdims=True)
        tot_ref[0, 2:3, lanes] = jnp.sum(dy * x, axis=0, keepdims=True)
        product = incoming[lanes, :] * entering[lanes, :].astype(f32)
        high = product.astype(bf16)
        low = (product - high.astype(f32)).astype(bf16)
        ones = jnp.ones((8, STATE), bf16)
        tot_ref[0, 0:1, lanes] = (dot(ones, high, NT) + dot(ones, low, NT))[0:1, :]
        adjoint[lanes, :] = state_decay(col, j, left_rows) * incoming[lanes, :] + dot(
            from_start, reads, TN
        )
    grad_products = grad_products.astype(bf16)
    dk_ref[...] = (grad_writes + dot(grad_products, reads)).astype(bf16)
    dr_ref[...] = (grad_reads + dot(grad_products, writes, TN)).astype(bf16)
    sums = sum_ref[...]
    red_ref[...] = (
        dot(keep[0], sums[0]) + dot(keep[1], sums[0]) + dot(keep[2], sums[1]) + dot(keep[3], sums[1])
    )


def scan_call(own, shared, col, row, skip, width):
    total_len = own.shape[0]
    count = total_len // CHUNK
    return pl.pallas_call(
        functools.partial(scan_kernel, width // 128),
        grid=(count,),
        in_specs=[
            pl.BlockSpec((CHUNK, width), lambda i: (i, 0)),
            pl.BlockSpec((CHUNK, STATE), lambda i: (i, 0)),
            pl.BlockSpec((CHUNK, STATE), lambda i: (i, 1)),
            pl.BlockSpec((CHUNK, 128), lambda i: (i, 0)),
            pl.BlockSpec((24, CHUNK), lambda i: (0, i)),
            pl.BlockSpec((8, width), lambda i: (0, 0)),
        ],
        out_specs=[
            pl.BlockSpec((CHUNK, width), lambda i: (i, 0)),
            pl.BlockSpec((1, width, STATE), lambda i: (i, 0, 0)),
        ],
        out_shape=[
            jax.ShapeDtypeStruct((total_len, width), f32),
            jax.ShapeDtypeStruct((count, width, STATE), bf16),
        ],
        scratch_shapes=[pltpu.VMEM((width, STATE), f32)],
        compiler_params=pltpu.CompilerParams(vmem_limit_bytes=48 * 2**20),
        cost_estimate=pl.CostEstimate(flops=1, bytes_accessed=1, transcendentals=0),
        name="state_scan",
    )(own, shared, shared, col, row, skip)


def scan_back_call(own, shared, col, row, skip, scanned, states, grad, width):
    total_len = own.shape[0]
    count = total_len // CHUNK
    owner = jnp.arange(width)[:, None] // HEAD_M
    lane = jnp.arange(128)[None, :]
    sums = jnp.stack([owner == lane, owner + 32 == lane]).astype(bf16)

    def back(i):
        return count - 1 - i

    return pl.pallas_call(
        functools.partial(scan_back_kernel, width // 128),
        grid=(count,),
        in_specs=[
            pl.BlockSpec((CHUNK, width), lambda i: (back(i), 0)),
            pl.BlockSpec((CHUNK, STATE), lambda i: (back(i), 0)),
            pl.BlockSpec((CHUNK, STATE), lambda i: (back(i), 1)),
            pl.BlockSpec((CHUNK, 128), lambda i: (back(i), 0)),
            pl.BlockSpec((24, CHUNK), lambda i: (0, back(i))),
            pl.BlockSpec((8, width), lambda i: (0, 0)),
            pl.BlockSpec((CHUNK, width), lambda i: (back(i), 0)),
            pl.BlockSpec((1, width, STATE), lambda i: (back(i), 0, 0)),
            pl.BlockSpec((CHUNK, width), lambda i: (back(i), 0)),
            pl.BlockSpec((2, width, 128), lambda i: (0, 0, 0)),
        ],
        out_specs=[
            pl.BlockSpec((CHUNK, width), lambda i: (back(i), 0)),
            pl.BlockSpec((CHUNK, STATE), lambda i: (back(i), 0)),
            pl.BlockSpec((CHUNK, STATE), lambda i: (back(i), 0)),
            pl.BlockSpec((CHUNK, 128), lambda i: (back(i), 0)),
            pl.BlockSpec((1, 8, width), lambda i: (back(i), 0, 0)),
        ],
        out_shape=[
            jax.ShapeDtypeStruct((total_len, width), bf16),
            jax.ShapeDtypeStruct((total_len, STATE), bf16),
            jax.ShapeDtypeStruct((total_len, STATE), bf16),
            jax.ShapeDtypeStruct((total_len, 128), f32),
            jax.ShapeDtypeStruct((count, 8, width), f32),
        ],
        scratch_shapes=[pltpu.VMEM((width, STATE), f32), pltpu.VMEM((4, CHUNK, width), bf16)],
        compiler_params=pltpu.CompilerParams(vmem_limit_bytes=48 * 2**20),
        cost_estimate=pl.CostEstimate(flops=1, bytes_accessed=1, transcendentals=0),
        name="state_scan_back",
    )(own, shared, shared, col, row, skip, scanned, states, grad, sums)


def feed_kernel(per_block, *refs):
    own_ref, side_ref, cot_ref, gate_ref, up_ref, down_ref = refs[:6]
    back_ref, mid_ref, hidden_ref, grad_gate_ref, grad_up_ref = refs[-5:]
    first = pl.program_id(0) < per_block
    mid = jnp.where(first, own_ref[...], side_ref[...])
    mid_ref[...] = mid
    gate = dot(mid, gate_ref[...])
    upper = dot(mid, up_ref[...])
    grad_hidden = dot(cot_ref[...], down_ref[...], NT)
    sigma = jax.nn.sigmoid(gate)
    gate_half = gate * sigma
    hidden_ref[...] = (gate_half * upper).astype(bf16)
    grad_gate = (grad_hidden * upper * (sigma * (1.0 + gate * (1.0 - sigma)))).astype(bf16)
    grad_up = (grad_hidden * gate_half).astype(bf16)
    grad_gate_ref[...] = grad_gate
    grad_up_ref[...] = grad_up
    back_ref[...] = (dot(grad_gate, gate_ref[...], NT) + dot(grad_up, up_ref[...], NT)).astype(bf16)


def feed_call(e, own, side, cot, w_gate, w_up, w_down, kept):
    length = own.shape[0]
    total_len = cot.shape[0]
    columns = w_gate.shape[1]
    tile = min(256, length)
    per_block = length // tile
    tiles = 2 * per_block

    def held(shape):
        return pl.BlockSpec(shape, lambda i: (0, 0), pipeline_mode=pl.Buffered(1))

    def spread(n):
        return pl.BlockSpec((tile, n), lambda i: (i + e * tiles, 0))

    kept_shapes = [(total_len, D)] + [(total_len, columns)] * 3
    return pl.pallas_call(
        functools.partial(feed_kernel, per_block),
        grid=(tiles,),
        in_specs=[
            pl.BlockSpec((tile, D), lambda i: (jnp.minimum(i, per_block - 1), 0)),
            pl.BlockSpec((tile, D), lambda i: (jnp.maximum(i - per_block, 0), 0)),
            spread(D),
            held(w_gate.shape),
            held(w_up.shape),
            held(w_down.shape),
        ]
        + [pl.BlockSpec(memory_space=pl.ANY)] * len(kept),
        out_specs=[
            pl.BlockSpec((tile, D), lambda i: (i, 0)),
            spread(D),
            spread(columns),
            spread(columns),
            spread(columns),
        ],
        out_shape=[jax.ShapeDtypeStruct((2 * length, D), bf16)]
        + [jax.ShapeDtypeStruct(shape, bf16) for shape in kept_shapes],
        input_output_aliases={6 + n: 1 + n for n in range(len(kept))},
        compiler_params=pltpu.CompilerParams(vmem_limit_bytes=56 * 2**20),
        cost_estimate=pl.CostEstimate(flops=1, bytes_accessed=1, transcendentals=0),
        name="feed_forward",
    )(own, side, cot, w_gate, w_up, w_down, *kept)


def token_sum_kernel(a_ref, b_ref, out_ref):
    out_ref[...] = dot(a_ref[...], b_ref[...], TN).astype(bf16)


def token_sum(a, b):
    total_len, rows = a.shape
    columns = b.shape[1]
    tile = math.gcd(rows, 512)
    return pl.pallas_call(
        token_sum_kernel,
        grid=(rows // tile,),
        in_specs=[
            pl.BlockSpec((total_len, tile), lambda i: (0, i)),
            pl.BlockSpec((total_len, columns), lambda i: (0, 0), pipeline_mode=pl.Buffered(1)),
        ],
        out_specs=pl.BlockSpec((tile, columns), lambda i: (i, 0)),
        out_shape=jax.ShapeDtypeStruct((rows, columns), bf16),
        compiler_params=pltpu.CompilerParams(vmem_limit_bytes=56 * 2**20),
        cost_estimate=pl.CostEstimate(flops=1, bytes_accessed=1, transcendentals=0),
        name="token_sum",
    )(a, b)


def normed_kernel(chip_ref, *refs):
    grads, weights, out_ref = refs[:3], refs[3:6], refs[6]
    total = dot(grads[0][...], weights[0][...], NT)
    total += dot(grads[1][...], weights[1][...], NT)
    total += dot(grads[2][...], weights[2][...], NT)
    out_ref[...] = total.astype(bf16)


def normed_call(chip, rows, grads, weights):
    tile = 256
    tiles = rows // tile

    def picked(grad):
        return pl.BlockSpec((tile, grad.shape[1]), lambda i, chip: (chip[0] * tiles + i, 0))

    def held(weight):
        return pl.BlockSpec(weight.shape, lambda i, chip: (0, 0), pipeline_mode=pl.Buffered(1))

    return pl.pallas_call(
        normed_kernel,
        grid_spec=pltpu.PrefetchScalarGridSpec(
            num_scalar_prefetch=1,
            grid=(tiles,),
            in_specs=[picked(grad) for grad in grads] + [held(weight) for weight in weights],
            out_specs=pl.BlockSpec((tile, D), lambda i, chip: (i, 0)),
        ),
        out_shape=jax.ShapeDtypeStruct((rows, D), bf16),
        compiler_params=pltpu.CompilerParams(vmem_limit_bytes=48 * 2**20),
        cost_estimate=pl.CostEstimate(flops=1, bytes_accessed=1, transcendentals=0),
        name="grad_normed",
    )(chip, *grads, *weights)


def place_rows_kernel(place_ref, *refs):
    for m, block_ref in enumerate(refs[:-1]):

        @pl.when(pl.program_id(0) == m)
        def _():
            refs[-1][...] = block_ref[...]


def place_rows(place, blocks):
    count = len(blocks)
    rows, columns = blocks[0].shape
    tile = min(256, rows)
    tiles = rows // tile

    def source(k):
        def at(m, i, place):
            return jnp.where(m == k, i, jnp.where(m < k, 0, tiles - 1)), 0

        return pl.BlockSpec((tile, columns), at)

    return pl.pallas_call(
        place_rows_kernel,
        grid_spec=pltpu.PrefetchScalarGridSpec(
            num_scalar_prefetch=1,
            grid=(count, tiles),
            in_specs=[source(k) for k in range(count)],
            out_specs=pl.BlockSpec(
                (tile, columns), lambda m, i, place: ((place[0] ^ m) * tiles + i, 0)
            ),
        ),
        out_shape=jax.ShapeDtypeStruct((count * rows, columns), blocks[0].dtype),
        compiler_params=pltpu.CompilerParams(vmem_limit_bytes=48 * 2**20),
        cost_estimate=pl.CostEstimate(flops=1, bytes_accessed=1, transcendentals=0),
        name="place_rows",
    )(place, *[blocks[m] for m in range(count)])


def pack_in_kernel(count, place_ref, w_ref, own_ref, shared_ref):
    place = place_ref[0]
    width = DSSM // count
    first_z = width + QH * HD // count
    query = 2 * DSSM + 2 * STATE + HEADS_M
    for c in range(count):
        m = c ^ place
        for n in range(DSSM // (count * HD)):
            at = (n * count + c) * HD
            to = slice(n * HD, (n + 1) * HD)
            own_ref[m, :, to] = w_ref[:, DSSM + at : DSSM + at + HD].astype(bf16)
            to = slice(first_z + n * HD, first_z + (n + 1) * HD)
            own_ref[m, :, to] = w_ref[:, at : at + HD].astype(bf16)
        for n in range(QH // count):
            at = query + (n * count + c) * HD
            to = slice(width + n * HD, width + (n + 1) * HD)
            own_ref[m, :, to] = w_ref[:, at : at + HD].astype(bf16)
    shared_ref[:, : 2 * STATE] = w_ref[:, 2 * DSSM : 2 * DSSM + 2 * STATE].astype(bf16)
    shared_ref[:, 2 * STATE : SHARED - 128] = w_ref[:, query + QH * HD :].astype(bf16)
    steps = w_ref[:, query - HEADS_M : query - HEADS_M + 128]
    lane = lax.broadcasted_iota(jnp.int32, steps.shape, 1)
    shared_ref[:, SHARED - 128 :] = jnp.where(lane < HEADS_M, steps, 0.0).astype(bf16)


def pack_in(place, weight):
    rows = weight.shape[0]
    count = lax.axis_size("ctx")
    own_width = (2 * DSSM + QH * HD) // count
    return pl.pallas_call(
        functools.partial(pack_in_kernel, count),
        in_specs=[pl.BlockSpec(memory_space=pltpu.SMEM), pl.BlockSpec(memory_space=pltpu.VMEM)],
        out_specs=[pl.BlockSpec(memory_space=pltpu.VMEM)] * 2,
        out_shape=[
            jax.ShapeDtypeStruct((count, rows, own_width), bf16),
            jax.ShapeDtypeStruct((rows, SHARED), bf16),
        ],
        compiler_params=pltpu.CompilerParams(vmem_limit_bytes=48 * 2**20),
        name="pack_in",
    )(place, weight)


def pack_gate_up_kernel(count, place_ref, w_ref, out_ref):
    place = place_ref[0]
    blocks = FF // (count * HD)
    for c in range(count):
        m = c ^ place
        for n in range(2 * blocks):
            at = (n * count + c) * HD
            out_ref[m, :, n * HD : (n + 1) * HD] = w_ref[:, at : at + HD].astype(bf16)


def pack_gate_up(place, weight):
    rows = weight.shape[0]
    count = lax.axis_size("ctx")
    return pl.pallas_call(
        functools.partial(pack_gate_up_kernel, count),
        in_specs=[pl.BlockSpec(memory_space=pltpu.SMEM), pl.BlockSpec(memory_space=pltpu.VMEM)],
        out_specs=pl.BlockSpec(memory_space=pltpu.VMEM),
        out_shape=jax.ShapeDtypeStruct((count, rows, 2 * FF // count), bf16),
        compiler_params=pltpu.CompilerParams(vmem_limit_bytes=48 * 2**20),
        name="pack_gate_up",
    )(place, weight)


def update_kernel(count, spans, rate, place_ref, g_ref, *refs):
    tail_ref = refs[0] if len(refs) == 7 else None
    w_ref, first_ref, second_ref, new_w_ref, new_first_ref, new_second_ref = refs[-6:]
    place = place_ref[0]

    def update(cols, grad):
        new = adam_step(w_ref[:, cols], grad, first_ref[:, cols], second_ref[:, cols], rate)
        new_w_ref[:, cols], new_first_ref[:, cols], new_second_ref[:, cols] = new

    for first, columns, at in spans:
        for n in range(columns // (count * HD)):
            for c in range(count):
                start = first + (n * count + c) * HD
                grad = g_ref[c ^ place, :, at : at + HD].astype(f32)
                update(slice(start, start + HD), grad)
            at += HD
    if tail_ref is not None:
        update(slice(2 * DSSM, w_ref.shape[1]), tail_ref[...])


def update_dealt(place, got, tail, weight, first, second, spans, rate):
    rows, columns = weight.shape
    count = lax.axis_size("ctx")
    got = jnp.stack([got[m] for m in range(count)])
    block = 16

    def flat(n):
        return pl.BlockSpec((block, n), lambda i: (i, 0))

    tails = [] if tail is None else [tail]
    return pl.pallas_call(
        functools.partial(update_kernel, count, spans, rate),
        grid=(rows // block,),
        in_specs=[
            pl.BlockSpec(memory_space=pltpu.SMEM),
            pl.BlockSpec((count, block, got.shape[2]), lambda i: (0, i, 0)),
        ]
        + [flat(t.shape[1]) for t in tails]
        + [flat(columns)] * 3,
        out_specs=[flat(columns)] * 3,
        out_shape=[jax.ShapeDtypeStruct((rows, columns), f32)] * 3,
        compiler_params=pltpu.CompilerParams(vmem_limit_bytes=48 * 2**20),
        cost_estimate=pl.CostEstimate(flops=1, bytes_accessed=1, transcendentals=0),
        name="update",
    )(place, got, *tails, weight, first, second)


def rms_scale(values):
    return lax.rsqrt(jnp.mean(values * values, axis=-1, keepdims=True) + norm_eps)


def norm_back(grad_unit, unit, scale):
    return scale * (grad_unit - unit * jnp.mean(grad_unit * unit, axis=-1, keepdims=True))


def silu_slope(values):
    sigma = jax.nn.sigmoid(values)
    return sigma * (1.0 + values * (1.0 - sigma))


def split_small(small):
    widths = [D, D, DSSM, HEADS_M, HEADS_M, HEADS_M]
    pieces = []
    start = 0
    for count in widths:
        pieces.append(small[start : start + count])
        start += count
    return pieces


def adam_step(weight, grad, first, second, rate):
    first = beta_one * first + (1.0 - beta_one) * grad
    second = beta_two * second + (1.0 - beta_two) * grad * grad
    fixed_first = first / (1.0 - beta_one**STEP)
    fixed_second = second / (1.0 - beta_two**STEP)
    weight = weight - rate * (
        fixed_first / (jnp.sqrt(fixed_second) + adam_eps) + weight_decay * weight
    )
    return (weight, first, second)


def pad_lanes(a, width):
    return jnp.pad(a, ((0, 0), (0, width - a.shape[1])))


def shards(
    block_input,
    segment_ids,
    cotangent,
    in_weight,
    out_weight,
    gate_up_weight,
    down_weight,
    in_first,
    out_first,
    gate_up_first,
    down_first,
    in_second,
    out_second,
    gate_up_second,
    down_second,
    small_params,
    small_first,
    small_second,
):
    peers = lax.axis_size("ctx")
    groups = lax.axis_size("dp")
    place = lax.axis_index("ctx")
    length = block_input.shape[0] * block_input.shape[1]
    total_len = length * peers
    row_block = out_weight.shape[0]
    in_rows = in_weight.shape[0]
    strided = row_block == HD
    width = DSSM // peers
    heads = HEADS_M // peers
    query_heads = QH // peers
    query_width = query_heads * HD
    own_width = 2 * width + query_width
    ff_width = FF // peers
    pair_block = 2 * HEAD_M if strided else width
    query_block = HD if strided else query_width
    head_block = 2 if strided else heads
    gain_in, gain_mid, gain_mix, step_bias, decay_log, skip = split_small(small_params)

    place_arg = place.astype(jnp.int32).reshape(1)
    base = 2 * DSSM + 2 * STATE + HEADS_M
    query_end = base + QH * HD
    if strided:
        own_low, shared_low = pack_in(place_arg, in_weight)
        gu_low = pack_gate_up(place_arg, gate_up_weight)
        own_low = [own_low[m] for m in range(peers)]
        gu_low = [gu_low[m] for m in range(peers)]
    else:
        in_low = in_weight.astype(bf16)
        shared_low = jnp.concatenate(
            [
                in_low[:, 2 * DSSM : 2 * DSSM + 2 * STATE],
                in_low[:, query_end:],
                in_low[:, 2 * DSSM + 2 * STATE : base],
                jnp.zeros((in_rows, 128 - HEADS_M), bf16),
            ],
            axis=1,
        )
        own_low = jnp.concatenate(
            [
                split_cols(in_low[:, DSSM : 2 * DSSM], pair_block),
                split_cols(in_low[:, base:query_end], query_block),
                split_cols(in_low[:, :DSSM], pair_block),
            ],
            axis=2,
        )
        own_low = by_distance(own_low)
        gu_low = gate_up_weight.astype(bf16)
        gu_low = jnp.concatenate(
            [split_cols(gu_low[:, :FF], row_block), split_cols(gu_low[:, FF:], row_block)], axis=2
        )
        gu_low = by_distance(gu_low)
    own_rows = place_ctx(exchange_ctx(own_low)).reshape(peers * in_rows, own_width)
    x_own = block_input.reshape(length, D)
    seg_own = segment_ids.reshape(length)
    own_rows, x_own, shared_low, gu_low, seg_own = fence(
        own_rows, x_own, shared_low, gu_low, seg_own
    )

    sq_width = width + query_width
    s_along = gather_outer(own_rows[:, :width])
    qz_along = gather_outer(own_rows[:, width:])
    seg_far = across(seg_own)
    segments = place_ctx(beside({0: seg_own, **seg_far})).reshape(total_len)
    shared_along = gather_outer_permuted(shared_low)
    out_low = out_weight.astype(bf16)
    down_low = down_weight.astype(bf16)
    x_far = across(x_own)
    shared_rows = place_dp(shared_along, gather_inner(shared_along))
    shared_rows = shared_rows.reshape((groups,) + shared_low.shape)
    down_inner = gather_inner(down_low)
    cot_own = cotangent.reshape(length, D)
    own_bias = own_cols(step_bias[None, :], head_block)
    own_decay = jnp.exp(own_cols(decay_log[None, :], head_block))
    own_skip = jnp.repeat(own_cols(skip[None, :], head_block), HEAD_M, axis=1)
    own_skip = jnp.broadcast_to(own_skip, (8, width))
    own_gain_mix = own_cols(gain_mix[None, :], pair_block)
    chunks = total_len // CHUNK
    seg_chunks = segments.reshape(chunks, CHUNK)
    seg_last = seg_chunks[:, -1:]
    seg_before = jnp.concatenate([jnp.full((1, 1), -1, seg_last.dtype), seg_last[:-1]], axis=0)
    entering = (seg_chunks == seg_before).astype(f32)[:, :, None]
    leaving = jnp.where(seg_chunks == seg_last, 0.0, -1e30)[:, :, None]
    seg_float = segments.astype(f32)
    seg_col = jnp.broadcast_to(seg_float[:, None], (total_len, 128))
    seg_row = jnp.broadcast_to(seg_float[None, :], (8, total_len))
    (x_own, x_far, shared_rows, gu_low, cot_own, s_along, out_low, down_low, down_inner) = fence(
        x_own, x_far, shared_rows, gu_low, cot_own, s_along, out_low, down_low, down_inner
    )
    own_bias, own_decay, own_skip, own_gain_mix, entering, leaving, seg_col, seg_row, x_far = fence(
        own_bias, own_decay, own_skip, own_gain_mix, entering, leaving, seg_col, seg_row, x_far
    )

    shared_far = across(shared_rows)
    if strided:
        out_along = gather_outer(out_low)
    s_others = gather_inner(s_along)
    tokens = place_rows(place_arg, beside({0: x_own, **x_far}))
    scale_in = rms_scale(tokens.astype(f32))
    normed = (tokens.astype(f32) * scale_in * gain_in).astype(bf16)
    normed, shared_rows, shared_far, s_along, s_others, qz_along, cot_own, gu_low = fence(
        normed, shared_rows, shared_far, s_along, s_others, qz_along, cot_own, gu_low
    )

    qz_others = gather_inner(qz_along)
    w_shared = place_ctx(beside({0: shared_rows, **shared_far}), 1).reshape(D, SHARED)
    pairs = dot(normed, w_shared[:, 2 * STATE : SHARED - 128]).astype(bf16)
    writes_reads = dot(normed, w_shared[:, : 2 * STATE])
    raw_all = dot(normed, w_shared[:, SHARED - 128 :])
    if not strided:
        out_along = {}
    normed, pairs, writes_reads, raw_all, cot_own, gu_low = fence(
        normed, pairs, writes_reads, raw_all, cot_own, gu_low
    )

    gu_rows = place_ctx(exchange_ctx(gu_low)).reshape(peers * in_rows, 2 * ff_width)
    gate_along = gather_outer(gu_rows[:, :ff_width])
    up_along = gather_outer(gu_rows[:, ff_width:])
    cot_far = across(cot_own)
    w_streams = place_dp(s_along, s_others).reshape(D, width)
    streams = dot(normed, w_streams)
    streams, out_along = fence(streams, out_along)
    out_others = gather_inner(out_along) if strided else {}
    raw_step = own_cols(raw_all[:, :HEADS_M], head_block)
    offset = KVH
    if query_heads < KVH:
        offset = query_heads
        own_kv = (place * query_heads * KVH // QH) * HD
        pairs = jnp.concatenate(
            [
                lax.dynamic_slice_in_dim(pairs, own_kv, query_width, 1),
                lax.dynamic_slice_in_dim(pairs, KVH * HD + own_kv, query_width, 1),
            ],
            axis=1,
        )
    step = jax.nn.softplus(raw_step + own_bias)
    rates = (-own_decay * step).reshape(chunks, CHUNK, heads)
    order = jnp.arange(CHUNK)
    lower = (order[:, None] >= order[None, :]).astype(f32)
    running = jnp.einsum("ts,csh->cth", lower, rates, precision=lax.Precision.HIGHEST)
    from_start = jnp.exp(running) * entering
    to_end = jnp.exp(jnp.where(leaving == 0.0, running[:, -1:, :] - running, -1e30))
    running = running.reshape(total_len, heads)
    col = jnp.concatenate(
        [
            pad_lanes(running, 32),
            pad_lanes(step, 32),
            pad_lanes(from_start.reshape(total_len, heads), 32),
            pad_lanes(to_end.reshape(total_len, heads), 31),
            seg_col[:, :1],
        ],
        axis=1,
    )
    row = jnp.concatenate([jnp.pad(running.T, ((0, 16 - heads), (0, 0))), seg_row], axis=0)

    scanned, states = scan_call(streams, writes_reads, col, row, own_skip, width)
    normed, scanned, qz_along, qz_others, out_along, out_others, gate_along, cot_own, cot_far = fence(
        normed, scanned, qz_along, qz_others, out_along, out_others, gate_along, cot_own, cot_far
    )

    gate_others = gather_inner(gate_along)
    inner_place = lax.rem(lax.axis_index("dp"), groups // 4)
    down_pair = jnp.stack([down_low] * (groups // 4))
    for k, block in down_inner.items():
        at = lax.rem(inner_place + k, groups // 4)
        down_pair = lax.dynamic_update_index_in_dim(down_pair, block, at, 0)
    w_down = gather_outer(down_pair).reshape(ff_width, D)
    cot = jnp.concatenate(
        [block for _, block in sorted(beside({0: cot_own, **cot_far}).items())], axis=0
    )
    w_qz = place_dp(qz_along, qz_others).reshape(D, sq_width)
    queries = dot(normed, w_qz[:, :query_width]).astype(bf16)
    gate_z = dot(normed, w_qz[:, query_width:])
    attended, log_total = attention_call(queries, pairs, offset, seg_col, seg_row)
    gate_act = jax.nn.silu(gate_z)
    gated = scanned * gate_act
    square = sum_ctx(jnp.sum(gated * gated, axis=-1))
    scale_mix = lax.rsqrt(square / DSSM + norm_eps)[:, None]
    unit_mix = gated * scale_mix
    joined = jnp.concatenate([(unit_mix * own_gain_mix).astype(bf16), attended], axis=1)
    joined, gate_along, gate_others, up_along = fence(joined, gate_along, gate_others, up_along)
    if strided:
        w_out = place_dp(out_along, out_others).reshape(sq_width, D)
    else:
        whole_out = lax.all_gather(out_low, ("dp", "ctx"), axis=0, tiled=True)
        w_out = jnp.concatenate(
            [
                lax.dynamic_slice_in_dim(whole_out, place * width, width, 0),
                lax.dynamic_slice_in_dim(whole_out, DSSM + place * query_width, query_width, 0),
            ],
            axis=0,
        )

    chips = list(range(peers // 2))
    parity = place % 2

    def chip_rows(full, e):
        start = ((place // 2) ^ e) * 2 * length
        return lax.dynamic_slice_in_dim(full, start, 2 * length, 0)

    def core_part(parts):
        return lambda m: lax.dynamic_index_in_dim(parts[m // 2], (m % 2) ^ parity, 0, False)

    def mixed_rows(e):
        return dot(chip_rows(joined, e), w_out).astype(bf16).reshape(2, length, D)

    sums = far_sums(core_part({e: mixed_rows(e) for e in chips[1:]}))
    sums, joined, gate_along, gate_others, up_along = fence(
        sums, joined, gate_along, gate_others, up_along
    )
    up_others = gather_inner(up_along)
    w_gate = place_dp(gate_along, gate_others).reshape(D, ff_width)
    got = send_far(sums)
    near = chip_sum(core_part({0: mixed_rows(0)}), 0)
    got, near, up_others, w_gate = fence(got, near, up_others, w_gate)

    middle = x_own.astype(f32) + total_of(near, got)
    scale_mid = rms_scale(middle)
    unit_mid = middle * scale_mid
    mid_own = (unit_mid * gain_mid).astype(bf16)
    w_up = place_dp(up_along, up_others).reshape(D, ff_width)
    def feed_forward(e, own, side, kept):
        back, *kept = feed_call(e, own, side, cot, w_gate, w_up, w_down, kept)
        return back.reshape(2, length, D), kept

    far = across(mid_own)
    near_back, kept = feed_forward(0, mid_own, from_ctx(mid_own, 1), [])
    far, near_back, kept = fence(far, near_back, kept)
    far = beside(far)
    far_back = {}
    for e in chips[1:]:
        far_back[e], kept = feed_forward(e, far[2 * e], far[2 * e + 1], kept)
    sums = far_sums(lambda m: far_back[m // 2][m % 2])
    sums, near_back, kept = fence(sums, near_back, kept)
    normed_mid, hidden, grad_gate, grad_up = kept
    got = send_far(sums)
    near = chip_sum(lambda m: near_back[m], 0)
    grad_gate = token_sum(normed_mid, grad_gate)
    grad_down = token_sum(hidden, cot)
    got, near, grad_gate, grad_down, normed_mid, grad_up = fence(
        got, near, grad_gate, grad_down, normed_mid, grad_up
    )

    gate_parts = scatter_inner(grad_gate.reshape(groups, -1, ff_width))
    sum_down = lax.psum_scatter(
        grad_down.reshape(4, groups // 4, row_block, D),
        "dp",
        scatter_dimension=0,
        axis_index_groups=outer_groups(),
        tiled=True,
    )
    grad_normed_mid = total_of(near, got)
    grad_middle = cot_own.astype(f32) + norm_back(grad_normed_mid * gain_mid, unit_mid, scale_mid)
    grad_middle_low = grad_middle.astype(bf16)
    grad_middle_low, hidden, normed_mid, grad_up = fence(
        grad_middle_low, hidden, normed_mid, grad_up
    )

    far = across(grad_middle_low)
    beside_own = beside({0: grad_middle_low})
    result_part = dot(hidden, w_down).astype(bf16).reshape(peers, length, D)
    grad_up = token_sum(normed_mid, grad_up)
    far, beside_own, result_part, gate_parts, grad_up = fence(
        far, beside_own, result_part, gate_parts, grad_up
    )

    grad_mixed = place_rows(place_arg, {**beside_own, **beside(far)})
    sum_gate = scatter_outer(*gate_parts)
    up_parts = scatter_inner(grad_up.reshape(groups, -1, ff_width))
    grad_gain_mid = jnp.sum(grad_normed_mid * unit_mid, axis=0)
    sums = far_sums(lambda m: result_part[m])
    result_near = chip_sum(lambda m: result_part[m], 0)
    grad_joined = dot(grad_mixed, w_out, NT)
    if strided:
        grad_out = token_sum(joined, grad_mixed)
        out_parts = scatter_inner(grad_out.reshape(groups, row_block, D))
    else:
        grad_out = dot(joined, grad_mixed, TN)
        out_parts = ()
        spread = jnp.zeros((DSSM + QH * HD, D), f32)
        spread = lax.dynamic_update_slice_in_dim(spread, grad_out[:width], place * width, 0)
        spread = lax.dynamic_update_slice_in_dim(
            spread, grad_out[width:], DSSM + place * query_width, 0
        )
        sum_out = lax.psum_scatter(spread, ("dp", "ctx"), scatter_dimension=0, tiled=True)
    grad_attended = grad_joined[:, width:].astype(bf16)
    grad_mix_part = grad_joined[:, :width]
    grad_unit = grad_mix_part * own_gain_mix
    inner = sum_ctx(jnp.sum(grad_unit * unit_mix, axis=-1))[:, None] / DSSM
    grad_queries, grad_keys, grad_values = attention_back_call(
        queries, pairs, offset, seg_col, seg_row, log_total, grad_attended
    )
    grad_queries, inner, up_parts, out_parts, sums = fence(
        grad_queries, inner, up_parts, out_parts, sums
    )

    result_got = send_far(sums)
    inner_count = groups // 4
    down_own = lax.dynamic_index_in_dim(sum_down[0], inner_place, 0, False)
    down_got = {
        k: from_dp(
            lax.dynamic_index_in_dim(
                sum_down[0], lax.rem(inner_place + k, inner_count), 0, False
            ),
            0,
            -k,
        )
        for k in range(1, inner_count)
    }
    sum_down = total_of(down_own.astype(f32), down_got)
    sum_up = scatter_outer(*up_parts)
    if strided:
        sum_out = scatter_outer(*out_parts).astype(f32)
    grad_gain_mix = jnp.sum(grad_mix_part * unit_mix, axis=0)
    grad_gated = scale_mix * (grad_unit - unit_mix * inner)
    grad_scan = grad_gated * gate_act
    grad_z = grad_gated * scanned * silu_slope(gate_z)
    grad_qz = jnp.concatenate([grad_queries.astype(bf16), grad_z.astype(bf16)], axis=1)
    grad_in_qz = token_sum(normed, grad_qz)
    grad_in_qz, grad_scan = fence(grad_in_qz, grad_scan)

    qz_parts = scatter_inner(grad_in_qz.reshape(groups, -1, sq_width))
    grad_streams, grad_writes, grad_reads, reduced, totals = scan_back_call(
        streams, writes_reads, col, row, own_skip, scanned, states, grad_scan, width
    )
    grad_streams, grad_writes, grad_reads, reduced, totals, qz_parts, result_got = fence(
        grad_streams, grad_writes, grad_reads, reduced, totals, qz_parts, result_got
    )

    grad_in_streams = token_sum(normed, grad_streams)
    sum_qz = scatter_outer(*qz_parts)
    totals = totals.reshape(chunks, 8, heads, HEAD_M).sum(axis=3)
    last = from_start[:, -1, :] * totals[:, 0, :] + totals[:, 1, :]
    flow = reduced[:, :heads].reshape(chunks, CHUNK, heads)
    grad_rate = jnp.einsum("ts,cth->csh", lower, flow, precision=lax.Precision.HIGHEST)
    grad_rate = (grad_rate + last[:, None, :]).reshape(total_len, heads)
    grad_step = reduced[:, 32 : 32 + heads] - own_decay * grad_rate
    grad_raw = grad_step * jax.nn.sigmoid(raw_step + own_bias)
    if query_heads < KVH:
        blank = jnp.zeros((total_len, KVH * HD), f32)
        grad_keys = lax.dynamic_update_slice_in_dim(blank, grad_keys, own_kv, 1)
        grad_values = lax.dynamic_update_slice_in_dim(blank, grad_values, own_kv, 1)
    grad_shared = jnp.concatenate(
        [
            grad_writes,
            grad_reads,
            grad_keys.astype(bf16),
            grad_values.astype(bf16),
            pad_lanes(spread_cols(grad_raw.astype(bf16), head_block), 128),
        ],
        axis=1,
    )
    grad_in_streams, grad_shared, normed, grad_raw, grad_rate, totals, sum_gate, sum_up = fence(
        grad_in_streams, grad_shared, normed, grad_raw, grad_rate, totals, sum_gate, sum_up
    )

    def normed_rows(e):
        chip = ((place // 2) ^ e).astype(jnp.int32).reshape(1)
        grads = grad_streams, grad_qz, grad_shared
        part = normed_call(chip, 2 * length, grads, (w_streams, w_qz, w_shared))
        return part.reshape(2, length, D)

    streams_parts = scatter_inner(grad_in_streams.reshape(groups, -1, width))
    grad_in_shared = token_sum(normed, grad_shared)
    far_rows = {e: normed_rows(e) for e in chips[1:]}
    streams_parts, grad_in_shared, far_rows, sum_gate, sum_up, sum_out, sum_down, result_got = fence(
        streams_parts, grad_in_shared, far_rows, sum_gate, sum_up, sum_out, sum_down, result_got
    )

    sum_streams = scatter_outer(*streams_parts)
    shared_part = grad_in_shared.reshape(groups, peers, in_rows, SHARED)

    def shared_of(m):
        return lax.dynamic_index_in_dim(shared_part, place ^ m, 1, False)

    shared_sums = far_sums(shared_of)
    sums = far_sums(core_part(far_rows))
    shared_sums, sums, shared_part, grad_shared = fence(shared_sums, sums, shared_part, grad_shared)

    got_shared = send_far(shared_sums)
    shared_near = chip_sum(shared_of, 0)
    near_rows = normed_rows(0)
    got_shared, shared_near, near_rows, sums = fence(got_shared, shared_near, near_rows, sums)

    got = send_far(sums)
    sum_shared = total_of(shared_near, got_shared).astype(bf16)
    sum_shared = scatter_outer(*scatter_inner(sum_shared)).astype(f32)
    near = chip_sum(core_part({0: near_rows}), 0)
    grad_gain_in = 0.0
    for e, rows in {0: near_rows, **far_rows}.items():
        unit = chip_rows(tokens, e).astype(f32) * chip_rows(scale_in, e)
        grad_gain_in += jnp.sum(rows.reshape(2 * length, D).astype(f32) * unit, axis=0)
    got, near, grad_gain_in = fence(got, near, grad_gain_in)

    sum_own = jnp.concatenate([sum_streams, sum_qz], axis=1)
    got_own = exchange_ctx(by_distance(sum_own.reshape(peers, in_rows, own_width)))
    sum_gate_up = jnp.concatenate([sum_gate, sum_up], axis=1)
    gu_sums = by_distance(sum_gate_up.reshape(peers, in_rows, 2 * ff_width))
    got_gate_up = exchange_ctx(gu_sums)
    grad_bias = jnp.sum(grad_raw, axis=0)
    grad_decay = jnp.sum(grad_rate * rates.reshape(total_len, heads), axis=0)
    grad_skip = jnp.sum(totals[:, 2, :], axis=0)

    result = middle + total_of(result_near, result_got)
    block_output = result.astype(bf16).reshape(block_input.shape)
    grad_normed = total_of(near, got)
    x_float = x_own.astype(f32)
    own_scale = rms_scale(x_float)
    own_unit = x_float * own_scale
    input_grad = grad_middle + norm_back(grad_normed * gain_in, own_unit, own_scale)
    input_grad = input_grad.reshape(block_input.shape)
    small_grad = jnp.concatenate(
        [
            grad_gain_in,
            grad_gain_mid,
            spread_cols(grad_gain_mix[None, :], pair_block)[0],
            spread_cols(grad_bias[None, :], head_block)[0],
            spread_cols(grad_decay[None, :], head_block)[0],
            spread_cols(grad_skip[None, :], head_block)[0],
        ]
    )
    small_grad = sum_dp(sum_ctx(small_grad))
    in_rate = rate_scale / math.sqrt(D)
    gate_up_state = (gate_up_weight, gate_up_first, gate_up_second)
    if strided:
        new_gate_up = update_dealt(
            place_arg, got_gate_up, None, *gate_up_state, ((0, 2 * FF, 0),), in_rate
        )
    else:
        got = place_ctx(got_gate_up).astype(f32)
        sum_gate_up = jnp.concatenate(
            [
                join_cols(got[:, :, :ff_width], row_block),
                join_cols(got[:, :, ff_width:], row_block),
            ],
            axis=1,
        )
        new_gate_up = adam_step(gate_up_weight, sum_gate_up, *gate_up_state[1:], in_rate)
    new_out = adam_step(
        out_weight, sum_out, out_first, out_second, rate_scale / math.sqrt(DSSM + QH * HD)
    )
    new_down = adam_step(
        down_weight, sum_down, down_first, down_second, rate_scale / math.sqrt(FF)
    )
    got = got_own
    placed = place_ctx({m: block[:, width:sq_width] for m, block in got.items()}).astype(f32)
    tail = jnp.concatenate(
        [
            sum_shared[:, : 2 * STATE],
            sum_shared[:, SHARED - 128 : SHARED - 128 + HEADS_M],
            join_cols(placed, query_block),
            sum_shared[:, 2 * STATE : SHARED - 128],
        ],
        axis=1,
    )
    if strided:
        spans = ((0, DSSM, sq_width), (DSSM, DSSM, 0))
        new_in = update_dealt(
            place_arg, got, tail, in_weight, in_first, in_second, spans, in_rate
        )
    else:
        got = place_ctx(got).astype(f32)
        sum_in = jnp.concatenate(
            [
                join_cols(got[:, :, sq_width:], pair_block),
                join_cols(got[:, :, :width], pair_block),
                tail,
            ],
            axis=1,
        )
        new_in = adam_step(in_weight, sum_in, in_first, in_second, in_rate)
    new_small = adam_step(small_params, small_grad, small_first, small_second, small_rate)
    return (block_output, input_grad, *new_in, *new_out, *new_gate_up, *new_down, *new_small)


def solution(mesh):
    rows = P(("dp", "ctx"), None)
    tokens = P("dp", "ctx", None)
    return jax.shard_map(
        shards,
        mesh=mesh,
        in_specs=(tokens, P("dp", "ctx"), tokens) + (rows,) * 12 + (P(),) * 3,
        out_specs=(tokens, tokens) + (rows,) * 12 + (P(),) * 3,
        check_vma=False,
    )
```

```python
import functools
import math

import jax
import jax.numpy as jnp
from jax import lax
from jax.experimental import pallas as pl
from jax.experimental.pallas import tpu as pltpu
from jax.sharding import PartitionSpec as P

D = 2048
FF = 4096
QH = 8
KVH = 2
HD = 128
HEADS_M = 48
HEAD_M = 64
STATE = 256
STEP = 10
DOC_MOST = 800
DSSM = HEADS_M * HEAD_M
SHARED = 2 * STATE + 2 * KVH * HD + 128
CHUNK = 256
QBLOCK = 256

norm_eps = 1e-05
beta_one = 0.9
beta_two = 0.95
adam_eps = 1e-08
weight_decay = 0.1
rate_scale = 3.0
small_rate = 0.3
bf16 = jnp.bfloat16
f32 = jnp.float32
NN = (((1,), (0,)), ((), ()))
NT = (((1,), (1,)), ((), ()))
TN = (((0,), (0,)), ((), ()))


def dot(a, b, dims=NN):
    return lax.dot_general(a, b, dims, preferred_element_type=f32)


def from_ctx(x, m):
    count = lax.axis_size("ctx")
    return lax.ppermute(x, "ctx", [(i ^ m, i) for i in range(count)])


def from_dp(x, j, k):
    count = lax.axis_size("dp")
    inner = count // 4
    pairs = []
    for i in range(count):
        z, w = divmod(i, inner)
        pairs.append((((z + j) % 4) * inner + (w + k) % inner, i))
    return lax.ppermute(x, "dp", pairs)


def fence(*trees):
    return lax.optimization_barrier(trees)


def outer_groups():
    count = lax.axis_size("dp")
    inner = count // 4
    return [[j * inner + k for j in range(4)] for k in range(inner)]


def gather_outer(own):
    return lax.all_gather(own, "dp", axis_index_groups=outer_groups())


def gather_outer_permuted(own):
    outer = lax.axis_index("dp") // (lax.axis_size("dp") // 4)
    full = jnp.stack([own] * 4)
    for j in (1, 3, 2):
        full = lax.dynamic_update_index_in_dim(
            full, from_dp(own, j, 0), lax.rem(outer + j, 4), 0
        )
    return full


def gather_inner(along):
    return {k: from_dp(along, 0, k) for k in range(1, lax.axis_size("dp") // 4)}


def place_dp(along, others):
    inner = lax.axis_size("dp") // 4
    place = lax.rem(lax.axis_index("dp"), inner)
    full = jnp.stack([along] * inner, axis=1)
    for k, block in others.items():
        full = lax.dynamic_update_index_in_dim(full, block, lax.rem(place + k, inner), 1)
    return full


def scatter_inner(full):
    inner = lax.axis_size("dp") // 4
    place = lax.rem(lax.axis_index("dp"), inner)
    full = full.reshape((4, inner) + full.shape[1:])

    def part(k):
        return lax.dynamic_index_in_dim(full, lax.rem(place + k, inner), 1, False)

    return part(0), {k: from_dp(part(k), 0, -k) for k in range(1, inner)}


def scatter_outer(own, got):
    total = own.astype(f32)
    for block in got.values():
        total = total + block.astype(f32)
    total = total.astype(bf16)
    total = lax.psum_scatter(
        total, "dp", scatter_dimension=0, axis_index_groups=outer_groups(), tiled=True
    )
    return total[0]


def across(own):
    return {m: from_ctx(own, m) for m in range(2, lax.axis_size("ctx"), 2)}


def beside(blocks):
    out = {}
    for m, block in blocks.items():
        out[m] = block
        out[m + 1] = from_ctx(block, 1)
    return out


def place_ctx(blocks, dim=0):
    shape = blocks[0].shape
    place = lax.axis_index("ctx")
    full = jnp.zeros(shape[:dim] + (lax.axis_size("ctx"),) + shape[dim:], blocks[0].dtype)
    for m, block in blocks.items():
        full = lax.dynamic_update_index_in_dim(full, block, place ^ m, dim)
    return full


def chip_sum(part, m):
    return part(m).astype(f32) + from_ctx(part(m + 1), 1).astype(f32)


def far_sums(part):
    return {m: chip_sum(part, m).astype(bf16) for m in range(2, lax.axis_size("ctx"), 2)}


def send_far(sums):
    return {m: from_ctx(block, m) for m, block in sums.items()}


def total_of(near, got):
    for block in got.values():
        near = near + block.astype(f32)
    return near


def scatter_ctx(part):
    got = send_far(far_sums(part))
    return total_of(chip_sum(part, 0), got)


def exchange_ctx(blocks):
    moved = [m for m in range(2, lax.axis_size("ctx"))] + [1]
    return {0: blocks[0], **{m: from_ctx(blocks[m], m) for m in moved}}


def by_distance(blocks):
    place = lax.axis_index("ctx")
    return [
        lax.dynamic_index_in_dim(blocks, place ^ m, 0, False) for m in range(lax.axis_size("ctx"))
    ]


def sum_ctx(x):
    m = 1
    while m < lax.axis_size("ctx"):
        x = x + from_ctx(x, m)
        m *= 2
    return x


def sum_dp(x):
    count = lax.axis_size("dp")
    m = 1
    while m < count:
        x = x + lax.ppermute(x, "dp", [(i ^ m, i) for i in range(count)])
        m *= 2
    return x


def split_cols(a, block):
    count = lax.axis_size("ctx")
    rows, n = a.shape
    a = a.reshape(rows, n // (count * block), count, block)
    return a.transpose(2, 0, 1, 3).reshape(count, rows, n // count)


def join_cols(a, block):
    count, rows, n = a.shape
    a = a.reshape(count, rows, n // block, block)
    return a.transpose(1, 2, 0, 3).reshape(rows, count * n)


def own_cols(a, block):
    count = lax.axis_size("ctx")
    rows, n = a.shape
    a = a.reshape(rows, n // (count * block), count, block)
    a = lax.dynamic_index_in_dim(a, lax.axis_index("ctx"), 2, False)
    return a.reshape(rows, n // count)


def spread_cols(a, block):
    count = lax.axis_size("ctx")
    rows, n = a.shape
    a = a.reshape(rows, n // block, block)
    full = jnp.zeros((rows, n // block, count, block), a.dtype)
    full = lax.dynamic_update_index_in_dim(full, a, lax.axis_index("ctx"), 2)
    return full.reshape(rows, count * n)


def attention_window(total_len):
    reach = -(-(DOC_MOST - 1) // QBLOCK) * QBLOCK
    return min(reach, total_len - QBLOCK), min(reach + QBLOCK, total_len)


def attention_spans(total_len, col_ref, row_ref, body):
    _, window = attention_window(total_len)
    first = pl.program_id(1) * QBLOCK
    lowest = jnp.min(col_ref[:, 0:1])
    open_still = first >= 0
    for size in (2 * QBLOCK, 3 * QBLOCK, window):
        start = pl.multiple_of(jnp.maximum(first - (size - QBLOCK), 0), QBLOCK)
        if size < window:
            before = pl.multiple_of(jnp.maximum(first - size, 0), QBLOCK)
            highest = jnp.max(row_ref[0:1, pl.ds(before, QBLOCK)])
            fits = jnp.logical_or(first < size, highest < lowest)
        else:
            fits = first >= 0
        pl.when(jnp.logical_and(open_still, fits))(functools.partial(body, start, size))
        open_still = jnp.logical_and(open_still, jnp.logical_not(fits))


def attention_scores(start, size, q_ref, k_ref, col_ref, row_ref):
    first = pl.program_id(1) * QBLOCK
    keys = k_ref[pl.ds(start, size), :]
    scores = dot(q_ref[...], keys, NT) * HD ** (-0.5)
    query_place = first + lax.broadcasted_iota(jnp.int32, (QBLOCK, size), 0)
    key_place = start + lax.broadcasted_iota(jnp.int32, (QBLOCK, size), 1)
    key_seg = row_ref[0:1, pl.ds(start, size)]
    allowed = (key_place <= query_place) & (col_ref[:, 0:1] == key_seg)
    return keys, jnp.where(allowed, scores, -1e30)


def attend_kernel(total_len, q_ref, k_ref, v_ref, col_ref, row_ref, out_ref, log_ref):
    def body(start, size):
        _, scores = attention_scores(start, size, q_ref, k_ref, col_ref, row_ref)
        peak = jnp.max(scores, axis=1, keepdims=True)
        expo = jnp.exp(scores - peak)
        total = jnp.sum(expo, axis=1, keepdims=True)
        shares = (expo * (1.0 / total)).astype(bf16)
        out_ref[...] = dot(shares, v_ref[pl.ds(start, size), :]).astype(out_ref.dtype)
        log_ref[...] = jnp.broadcast_to(peak + jnp.log(total), log_ref.shape)

    attention_spans(total_len, col_ref, row_ref, body)


def attend_back_kernel(
    total_len, q_ref, k_ref, v_ref, col_ref, row_ref, log_ref, grad_ref, dq_ref, dk_ref, dv_ref
):
    @pl.when(pl.program_id(1) == 0)
    def _():
        dk_ref[...] = jnp.zeros_like(dk_ref)
        dv_ref[...] = jnp.zeros_like(dv_ref)

    def body(start, size):
        keys, scores = attention_scores(start, size, q_ref, k_ref, col_ref, row_ref)
        shares = jnp.exp(scores - log_ref[:, 0:1])
        grad = grad_ref[...]
        grad_shares = dot(grad, v_ref[pl.ds(start, size), :], NT)
        inner = jnp.sum(shares * grad_shares, axis=1, keepdims=True)
        grad_scores = (shares * (grad_shares - inner)).astype(bf16)
        scale = HD ** (-0.5)
        dq_ref[...] = dot(grad_scores, keys) * scale
        span = pl.ds(start, size)
        dk_ref[span, :] += dot(grad_scores, q_ref[...], TN) * scale
        dv_ref[span, :] += dot(shares.astype(bf16), grad, TN)

    attention_spans(total_len, col_ref, row_ref, body)


def attention_specs(total_len, offset):
    tile = pl.BlockSpec((QBLOCK, HD), lambda h, i: (i, h))
    whole = pl.BlockSpec((total_len, HD), lambda h, i: (0, h))
    later = pl.BlockSpec((total_len, HD), lambda h, i: (0, h + offset))
    col = pl.BlockSpec((QBLOCK, 128), lambda h, i: (i, 0))
    row = pl.BlockSpec((8, total_len), lambda h, i: (0, 0))
    return tile, whole, later, col, row


def attention_call(queries, pairs, offset, seg_col, seg_row):
    total_len, width = queries.shape
    tile, whole, later, col, row = attention_specs(total_len, offset)
    return pl.pallas_call(
        functools.partial(attend_kernel, total_len),
        grid=(width // HD, total_len // QBLOCK),
        in_specs=[tile, whole, later, col, row],
        out_specs=[tile, tile],
        out_shape=[
            jax.ShapeDtypeStruct((total_len, width), bf16),
            jax.ShapeDtypeStruct((total_len, width), f32),
        ],
        compiler_params=pltpu.CompilerParams(vmem_limit_bytes=48 * 2**20),
        cost_estimate=pl.CostEstimate(flops=1, bytes_accessed=1, transcendentals=0),
        name="attend",
    )(queries, pairs, pairs, seg_col, seg_row)


def attention_back_call(queries, pairs, offset, seg_col, seg_row, log_total, grad):
    total_len, width = queries.shape
    tile, whole, later, col, row = attention_specs(total_len, offset)
    return pl.pallas_call(
        functools.partial(attend_back_kernel, total_len),
        grid=(width // HD, total_len // QBLOCK),
        in_specs=[tile, whole, later, col, row, tile, tile],
        out_specs=[tile, whole, whole],
        out_shape=[jax.ShapeDtypeStruct((total_len, width), f32)] * 3,
        compiler_params=pltpu.CompilerParams(vmem_limit_bytes=48 * 2**20),
        cost_estimate=pl.CostEstimate(flops=1, bytes_accessed=1, transcendentals=0),
        name="attend_back",
    )(queries, pairs, pairs, seg_col, seg_row, log_total, grad)


def pair_of(col, offset, j, left):
    a = offset + 2 * j
    return jnp.where(left, col[:, a : a + 1], col[:, a + 1 : a + 2])


def state_decay(col, j, left_rows):
    last = col[CHUNK - 1 : CHUNK, :]
    a = 64 + 2 * j
    return jnp.where(left_rows, last[:, a : a + 1], last[:, a + 1 : a + 2])


def scan_kernel(pairs, x_ref, k_ref, r_ref, col_ref, row_ref, skip_ref, y_ref, s_ref, state):
    @pl.when(pl.program_id(0) == 0)
    def _():
        state[...] = jnp.zeros_like(state)

    writes = k_ref[...].astype(bf16)
    reads = r_ref[...].astype(bf16)
    col = col_ref[...]
    row = row_ref[...]
    entering = state[...].astype(bf16)
    s_ref[0] = entering
    products = dot(reads, writes, NT)
    later = lax.broadcasted_iota(jnp.int32, (CHUNK, CHUNK), 0)
    earlier = lax.broadcasted_iota(jnp.int32, (CHUNK, CHUNK), 1)
    mask = (later >= earlier) & (col[:, 127:128] == row[16:17, :])
    left = lax.broadcasted_iota(jnp.int32, (CHUNK, 128), 1) < HEAD_M
    left_rows = lax.broadcasted_iota(jnp.int32, (128, STATE), 0) < HEAD_M
    through = dot(reads, entering, NT)
    for j in range(pairs):
        lanes = slice(128 * j, 128 * j + 128)
        x = x_ref[:, lanes]
        scaled = x * pair_of(col, 32, j, left)
        scaled_low = scaled.astype(bf16)
        outs = []
        for h in (2 * j, 2 * j + 1):
            spread = col[:, h : h + 1] - row[h : h + 1, :]
            mixing = jnp.exp(jnp.where(mask, spread, -1e30)) * products
            outs.append(dot(mixing.astype(bf16), scaled_low))
        y_ref[:, lanes] = (
            jnp.where(left, outs[0], outs[1])
            + pair_of(col, 64, j, left) * through[:, lanes]
            + skip_ref[0:1, lanes] * x
        )
        to_end = (scaled * pair_of(col, 96, j, left)).astype(bf16)
        state[lanes, :] = state_decay(col, j, left_rows) * state[lanes, :] + dot(to_end, writes, TN)


def scan_back_kernel(
    pairs,
    x_ref,
    k_ref,
    r_ref,
    col_ref,
    row_ref,
    skip_ref,
    y_ref,
    s_ref,
    dy_ref,
    sum_ref,
    dx_ref,
    dk_ref,
    dr_ref,
    red_ref,
    tot_ref,
    adjoint,
    keep,
):
    @pl.when(pl.program_id(0) == 0)
    def _():
        adjoint[...] = jnp.zeros_like(adjoint)

    writes = k_ref[...].astype(bf16)
    reads = r_ref[...].astype(bf16)
    col = col_ref[...]
    row = row_ref[...]
    entering = s_ref[0]
    products = dot(writes, reads, NT)
    earlier = lax.broadcasted_iota(jnp.int32, (CHUNK, CHUNK), 0)
    later = lax.broadcasted_iota(jnp.int32, (CHUNK, CHUNK), 1)
    mask = (later >= earlier) & (col[:, 127:128] == row[16:17, :])
    left = lax.broadcasted_iota(jnp.int32, (CHUNK, 128), 1) < HEAD_M
    left_rows = lax.broadcasted_iota(jnp.int32, (128, STATE), 0) < HEAD_M
    incoming = adjoint[...]
    incoming_low = incoming.astype(bf16)
    values = dot(writes, incoming_low, NT)
    grad_products = jnp.zeros((CHUNK, CHUNK), f32)
    grad_writes = jnp.zeros((CHUNK, STATE), f32)
    grad_reads = jnp.zeros((CHUNK, STATE), f32)
    tot_ref[0] = jnp.zeros(tot_ref.shape[1:], f32)
    for j in range(pairs):
        lanes = slice(128 * j, 128 * j + 128)
        x = x_ref[:, lanes]
        step = pair_of(col, 32, j, left)
        scaled = x * step
        scaled_low = scaled.astype(bf16)
        dy = dy_ref[:, lanes]
        dy_low = dy.astype(bf16)
        grads = []
        for side, h in enumerate((2 * j, 2 * j + 1)):
            spread = row[h : h + 1, :] - col[:, h : h + 1]
            decay = jnp.exp(jnp.where(mask, spread, -1e30))
            half = left if side == 0 else jnp.logical_not(left)
            grad_mixing = dot(jnp.where(half, scaled_low, jnp.zeros_like(scaled_low)), dy_low, NT)
            grad_products += grad_mixing * decay
            grads.append(dot((decay * products).astype(bf16), dy_low))
        grad_scaled = jnp.where(left, grads[0], grads[1])
        decay_end = pair_of(col, 96, j, left)
        to_end = (scaled * decay_end).astype(bf16)
        passed = to_end.astype(f32) * values[:, lanes]
        skip = skip_ref[0:1, lanes]
        flow = (
            dy_low.astype(f32) * (y_ref[:, lanes] - skip * x)
            - scaled_low.astype(f32) * grad_scaled
            - passed
        )
        grad_scaled += decay_end * values[:, lanes]
        dx_ref[:, lanes] = (step * grad_scaled + skip * dy).astype(bf16)
        from_start = (pair_of(col, 64, j, left) * dy).astype(bf16)
        grad_reads += dot(from_start, entering[lanes, :])
        grad_writes += dot(to_end, incoming_low[lanes, :])
        pieces = (flow, x * grad_scaled)
        for n, piece in enumerate(pieces):
            high = piece.astype(bf16)
            keep[2 * n, :, lanes] = high
            keep[2 * n + 1, :, lanes] = (piece - high.astype(f32)).astype(bf16)
        tot_ref[0, 1:2, lanes] = jnp.sum(passed, axis=0, keepdims=True)
        tot_ref[0, 2:3, lanes] = jnp.sum(dy * x, axis=0, keepdims=True)
        product = incoming[lanes, :] * entering[lanes, :].astype(f32)
        high = product.astype(bf16)
        low = (product - high.astype(f32)).astype(bf16)
        ones = jnp.ones((8, STATE), bf16)
        tot_ref[0, 0:1, lanes] = (dot(ones, high, NT) + dot(ones, low, NT))[0:1, :]
        adjoint[lanes, :] = state_decay(col, j, left_rows) * incoming[lanes, :] + dot(
            from_start, reads, TN
        )
    grad_products = grad_products.astype(bf16)
    dk_ref[...] = (grad_writes + dot(grad_products, reads)).astype(bf16)
    dr_ref[...] = (grad_reads + dot(grad_products, writes, TN)).astype(bf16)
    sums = sum_ref[...]
    red_ref[...] = (
        dot(keep[0], sums[0]) + dot(keep[1], sums[0]) + dot(keep[2], sums[1]) + dot(keep[3], sums[1])
    )


def scan_call(own, shared, col, row, skip, width):
    total_len = own.shape[0]
    count = total_len // CHUNK
    return pl.pallas_call(
        functools.partial(scan_kernel, width // 128),
        grid=(count,),
        in_specs=[
            pl.BlockSpec((CHUNK, width), lambda i: (i, 0)),
            pl.BlockSpec((CHUNK, STATE), lambda i: (i, 0)),
            pl.BlockSpec((CHUNK, STATE), lambda i: (i, 1)),
            pl.BlockSpec((CHUNK, 128), lambda i: (i, 0)),
            pl.BlockSpec((24, CHUNK), lambda i: (0, i)),
            pl.BlockSpec((8, width), lambda i: (0, 0)),
        ],
        out_specs=[
            pl.BlockSpec((CHUNK, width), lambda i: (i, 0)),
            pl.BlockSpec((1, width, STATE), lambda i: (i, 0, 0)),
        ],
        out_shape=[
            jax.ShapeDtypeStruct((total_len, width), f32),
            jax.ShapeDtypeStruct((count, width, STATE), bf16),
        ],
        scratch_shapes=[pltpu.VMEM((width, STATE), f32)],
        compiler_params=pltpu.CompilerParams(vmem_limit_bytes=48 * 2**20),
        cost_estimate=pl.CostEstimate(flops=1, bytes_accessed=1, transcendentals=0),
        name="state_scan",
    )(own, shared, shared, col, row, skip)


def scan_back_call(own, shared, col, row, skip, scanned, states, grad, width):
    total_len = own.shape[0]
    count = total_len // CHUNK
    owner = jnp.arange(width)[:, None] // HEAD_M
    lane = jnp.arange(128)[None, :]
    sums = jnp.stack([owner == lane, owner + 32 == lane]).astype(bf16)

    def back(i):
        return count - 1 - i

    return pl.pallas_call(
        functools.partial(scan_back_kernel, width // 128),
        grid=(count,),
        in_specs=[
            pl.BlockSpec((CHUNK, width), lambda i: (back(i), 0)),
            pl.BlockSpec((CHUNK, STATE), lambda i: (back(i), 0)),
            pl.BlockSpec((CHUNK, STATE), lambda i: (back(i), 1)),
            pl.BlockSpec((CHUNK, 128), lambda i: (back(i), 0)),
            pl.BlockSpec((24, CHUNK), lambda i: (0, back(i))),
            pl.BlockSpec((8, width), lambda i: (0, 0)),
            pl.BlockSpec((CHUNK, width), lambda i: (back(i), 0)),
            pl.BlockSpec((1, width, STATE), lambda i: (back(i), 0, 0)),
            pl.BlockSpec((CHUNK, width), lambda i: (back(i), 0)),
            pl.BlockSpec((2, width, 128), lambda i: (0, 0, 0)),
        ],
        out_specs=[
            pl.BlockSpec((CHUNK, width), lambda i: (back(i), 0)),
            pl.BlockSpec((CHUNK, STATE), lambda i: (back(i), 0)),
            pl.BlockSpec((CHUNK, STATE), lambda i: (back(i), 0)),
            pl.BlockSpec((CHUNK, 128), lambda i: (back(i), 0)),
            pl.BlockSpec((1, 8, width), lambda i: (back(i), 0, 0)),
        ],
        out_shape=[
            jax.ShapeDtypeStruct((total_len, width), bf16),
            jax.ShapeDtypeStruct((total_len, STATE), bf16),
            jax.ShapeDtypeStruct((total_len, STATE), bf16),
            jax.ShapeDtypeStruct((total_len, 128), f32),
            jax.ShapeDtypeStruct((count, 8, width), f32),
        ],
        scratch_shapes=[pltpu.VMEM((width, STATE), f32), pltpu.VMEM((4, CHUNK, width), bf16)],
        compiler_params=pltpu.CompilerParams(vmem_limit_bytes=48 * 2**20),
        cost_estimate=pl.CostEstimate(flops=1, bytes_accessed=1, transcendentals=0),
        name="state_scan_back",
    )(own, shared, shared, col, row, skip, scanned, states, grad, sums)


def feed_kernel(per_block, *refs):
    own_ref, side_ref, cot_ref, gate_ref, up_ref, down_ref = refs[:6]
    back_ref, mid_ref, hidden_ref, grad_gate_ref, grad_up_ref = refs[-5:]
    first = pl.program_id(0) < per_block
    mid = jnp.where(first, own_ref[...], side_ref[...])
    mid_ref[...] = mid
    gate = dot(mid, gate_ref[...])
    upper = dot(mid, up_ref[...])
    grad_hidden = dot(cot_ref[...], down_ref[...], NT)
    sigma = jax.nn.sigmoid(gate)
    gate_half = gate * sigma
    hidden_ref[...] = (gate_half * upper).astype(bf16)
    grad_gate = (grad_hidden * upper * (sigma * (1.0 + gate * (1.0 - sigma)))).astype(bf16)
    grad_up = (grad_hidden * gate_half).astype(bf16)
    grad_gate_ref[...] = grad_gate
    grad_up_ref[...] = grad_up
    back_ref[...] = (dot(grad_gate, gate_ref[...], NT) + dot(grad_up, up_ref[...], NT)).astype(bf16)


def feed_call(e, own, side, cot, w_gate, w_up, w_down, kept):
    length = own.shape[0]
    total_len = cot.shape[0]
    columns = w_gate.shape[1]
    tile = min(256, length)
    per_block = length // tile
    tiles = 2 * per_block

    def held(shape):
        return pl.BlockSpec(shape, lambda i: (0, 0), pipeline_mode=pl.Buffered(1))

    def spread(n):
        return pl.BlockSpec((tile, n), lambda i: (i + e * tiles, 0))

    kept_shapes = [(total_len, D)] + [(total_len, columns)] * 3
    return pl.pallas_call(
        functools.partial(feed_kernel, per_block),
        grid=(tiles,),
        in_specs=[
            pl.BlockSpec((tile, D), lambda i: (jnp.minimum(i, per_block - 1), 0)),
            pl.BlockSpec((tile, D), lambda i: (jnp.maximum(i - per_block, 0), 0)),
            spread(D),
            held(w_gate.shape),
            held(w_up.shape),
            held(w_down.shape),
        ]
        + [pl.BlockSpec(memory_space=pl.ANY)] * len(kept),
        out_specs=[
            pl.BlockSpec((tile, D), lambda i: (i, 0)),
            spread(D),
            spread(columns),
            spread(columns),
            spread(columns),
        ],
        out_shape=[jax.ShapeDtypeStruct((2 * length, D), bf16)]
        + [jax.ShapeDtypeStruct(shape, bf16) for shape in kept_shapes],
        input_output_aliases={6 + n: 1 + n for n in range(len(kept))},
        compiler_params=pltpu.CompilerParams(vmem_limit_bytes=56 * 2**20),
        cost_estimate=pl.CostEstimate(flops=1, bytes_accessed=1, transcendentals=0),
        name="feed_forward",
    )(own, side, cot, w_gate, w_up, w_down, *kept)


def token_sum_kernel(a_ref, b_ref, out_ref):
    out_ref[...] = dot(a_ref[...], b_ref[...], TN).astype(bf16)


def token_sum(a, b):
    total_len, rows = a.shape
    columns = b.shape[1]
    tile = math.gcd(rows, 512)
    return pl.pallas_call(
        token_sum_kernel,
        grid=(rows // tile,),
        in_specs=[
            pl.BlockSpec((total_len, tile), lambda i: (0, i)),
            pl.BlockSpec((total_len, columns), lambda i: (0, 0), pipeline_mode=pl.Buffered(1)),
        ],
        out_specs=pl.BlockSpec((tile, columns), lambda i: (i, 0)),
        out_shape=jax.ShapeDtypeStruct((rows, columns), bf16),
        compiler_params=pltpu.CompilerParams(vmem_limit_bytes=56 * 2**20),
        cost_estimate=pl.CostEstimate(flops=1, bytes_accessed=1, transcendentals=0),
        name="token_sum",
    )(a, b)


def normed_kernel(chip_ref, *refs):
    grads, weights, out_ref = refs[:3], refs[3:6], refs[6]
    total = dot(grads[0][...], weights[0][...], NT)
    total += dot(grads[1][...], weights[1][...], NT)
    total += dot(grads[2][...], weights[2][...], NT)
    out_ref[...] = total.astype(bf16)


def normed_call(chip, rows, grads, weights):
    tile = 256
    tiles = rows // tile

    def picked(grad):
        return pl.BlockSpec((tile, grad.shape[1]), lambda i, chip: (chip[0] * tiles + i, 0))

    def held(weight):
        return pl.BlockSpec(weight.shape, lambda i, chip: (0, 0), pipeline_mode=pl.Buffered(1))

    return pl.pallas_call(
        normed_kernel,
        grid_spec=pltpu.PrefetchScalarGridSpec(
            num_scalar_prefetch=1,
            grid=(tiles,),
            in_specs=[picked(grad) for grad in grads] + [held(weight) for weight in weights],
            out_specs=pl.BlockSpec((tile, D), lambda i, chip: (i, 0)),
        ),
        out_shape=jax.ShapeDtypeStruct((rows, D), bf16),
        compiler_params=pltpu.CompilerParams(vmem_limit_bytes=48 * 2**20),
        cost_estimate=pl.CostEstimate(flops=1, bytes_accessed=1, transcendentals=0),
        name="grad_normed",
    )(chip, *grads, *weights)


def place_rows_kernel(place_ref, *refs):
    for m, block_ref in enumerate(refs[:-1]):

        @pl.when(pl.program_id(0) == m)
        def _():
            refs[-1][...] = block_ref[...]


def place_rows(place, blocks):
    count = len(blocks)
    rows, columns = blocks[0].shape
    tile = min(256, rows)
    tiles = rows // tile

    def source(k):
        def at(m, i, place):
            return jnp.where(m == k, i, jnp.where(m < k, 0, tiles - 1)), 0

        return pl.BlockSpec((tile, columns), at)

    return pl.pallas_call(
        place_rows_kernel,
        grid_spec=pltpu.PrefetchScalarGridSpec(
            num_scalar_prefetch=1,
            grid=(count, tiles),
            in_specs=[source(k) for k in range(count)],
            out_specs=pl.BlockSpec(
                (tile, columns), lambda m, i, place: ((place[0] ^ m) * tiles + i, 0)
            ),
        ),
        out_shape=jax.ShapeDtypeStruct((count * rows, columns), blocks[0].dtype),
        compiler_params=pltpu.CompilerParams(vmem_limit_bytes=48 * 2**20),
        cost_estimate=pl.CostEstimate(flops=1, bytes_accessed=1, transcendentals=0),
        name="place_rows",
    )(place, *[blocks[m] for m in range(count)])


def pack_in_kernel(count, place_ref, w_ref, own_ref, shared_ref):
    place = place_ref[0]
    width = DSSM // count
    first_z = width + QH * HD // count
    query = 2 * DSSM + 2 * STATE + HEADS_M
    for c in range(count):
        m = c ^ place
        for n in range(DSSM // (count * HD)):
            at = (n * count + c) * HD
            to = slice(n * HD, (n + 1) * HD)
            own_ref[m, :, to] = w_ref[:, DSSM + at : DSSM + at + HD].astype(bf16)
            to = slice(first_z + n * HD, first_z + (n + 1) * HD)
            own_ref[m, :, to] = w_ref[:, at : at + HD].astype(bf16)
        for n in range(QH // count):
            at = query + (n * count + c) * HD
            to = slice(width + n * HD, width + (n + 1) * HD)
            own_ref[m, :, to] = w_ref[:, at : at + HD].astype(bf16)
    shared_ref[:, : 2 * STATE] = w_ref[:, 2 * DSSM : 2 * DSSM + 2 * STATE].astype(bf16)
    shared_ref[:, 2 * STATE : SHARED - 128] = w_ref[:, query + QH * HD :].astype(bf16)
    steps = w_ref[:, query - HEADS_M : query - HEADS_M + 128]
    lane = lax.broadcasted_iota(jnp.int32, steps.shape, 1)
    shared_ref[:, SHARED - 128 :] = jnp.where(lane < HEADS_M, steps, 0.0).astype(bf16)


def pack_in(place, weight):
    rows = weight.shape[0]
    count = lax.axis_size("ctx")
    own_width = (2 * DSSM + QH * HD) // count
    return pl.pallas_call(
        functools.partial(pack_in_kernel, count),
        in_specs=[pl.BlockSpec(memory_space=pltpu.SMEM), pl.BlockSpec(memory_space=pltpu.VMEM)],
        out_specs=[pl.BlockSpec(memory_space=pltpu.VMEM)] * 2,
        out_shape=[
            jax.ShapeDtypeStruct((count, rows, own_width), bf16),
            jax.ShapeDtypeStruct((rows, SHARED), bf16),
        ],
        compiler_params=pltpu.CompilerParams(vmem_limit_bytes=48 * 2**20),
        name="pack_in",
    )(place, weight)


def pack_gate_up_kernel(count, place_ref, w_ref, out_ref):
    place = place_ref[0]
    blocks = FF // (count * HD)
    for c in range(count):
        m = c ^ place
        for n in range(2 * blocks):
            at = (n * count + c) * HD
            out_ref[m, :, n * HD : (n + 1) * HD] = w_ref[:, at : at + HD].astype(bf16)


def pack_gate_up(place, weight):
    rows = weight.shape[0]
    count = lax.axis_size("ctx")
    return pl.pallas_call(
        functools.partial(pack_gate_up_kernel, count),
        in_specs=[pl.BlockSpec(memory_space=pltpu.SMEM), pl.BlockSpec(memory_space=pltpu.VMEM)],
        out_specs=pl.BlockSpec(memory_space=pltpu.VMEM),
        out_shape=jax.ShapeDtypeStruct((count, rows, 2 * FF // count), bf16),
        compiler_params=pltpu.CompilerParams(vmem_limit_bytes=48 * 2**20),
        name="pack_gate_up",
    )(place, weight)


def update_kernel(count, spans, rate, place_ref, g_ref, *refs):
    tail_ref = refs[0] if len(refs) == 7 else None
    w_ref, first_ref, second_ref, new_w_ref, new_first_ref, new_second_ref = refs[-6:]
    place = place_ref[0]

    def update(cols, grad):
        new = adam_step(w_ref[:, cols], grad, first_ref[:, cols], second_ref[:, cols], rate)
        new_w_ref[:, cols], new_first_ref[:, cols], new_second_ref[:, cols] = new

    for first, columns, at in spans:
        for n in range(columns // (count * HD)):
            for c in range(count):
                start = first + (n * count + c) * HD
                grad = g_ref[c ^ place, :, at : at + HD].astype(f32)
                update(slice(start, start + HD), grad)
            at += HD
    if tail_ref is not None:
        update(slice(2 * DSSM, w_ref.shape[1]), tail_ref[...])


def update_dealt(place, got, tail, weight, first, second, spans, rate):
    rows, columns = weight.shape
    count = lax.axis_size("ctx")
    got = jnp.stack([got[m] for m in range(count)])
    block = 16

    def flat(n):
        return pl.BlockSpec((block, n), lambda i: (i, 0))

    tails = [] if tail is None else [tail]
    return pl.pallas_call(
        functools.partial(update_kernel, count, spans, rate),
        grid=(rows // block,),
        in_specs=[
            pl.BlockSpec(memory_space=pltpu.SMEM),
            pl.BlockSpec((count, block, got.shape[2]), lambda i: (0, i, 0)),
        ]
        + [flat(t.shape[1]) for t in tails]
        + [flat(columns)] * 3,
        out_specs=[flat(columns)] * 3,
        out_shape=[jax.ShapeDtypeStruct((rows, columns), f32)] * 3,
        compiler_params=pltpu.CompilerParams(vmem_limit_bytes=48 * 2**20),
        cost_estimate=pl.CostEstimate(flops=1, bytes_accessed=1, transcendentals=0),
        name="update",
    )(place, got, *tails, weight, first, second)


def rms_scale(values):
    return lax.rsqrt(jnp.mean(values * values, axis=-1, keepdims=True) + norm_eps)


def norm_back(grad_unit, unit, scale):
    return scale * (grad_unit - unit * jnp.mean(grad_unit * unit, axis=-1, keepdims=True))


def silu_slope(values):
    sigma = jax.nn.sigmoid(values)
    return sigma * (1.0 + values * (1.0 - sigma))


def split_small(small):
    widths = [D, D, DSSM, HEADS_M, HEADS_M, HEADS_M]
    pieces = []
    start = 0
    for count in widths:
        pieces.append(small[start : start + count])
        start += count
    return pieces


def adam_step(weight, grad, first, second, rate):
    first = beta_one * first + (1.0 - beta_one) * grad
    second = beta_two * second + (1.0 - beta_two) * grad * grad
    fixed_first = first / (1.0 - beta_one**STEP)
    fixed_second = second / (1.0 - beta_two**STEP)
    weight = weight - rate * (
        fixed_first / (jnp.sqrt(fixed_second) + adam_eps) + weight_decay * weight
    )
    return (weight, first, second)


def pad_lanes(a, width):
    return jnp.pad(a, ((0, 0), (0, width - a.shape[1])))


def shards(
    block_input,
    segment_ids,
    cotangent,
    in_weight,
    out_weight,
    gate_up_weight,
    down_weight,
    in_first,
    out_first,
    gate_up_first,
    down_first,
    in_second,
    out_second,
    gate_up_second,
    down_second,
    small_params,
    small_first,
    small_second,
):
    peers = lax.axis_size("ctx")
    groups = lax.axis_size("dp")
    place = lax.axis_index("ctx")
    length = block_input.shape[0] * block_input.shape[1]
    total_len = length * peers
    row_block = out_weight.shape[0]
    in_rows = in_weight.shape[0]
    strided = row_block == HD
    width = DSSM // peers
    heads = HEADS_M // peers
    query_heads = QH // peers
    query_width = query_heads * HD
    own_width = 2 * width + query_width
    ff_width = FF // peers
    pair_block = 2 * HEAD_M if strided else width
    query_block = HD if strided else query_width
    head_block = 2 if strided else heads
    gain_in, gain_mid, gain_mix, step_bias, decay_log, skip = split_small(small_params)

    place_arg = place.astype(jnp.int32).reshape(1)
    base = 2 * DSSM + 2 * STATE + HEADS_M
    query_end = base + QH * HD
    if strided:
        own_low, shared_low = pack_in(place_arg, in_weight)
        gu_low = pack_gate_up(place_arg, gate_up_weight)
        own_low = [own_low[m] for m in range(peers)]
        gu_low = [gu_low[m] for m in range(peers)]
    else:
        in_low = in_weight.astype(bf16)
        shared_low = jnp.concatenate(
            [
                in_low[:, 2 * DSSM : 2 * DSSM + 2 * STATE],
                in_low[:, query_end:],
                in_low[:, 2 * DSSM + 2 * STATE : base],
                jnp.zeros((in_rows, 128 - HEADS_M), bf16),
            ],
            axis=1,
        )
        own_low = jnp.concatenate(
            [
                split_cols(in_low[:, DSSM : 2 * DSSM], pair_block),
                split_cols(in_low[:, base:query_end], query_block),
                split_cols(in_low[:, :DSSM], pair_block),
            ],
            axis=2,
        )
        own_low = by_distance(own_low)
        gu_low = gate_up_weight.astype(bf16)
        gu_low = jnp.concatenate(
            [split_cols(gu_low[:, :FF], row_block), split_cols(gu_low[:, FF:], row_block)], axis=2
        )
        gu_low = by_distance(gu_low)
    own_rows = place_ctx(exchange_ctx(own_low)).reshape(peers * in_rows, own_width)
    x_own = block_input.reshape(length, D)
    seg_own = segment_ids.reshape(length)
    own_rows, x_own, shared_low, gu_low, seg_own = fence(
        own_rows, x_own, shared_low, gu_low, seg_own
    )

    sq_width = width + query_width
    s_along = gather_outer(own_rows[:, :width])
    qz_along = gather_outer(own_rows[:, width:])
    seg_far = across(seg_own)
    segments = place_ctx(beside({0: seg_own, **seg_far})).reshape(total_len)
    shared_along = gather_outer_permuted(shared_low)
    out_low = out_weight.astype(bf16)
    down_low = down_weight.astype(bf16)
    x_far = across(x_own)
    shared_rows = place_dp(shared_along, gather_inner(shared_along))
    shared_rows = shared_rows.reshape((groups,) + shared_low.shape)
    down_inner = gather_inner(down_low)
    cot_own = cotangent.reshape(length, D)
    own_bias = own_cols(step_bias[None, :], head_block)
    own_decay = jnp.exp(own_cols(decay_log[None, :], head_block))
    own_skip = jnp.repeat(own_cols(skip[None, :], head_block), HEAD_M, axis=1)
    own_skip = jnp.broadcast_to(own_skip, (8, width))
    own_gain_mix = own_cols(gain_mix[None, :], pair_block)
    chunks = total_len // CHUNK
    seg_chunks = segments.reshape(chunks, CHUNK)
    seg_last = seg_chunks[:, -1:]
    seg_before = jnp.concatenate([jnp.full((1, 1), -1, seg_last.dtype), seg_last[:-1]], axis=0)
    entering = (seg_chunks == seg_before).astype(f32)[:, :, None]
    leaving = jnp.where(seg_chunks == seg_last, 0.0, -1e30)[:, :, None]
    seg_float = segments.astype(f32)
    seg_col = jnp.broadcast_to(seg_float[:, None], (total_len, 128))
    seg_row = jnp.broadcast_to(seg_float[None, :], (8, total_len))
    (x_own, x_far, shared_rows, gu_low, cot_own, s_along, out_low, down_low, down_inner) = fence(
        x_own, x_far, shared_rows, gu_low, cot_own, s_along, out_low, down_low, down_inner
    )
    own_bias, own_decay, own_skip, own_gain_mix, entering, leaving, seg_col, seg_row, x_far = fence(
        own_bias, own_decay, own_skip, own_gain_mix, entering, leaving, seg_col, seg_row, x_far
    )

    shared_far = across(shared_rows)
    if strided:
        out_along = gather_outer(out_low)
    s_others = gather_inner(s_along)
    tokens = place_rows(place_arg, beside({0: x_own, **x_far}))
    scale_in = rms_scale(tokens.astype(f32))
    normed = (tokens.astype(f32) * scale_in * gain_in).astype(bf16)
    normed, shared_rows, shared_far, s_along, s_others, qz_along, cot_own, gu_low = fence(
        normed, shared_rows, shared_far, s_along, s_others, qz_along, cot_own, gu_low
    )

    qz_others = gather_inner(qz_along)
    w_shared = place_ctx(beside({0: shared_rows, **shared_far}), 1).reshape(D, SHARED)
    pairs = dot(normed, w_shared[:, 2 * STATE : SHARED - 128]).astype(bf16)
    writes_reads = dot(normed, w_shared[:, : 2 * STATE])
    raw_all = dot(normed, w_shared[:, SHARED - 128 :])
    if not strided:
        out_along = {}
    normed, pairs, writes_reads, raw_all, cot_own, gu_low = fence(
        normed, pairs, writes_reads, raw_all, cot_own, gu_low
    )

    gu_rows = place_ctx(exchange_ctx(gu_low)).reshape(peers * in_rows, 2 * ff_width)
    gate_along = gather_outer(gu_rows[:, :ff_width])
    up_along = gather_outer(gu_rows[:, ff_width:])
    cot_far = across(cot_own)
    w_streams = place_dp(s_along, s_others).reshape(D, width)
    streams = dot(normed, w_streams)
    streams, out_along = fence(streams, out_along)
    out_others = gather_inner(out_along) if strided else {}
    raw_step = own_cols(raw_all[:, :HEADS_M], head_block)
    offset = KVH
    if query_heads < KVH:
        offset = query_heads
        own_kv = (place * query_heads * KVH // QH) * HD
        pairs = jnp.concatenate(
            [
                lax.dynamic_slice_in_dim(pairs, own_kv, query_width, 1),
                lax.dynamic_slice_in_dim(pairs, KVH * HD + own_kv, query_width, 1),
            ],
            axis=1,
        )
    step = jax.nn.softplus(raw_step + own_bias)
    rates = (-own_decay * step).reshape(chunks, CHUNK, heads)
    order = jnp.arange(CHUNK)
    lower = (order[:, None] >= order[None, :]).astype(f32)
    running = jnp.einsum("ts,csh->cth", lower, rates, precision=lax.Precision.HIGHEST)
    from_start = jnp.exp(running) * entering
    to_end = jnp.exp(jnp.where(leaving == 0.0, running[:, -1:, :] - running, -1e30))
    running = running.reshape(total_len, heads)
    col = jnp.concatenate(
        [
            pad_lanes(running, 32),
            pad_lanes(step, 32),
            pad_lanes(from_start.reshape(total_len, heads), 32),
            pad_lanes(to_end.reshape(total_len, heads), 31),
            seg_col[:, :1],
        ],
        axis=1,
    )
    row = jnp.concatenate([jnp.pad(running.T, ((0, 16 - heads), (0, 0))), seg_row], axis=0)

    scanned, states = scan_call(streams, writes_reads, col, row, own_skip, width)
    normed, scanned, qz_along, qz_others, out_along, out_others, gate_along, cot_own, cot_far = fence(
        normed, scanned, qz_along, qz_others, out_along, out_others, gate_along, cot_own, cot_far
    )

    gate_others = gather_inner(gate_along)
    inner_place = lax.rem(lax.axis_index("dp"), groups // 4)
    down_pair = jnp.stack([down_low] * (groups // 4))
    for k, block in down_inner.items():
        at = lax.rem(inner_place + k, groups // 4)
        down_pair = lax.dynamic_update_index_in_dim(down_pair, block, at, 0)
    w_down = gather_outer(down_pair).reshape(ff_width, D)
    cot = jnp.concatenate(
        [block for _, block in sorted(beside({0: cot_own, **cot_far}).items())], axis=0
    )
    w_qz = place_dp(qz_along, qz_others).reshape(D, sq_width)
    queries = dot(normed, w_qz[:, :query_width]).astype(bf16)
    gate_z = dot(normed, w_qz[:, query_width:])
    attended, log_total = attention_call(queries, pairs, offset, seg_col, seg_row)
    gate_act = jax.nn.silu(gate_z)
    gated = scanned * gate_act
    square = sum_ctx(jnp.sum(gated * gated, axis=-1))
    scale_mix = lax.rsqrt(square / DSSM + norm_eps)[:, None]
    unit_mix = gated * scale_mix
    joined = jnp.concatenate([(unit_mix * own_gain_mix).astype(bf16), attended], axis=1)
    joined, gate_along, gate_others, up_along = fence(joined, gate_along, gate_others, up_along)
    if strided:
        w_out = place_dp(out_along, out_others).reshape(sq_width, D)
    else:
        whole_out = lax.all_gather(out_low, ("dp", "ctx"), axis=0, tiled=True)
        w_out = jnp.concatenate(
            [
                lax.dynamic_slice_in_dim(whole_out, place * width, width, 0),
                lax.dynamic_slice_in_dim(whole_out, DSSM + place * query_width, query_width, 0),
            ],
            axis=0,
        )

    chips = list(range(peers // 2))
    parity = place % 2

    def chip_rows(full, e):
        start = ((place // 2) ^ e) * 2 * length
        return lax.dynamic_slice_in_dim(full, start, 2 * length, 0)

    def core_part(parts):
        return lambda m: lax.dynamic_index_in_dim(parts[m // 2], (m % 2) ^ parity, 0, False)

    def mixed_rows(e):
        return dot(chip_rows(joined, e), w_out).astype(bf16).reshape(2, length, D)

    sums = far_sums(core_part({e: mixed_rows(e) for e in chips[1:]}))
    sums, joined, gate_along, gate_others, up_along = fence(
        sums, joined, gate_along, gate_others, up_along
    )
    up_others = gather_inner(up_along)
    w_gate = place_dp(gate_along, gate_others).reshape(D, ff_width)
    got = send_far(sums)
    near = chip_sum(core_part({0: mixed_rows(0)}), 0)
    got, near, up_others, w_gate = fence(got, near, up_others, w_gate)

    middle = x_own.astype(f32) + total_of(near, got)
    scale_mid = rms_scale(middle)
    unit_mid = middle * scale_mid
    mid_own = (unit_mid * gain_mid).astype(bf16)
    w_up = place_dp(up_along, up_others).reshape(D, ff_width)
    def feed_forward(e, own, side, kept):
        back, *kept = feed_call(e, own, side, cot, w_gate, w_up, w_down, kept)
        return back.reshape(2, length, D), kept

    far = across(mid_own)
    near_back, kept = feed_forward(0, mid_own, from_ctx(mid_own, 1), [])
    far, near_back, kept = fence(far, near_back, kept)
    far = beside(far)
    far_back = {}
    for e in chips[1:]:
        far_back[e], kept = feed_forward(e, far[2 * e], far[2 * e + 1], kept)
    sums = far_sums(lambda m: far_back[m // 2][m % 2])
    sums, near_back, kept = fence(sums, near_back, kept)
    normed_mid, hidden, grad_gate, grad_up = kept
    got = send_far(sums)
    near = chip_sum(lambda m: near_back[m], 0)
    grad_gate = token_sum(normed_mid, grad_gate)
    grad_down = token_sum(hidden, cot)
    got, near, grad_gate, grad_down, normed_mid, grad_up = fence(
        got, near, grad_gate, grad_down, normed_mid, grad_up
    )

    gate_parts = scatter_inner(grad_gate.reshape(groups, -1, ff_width))
    sum_down = lax.psum_scatter(
        grad_down.reshape(4, groups // 4, row_block, D),
        "dp",
        scatter_dimension=0,
        axis_index_groups=outer_groups(),
        tiled=True,
    )
    grad_normed_mid = total_of(near, got)
    grad_middle = cot_own.astype(f32) + norm_back(grad_normed_mid * gain_mid, unit_mid, scale_mid)
    grad_middle_low = grad_middle.astype(bf16)
    grad_middle_low, hidden, normed_mid, grad_up = fence(
        grad_middle_low, hidden, normed_mid, grad_up
    )

    far = across(grad_middle_low)
    beside_own = beside({0: grad_middle_low})
    result_part = dot(hidden, w_down).astype(bf16).reshape(peers, length, D)
    grad_up = token_sum(normed_mid, grad_up)
    far, beside_own, result_part, gate_parts, grad_up = fence(
        far, beside_own, result_part, gate_parts, grad_up
    )

    grad_mixed = place_rows(place_arg, {**beside_own, **beside(far)})
    sum_gate = scatter_outer(*gate_parts)
    up_parts = scatter_inner(grad_up.reshape(groups, -1, ff_width))
    grad_gain_mid = jnp.sum(grad_normed_mid * unit_mid, axis=0)
    sums = far_sums(lambda m: result_part[m])
    result_near = chip_sum(lambda m: result_part[m], 0)
    grad_joined = dot(grad_mixed, w_out, NT)
    if strided:
        grad_out = token_sum(joined, grad_mixed)
        out_parts = scatter_inner(grad_out.reshape(groups, row_block, D))
    else:
        grad_out = dot(joined, grad_mixed, TN)
        out_parts = ()
        spread = jnp.zeros((DSSM + QH * HD, D), f32)
        spread = lax.dynamic_update_slice_in_dim(spread, grad_out[:width], place * width, 0)
        spread = lax.dynamic_update_slice_in_dim(
            spread, grad_out[width:], DSSM + place * query_width, 0
        )
        sum_out = lax.psum_scatter(spread, ("dp", "ctx"), scatter_dimension=0, tiled=True)
    grad_attended = grad_joined[:, width:].astype(bf16)
    grad_mix_part = grad_joined[:, :width]
    grad_unit = grad_mix_part * own_gain_mix
    inner = sum_ctx(jnp.sum(grad_unit * unit_mix, axis=-1))[:, None] / DSSM
    grad_queries, grad_keys, grad_values = attention_back_call(
        queries, pairs, offset, seg_col, seg_row, log_total, grad_attended
    )
    grad_queries, inner, up_parts, out_parts, sums = fence(
        grad_queries, inner, up_parts, out_parts, sums
    )

    result_got = send_far(sums)
    inner_count = groups // 4
    down_own = lax.dynamic_index_in_dim(sum_down[0], inner_place, 0, False)
    down_got = {
        k: from_dp(
            lax.dynamic_index_in_dim(
                sum_down[0], lax.rem(inner_place + k, inner_count), 0, False
            ),
            0,
            -k,
        )
        for k in range(1, inner_count)
    }
    sum_down = total_of(down_own.astype(f32), down_got)
    sum_up = scatter_outer(*up_parts)
    if strided:
        sum_out = scatter_outer(*out_parts).astype(f32)
    grad_gain_mix = jnp.sum(grad_mix_part * unit_mix, axis=0)
    grad_gated = scale_mix * (grad_unit - unit_mix * inner)
    grad_scan = grad_gated * gate_act
    grad_z = grad_gated * scanned * silu_slope(gate_z)
    grad_qz = jnp.concatenate([grad_queries.astype(bf16), grad_z.astype(bf16)], axis=1)
    grad_in_qz = token_sum(normed, grad_qz)
    grad_in_qz, grad_scan = fence(grad_in_qz, grad_scan)

    qz_parts = scatter_inner(grad_in_qz.reshape(groups, -1, sq_width))
    grad_streams, grad_writes, grad_reads, reduced, totals = scan_back_call(
        streams, writes_reads, col, row, own_skip, scanned, states, grad_scan, width
    )
    grad_streams, grad_writes, grad_reads, reduced, totals, qz_parts, result_got = fence(
        grad_streams, grad_writes, grad_reads, reduced, totals, qz_parts, result_got
    )

    grad_in_streams = token_sum(normed, grad_streams)
    sum_qz = scatter_outer(*qz_parts)
    totals = totals.reshape(chunks, 8, heads, HEAD_M).sum(axis=3)
    last = from_start[:, -1, :] * totals[:, 0, :] + totals[:, 1, :]
    flow = reduced[:, :heads].reshape(chunks, CHUNK, heads)
    grad_rate = jnp.einsum("ts,cth->csh", lower, flow, precision=lax.Precision.HIGHEST)
    grad_rate = (grad_rate + last[:, None, :]).reshape(total_len, heads)
    grad_step = reduced[:, 32 : 32 + heads] - own_decay * grad_rate
    grad_raw = grad_step * jax.nn.sigmoid(raw_step + own_bias)
    if query_heads < KVH:
        blank = jnp.zeros((total_len, KVH * HD), f32)
        grad_keys = lax.dynamic_update_slice_in_dim(blank, grad_keys, own_kv, 1)
        grad_values = lax.dynamic_update_slice_in_dim(blank, grad_values, own_kv, 1)
    grad_shared = jnp.concatenate(
        [
            grad_writes,
            grad_reads,
            grad_keys.astype(bf16),
            grad_values.astype(bf16),
            pad_lanes(spread_cols(grad_raw.astype(bf16), head_block), 128),
        ],
        axis=1,
    )
    grad_in_streams, grad_shared, normed, grad_raw, grad_rate, totals, sum_gate, sum_up = fence(
        grad_in_streams, grad_shared, normed, grad_raw, grad_rate, totals, sum_gate, sum_up
    )

    def normed_rows(e):
        chip = ((place // 2) ^ e).astype(jnp.int32).reshape(1)
        grads = grad_streams, grad_qz, grad_shared
        part = normed_call(chip, 2 * length, grads, (w_streams, w_qz, w_shared))
        return part.reshape(2, length, D)

    streams_parts = scatter_inner(grad_in_streams.reshape(groups, -1, width))
    grad_in_shared = token_sum(normed, grad_shared)
    far_rows = {e: normed_rows(e) for e in chips[1:]}
    streams_parts, grad_in_shared, far_rows, sum_gate, sum_up, sum_out, sum_down, result_got = fence(
        streams_parts, grad_in_shared, far_rows, sum_gate, sum_up, sum_out, sum_down, result_got
    )

    sum_streams = scatter_outer(*streams_parts)
    shared_part = grad_in_shared.reshape(groups, peers, in_rows, SHARED)

    def shared_of(m):
        return lax.dynamic_index_in_dim(shared_part, place ^ m, 1, False)

    shared_sums = far_sums(shared_of)
    sums = far_sums(core_part(far_rows))
    shared_sums, sums, shared_part, grad_shared = fence(shared_sums, sums, shared_part, grad_shared)

    got_shared = send_far(shared_sums)
    shared_near = chip_sum(shared_of, 0)
    near_rows = normed_rows(0)
    got_shared, shared_near, near_rows, sums = fence(got_shared, shared_near, near_rows, sums)

    got = send_far(sums)
    sum_shared = total_of(shared_near, got_shared).astype(bf16)
    sum_shared = scatter_outer(*scatter_inner(sum_shared)).astype(f32)
    near = chip_sum(core_part({0: near_rows}), 0)
    grad_gain_in = 0.0
    for e, rows in {0: near_rows, **far_rows}.items():
        unit = chip_rows(tokens, e).astype(f32) * chip_rows(scale_in, e)
        grad_gain_in += jnp.sum(rows.reshape(2 * length, D).astype(f32) * unit, axis=0)
    got, near = fence(got, near)

    sum_own = jnp.concatenate([sum_streams, sum_qz], axis=1)
    got_own = exchange_ctx(by_distance(sum_own.reshape(peers, in_rows, own_width)))
    sum_gate_up = jnp.concatenate([sum_gate, sum_up], axis=1)
    gu_sums = by_distance(sum_gate_up.reshape(peers, in_rows, 2 * ff_width))
    got_gate_up = exchange_ctx(gu_sums)
    grad_bias = jnp.sum(grad_raw, axis=0)
    grad_decay = jnp.sum(grad_rate * rates.reshape(total_len, heads), axis=0)
    grad_skip = jnp.sum(totals[:, 2, :], axis=0)

    result = middle + total_of(result_near, result_got)
    block_output = result.astype(bf16).reshape(block_input.shape)
    grad_normed = total_of(near, got)
    x_float = x_own.astype(f32)
    own_scale = rms_scale(x_float)
    own_unit = x_float * own_scale
    input_grad = grad_middle + norm_back(grad_normed * gain_in, own_unit, own_scale)
    input_grad = input_grad.reshape(block_input.shape)
    small_grad = jnp.concatenate(
        [
            grad_gain_in,
            grad_gain_mid,
            spread_cols(grad_gain_mix[None, :], pair_block)[0],
            spread_cols(grad_bias[None, :], head_block)[0],
            spread_cols(grad_decay[None, :], head_block)[0],
            spread_cols(grad_skip[None, :], head_block)[0],
        ]
    )
    small_grad = sum_dp(sum_ctx(small_grad))
    in_rate = rate_scale / math.sqrt(D)
    gate_up_state = (gate_up_weight, gate_up_first, gate_up_second)
    if strided:
        new_gate_up = update_dealt(
            place_arg, got_gate_up, None, *gate_up_state, ((0, 2 * FF, 0),), in_rate
        )
    else:
        got = place_ctx(got_gate_up).astype(f32)
        sum_gate_up = jnp.concatenate(
            [
                join_cols(got[:, :, :ff_width], row_block),
                join_cols(got[:, :, ff_width:], row_block),
            ],
            axis=1,
        )
        new_gate_up = adam_step(gate_up_weight, sum_gate_up, *gate_up_state[1:], in_rate)
    new_out = adam_step(
        out_weight, sum_out, out_first, out_second, rate_scale / math.sqrt(DSSM + QH * HD)
    )
    new_down = adam_step(
        down_weight, sum_down, down_first, down_second, rate_scale / math.sqrt(FF)
    )
    got = got_own
    placed = place_ctx({m: block[:, width:sq_width] for m, block in got.items()}).astype(f32)
    tail = jnp.concatenate(
        [
            sum_shared[:, : 2 * STATE],
            sum_shared[:, SHARED - 128 : SHARED - 128 + HEADS_M],
            join_cols(placed, query_block),
            sum_shared[:, 2 * STATE : SHARED - 128],
        ],
        axis=1,
    )
    if strided:
        spans = ((0, DSSM, sq_width), (DSSM, DSSM, 0))
        new_in = update_dealt(
            place_arg, got, tail, in_weight, in_first, in_second, spans, in_rate
        )
    else:
        got = place_ctx(got).astype(f32)
        sum_in = jnp.concatenate(
            [
                join_cols(got[:, :, sq_width:], pair_block),
                join_cols(got[:, :, :width], pair_block),
                tail,
            ],
            axis=1,
        )
        new_in = adam_step(in_weight, sum_in, in_first, in_second, in_rate)
    new_small = adam_step(small_params, small_grad, small_first, small_second, small_rate)
    return (block_output, input_grad, *new_in, *new_out, *new_gate_up, *new_down, *new_small)


def solution(mesh):
    rows = P(("dp", "ctx"), None)
    tokens = P("dp", "ctx", None)
    return jax.shard_map(
        shards,
        mesh=mesh,
        in_specs=(tokens, P("dp", "ctx"), tokens) + (rows,) * 12 + (P(),) * 3,
        out_specs=(tokens, tokens) + (rows,) * 12 + (P(),) * 3,
        check_vma=False,
    )
```
